32 devices in a mesh: dp: 8 (over z, y), mp: 4 (over x, core).
Axes of the slice: x: 2, y: 2, z: 4, core: 2. Of those that a mesh axis runs over, the one named last changes fastest.
Arguments:
- tokens: bfloat16 [4096, 1024], P('dp'), may hold values from -6 to 6
- cotangent: bfloat16 [4096, 1024], P('dp'), may hold values from -6 to 6
- segment_ids: int32 [4096], P('dp'), may hold values from -1 to 31, as said below
- table_index: int32 [4096], P('dp'), may hold values from 0 to 1043, as said below
- group_count: int32 [8], P('dp'), may hold values from 1 to 4
- owner_list: int32 [192], replicated, may hold values from 0 to 191, each once
- step_count: int32 [1], replicated, may hold values from 2 to 20
- query_weight: bfloat16 [1024, 1024], P(None, 'mp'), may hold values from -0.1875 to 0.1875
- key_weight: bfloat16 [1024, 1024], P(None, 'mp'), may hold values from -0.1875 to 0.1875
- value_weight: bfloat16 [1024, 1024], P(None, 'mp'), may hold values from -0.1875 to 0.1875
- output_weight: bfloat16 [1024, 1024], P('mp'), may hold values from -0.5 to 0.5
- hidden_weight: bfloat16 [1024, 4096], P(None, 'mp'), may hold values from -0.1875 to 0.1875
- return_weight: bfloat16 [4096, 1024], P('mp'), may hold values from -0.09375 to 0.09375
- norm_params: float32 [4, 1024], replicated, may hold values from 0.5 to 1.5
- norm_first: float32 [4, 1024], replicated, may hold values from -0.00390625 to 0.00390625
- norm_second: float32 [4, 1024], replicated, may hold values from 7.9447e-08 to 3.17788e-07
- master_blocks: float32 [192, 4, 128, 128], P('dp', 'mp'), may hold values from -0.1875 to 0.1875
- first_moment: float32 [192, 4, 128, 128], P('dp', 'mp'), may hold values from -0.00390625 to 0.00390625
- second_moment: float32 [192, 4, 128, 128], P('dp', 'mp'), may hold values from 7.9447e-08 to 3.17788e-07
- left_vector: float32 [192, 4, 128], P('dp', 'mp'), may hold values from -6 to 6
- right_vector: float32 [192, 4, 128], P('dp', 'mp'), may hold values from -6 to 6
Outputs:
- layer_output: float32 [4096, 1024], P('dp')
- input_grad: float32 [4096, 1024], P('dp')
- block_grads: float32 [192, 4, 128, 128], P('dp', 'mp')
- block_first: float32 [192, 4, 128, 128], P('dp', 'mp')
- block_second: float32 [192, 4, 128, 128], P('dp', 'mp')
- block_master: float32 [192, 4, 128, 128], P('dp', 'mp')
- block_copy: bfloat16 [192, 4, 128, 128], P('dp', 'mp')
- norm_grads: float32 [2, 4, 1024], replicated
- norm_square: float32 [4, 1024], replicated
- norm_value: float32 [4, 1024], replicated
- clip_norm: float32 [], replicated
The draws below stay inside these ranges and needn't reach their ends.
Inputs may be any that keep to these rules, and one draw needn't show every extreme that they name: `segment_ids`: on each dp index the items all have one length, 16, 49 or 196 patches, and lie one after another from the first slot, numbered from 0; the slots after them hold -1. Every device holds at least one item. `table_index`: rows 0 to 63 belong to images of 64 patches, 64 to 259 to images of 196, 260 to 1043 to images of 784; all slots of a dp index use the range whose image size matches its item length (64, 196, 784 patches for items of 16, 49, 196). `owner_list`: every block number appears once; slot s lies on dp index s // 24.
All inputs are finite; a program needn't handle non-finite values.
Results may differ from the reference program's by a relative error of at most 0.014.
Values may be sent and summed in bfloat16 or wider, within the bound.
No kernel may reach another device: no remote copies, remote signals or barrier semaphores. Data moves between devices by JAX's collectives and lax.ppermute only.
A program may use at most 128 MiB of HBM per device.

```python
import math
import jax
import jax.numpy as jnp
from jax import lax

D = 1024
FF = 4096
HEAD = 64
BLK = 128
TOK_DEV = 512
TOKENS = 4096
NBLK = 192
NPAR = 12587008
N_DP = 8
N_MP = 4


def item_layout(key):
    device_count = TOKENS // TOK_DEV
    base = jax.random.fold_in(key, 7)
    group_key = jax.random.fold_in(base, 1)
    count_key = jax.random.fold_in(base, 2)
    group = jax.random.randint(group_key, (device_count,), 0, 3)
    group = group.at[0].set(0).at[device_count - 1].set(2)
    lengths = jnp.array([16, 49, 196], jnp.int32)
    item_length = lengths[group]
    capacity = TOK_DEV // item_length
    least = jnp.maximum(capacity - capacity // 3, 1)
    spread = jax.random.randint(count_key, (device_count,), 0, 1 << 20)
    item_count = least + spread % (capacity - least + 1)
    item_count = item_count.at[0].set(capacity[0])
    return (group, item_length, item_count)


def draw_segment_ids(key, part):
    group, item_length, item_count = item_layout(key)
    slots = jnp.arange(TOK_DEV, dtype=jnp.int32)[None, :]
    filled = slots < (item_count * item_length)[:, None]
    segs = jnp.where(filled, slots // item_length[:, None], -1)
    return segs.reshape(-1).astype(jnp.int32)


def draw_table_index(key, part):
    group, item_length, item_count = item_layout(key)
    device_count = TOKENS // TOK_DEV
    patches = jnp.array([64, 196, 784], jnp.int32)
    offsets = jnp.array([0, 64, 260], jnp.int32)
    raw_bits = jax.random.randint(jax.random.fold_in(key, 11), (device_count, TOK_DEV), 0, 1 << 20)
    index = offsets[group][:, None] + raw_bits % patches[group][:, None]
    index = index.at[0, 0].set(0).at[device_count - 1, TOK_DEV - 1].set(1043)
    return index.reshape(-1).astype(jnp.int32)


def place_ends(values, rng, smallest, top_value):
    longest = values.shape.index(max(values.shape))
    spots = []
    for shift in (0, 1):
        where = [jax.random.randint(jax.random.fold_in(rng, axis), (), 0, length) for axis, length in enumerate(values.shape)]
        where[longest] = (where[longest] + shift) % values.shape[longest]
        spots.append(tuple(where))
    return values.at[spots[0]].set(smallest).at[spots[1]].set(top_value)


def shard_levels(key, extent, split, low, largest):
    def one(axis_at, blocks):
        draws = jax.random.uniform(jax.random.fold_in(jax.random.fold_in(key, 6), axis_at), (blocks,), jnp.float32, low / len(split), largest / len(split))
        return jnp.repeat(jnp.exp(draws), extent[axis_at] // blocks).reshape((-1,) + (1,) * (len(extent) - axis_at - 1))

    level = one(*split[0])
    for cut in split[1:]:
        level = level * one(*cut)
    return level


def gaussian(key, extent, scale, bound, shards=(), kind=jnp.bfloat16):
    level = shard_levels(key, extent, shards, -0.22, 0.18) if shards else 1.0
    entries = jax.random.normal(key, extent, jnp.float32) * scale * level
    return jnp.minimum(jnp.maximum(entries, -bound), bound).astype(kind)


def setup_inputs(seed: int = 0) -> dict:
    key_list = jax.random.split(jax.random.key(seed), 22)
    return {
        "tokens": gaussian(key_list[0], (TOKENS, D), 1.0, 6.0, ((0, 8),)),
        "cotangent": gaussian(key_list[1], (TOKENS, D), 1.0, 6.0, ((0, 8),)),
        "segment_ids": draw_segment_ids(jax.random.fold_in(key_list[21], 71), 0),
        "table_index": draw_table_index(jax.random.fold_in(key_list[21], 71), 0),
        "group_count": place_ends(jax.random.randint(key_list[4], (N_DP,), 1, 5), jax.random.fold_in(key_list[4], 1), 1, 4).astype(jnp.int32),
        "owner_list": jax.random.permutation(key_list[5], NBLK).astype(jnp.int32),
        "step_count": jax.random.randint(key_list[6], (1,), 2, 21).astype(jnp.int32),
        "query_weight": gaussian(key_list[7], (D, D), D ** -0.5, 0.1875, ((1, 4),)),
        "key_weight": gaussian(key_list[8], (D, D), D ** -0.5, 0.1875, ((1, 4),)),
        "value_weight": gaussian(key_list[9], (D, D), D ** -0.5, 0.1875, ((1, 4),)),
        "output_weight": gaussian(key_list[10], (D, D), (D // 8) ** -0.5, 0.5, ((0, 4),)),
        "hidden_weight": gaussian(key_list[11], (D, FF), D ** -0.5, 0.1875, ((1, 4),)),
        "return_weight": gaussian(key_list[12], (FF, D), FF ** -0.5, 0.09375, ((0, 4),)),
        "norm_params": jnp.clip(1.0 + 0.1 * jax.random.normal(key_list[13], (4, D), jnp.float32), 0.5, 1.5),
        "norm_first": gaussian(key_list[14], (4, D), ((1.0 / NPAR) ** 0.5), 0.00390625, (), jnp.float32),
        "norm_second": jnp.clip(jnp.exp(jax.random.uniform(key_list[15], (4, D), jnp.float32, math.log(7.944699831341495e-08), math.log(3.177879932536598e-07))), 7.944699831341495e-08, 3.177879932536598e-07),
        "master_blocks": gaussian(key_list[16], (NBLK, N_MP, BLK, BLK), D ** -0.5, 0.1875, ((0, 8), (1, 4)), jnp.float32),
        "first_moment": gaussian(key_list[17], (NBLK, N_MP, BLK, BLK), ((1.0 / NPAR) ** 0.5), 0.00390625, ((0, 8), (1, 4)), jnp.float32),
        "second_moment": jnp.clip(jnp.exp(math.log(3.177879932536598e-07) - 1.3862944 * jax.random.uniform(key_list[18], (NBLK, N_MP, BLK, BLK), jnp.float32) ** shard_levels(key_list[18], (NBLK, N_MP, BLK, BLK), ((0, 8), (1, 4)), -0.2, 0.2)), 7.944699831341495e-08, 3.177879932536598e-07),
        "left_vector": gaussian(key_list[19], (NBLK, N_MP, BLK), 1.0, 6.0, ((0, 8), (1, 4)), jnp.float32),
        "right_vector": gaussian(key_list[20], (NBLK, N_MP, BLK), 1.0, 6.0, ((0, 8), (1, 4)), jnp.float32),
    }


@jax.custom_vjp
def low(v):
    return lax.optimization_barrier(v.astype(jnp.bfloat16)).astype(jnp.float32)

@jax.custom_vjp
def low_back(v):
    return v

def low_keep(v):
    return (low(v), None)

def low_pass(kept, grad):
    return (grad,)

def back_keep(v):
    return (v, None)

def back_low(kept, grad):
    return (low(grad),)
low.defvjp(low_keep, low_pass)
low_back.defvjp(back_keep, back_low)
clip_max = 1.0
beta_one = 0.5
beta_two = 0.5
adam_eps = 1e-08
step_rate = 0.25
norm_eps = 1e-06
trust_eps = 1e-06

def both_round(value):
    return low(low_back(value))

def position_table(table_index):
    index = table_index.astype(jnp.int32)
    kind = (index >= 64).astype(jnp.int32) + (index >= 260).astype(jnp.int32)
    offset = jnp.where(kind == 0, 0, jnp.where(kind == 1, 64, 260)).astype(jnp.int32)
    side = jnp.where(kind == 0, 8, jnp.where(kind == 1, 14, 28)).astype(jnp.int32)
    spacing = jnp.where(kind == 0, 1.75, jnp.where(kind == 1, 1.0, 0.5)).astype(jnp.float32)
    local_index = index - offset
    row_pos = (local_index // side).astype(jnp.float32) * spacing
    col_pos = (local_index % side).astype(jnp.float32) * spacing
    quarter = D // 4
    freqs = jnp.power(10000.0, -jnp.arange(quarter, dtype=jnp.float32) / quarter)
    row_arg = row_pos[:, None] * freqs[None, :]
    col_arg = col_pos[:, None] * freqs[None, :]
    return jnp.concatenate([jnp.sin(row_arg), jnp.cos(row_arg), jnp.sin(col_arg), jnp.cos(col_arg)], axis=1)

def layer_norm(values, gain, shift):
    center = values - lax.optimization_barrier(jnp.mean(values, axis=-1, keepdims=True))
    spread = lax.optimization_barrier(jnp.mean(center * center, axis=-1, keepdims=True))
    return center * lax.rsqrt(spread + norm_eps) * gain + shift

def visible(seg_query, place_query, seg_key, place_key):
    same = (seg_query[:, None] == seg_key[None, :]) & (seg_query[:, None] >= 0)
    return same | (place_query[:, None] == place_key[None, :])

def forward(layer_in, weights, norm_params, segment_ids):
    query_weight, key_weight, value_weight, output_weight, hidden_weight, return_weight = weights
    highest = lax.Precision.HIGHEST
    length = layer_in.shape[0]
    heads = D // HEAD
    scale = 1.0 / math.sqrt(HEAD)
    normed = low(layer_norm(layer_in, norm_params[0], norm_params[1]))
    queries = both_round(jnp.dot(normed, query_weight, precision=highest, preferred_element_type=jnp.float32))
    keys = both_round(jnp.dot(normed, key_weight, precision=highest, preferred_element_type=jnp.float32))
    values = both_round(jnp.dot(normed, value_weight, precision=highest, preferred_element_type=jnp.float32))
    key_heads = keys.reshape(length, heads, HEAD)
    value_heads = values.reshape(length, heads, HEAD)
    block_rows = min(512, length)
    blocks = length // block_rows
    places = jnp.arange(length, dtype=jnp.int32)

    def attend_block(pieces):
        query_block, segment_block, place_block = pieces
        scores = jnp.einsum('qhd,khd->hqk', query_block, key_heads, precision=highest) * scale
        allowed = visible(segment_block, place_block, segment_ids, places)
        scores = low_back(jnp.where(allowed[None], scores, -1e+30))
        peak = lax.optimization_barrier(jnp.max(scores, axis=-1, keepdims=True))
        expon = jnp.exp(scores - peak)
        probs = low(expon / lax.optimization_barrier(jnp.sum(expon, axis=-1, keepdims=True)))
        return jnp.einsum('hqk,khd->qhd', probs, value_heads, precision=highest)
    mixed = lax.map(jax.checkpoint(attend_block), (queries.reshape(blocks, block_rows, heads, HEAD), segment_ids.reshape(blocks, block_rows), places.reshape(blocks, block_rows)))
    mixed = both_round(mixed.reshape(length, D))
    model_part = D // N_MP
    unit_part = FF // N_MP
    attn = jnp.zeros((length, D), jnp.float32)
    for shard in range(N_MP):
        lo_col = shard * model_part
        attn = attn + low(jnp.dot(mixed[:, lo_col:lo_col + model_part], output_weight[lo_col:lo_col + model_part], precision=highest, preferred_element_type=jnp.float32))
    attn = low_back(attn)
    hidden_in = layer_in + attn
    second = low(layer_norm(hidden_in, norm_params[2], norm_params[3]))
    pre = low_back(jnp.dot(second, hidden_weight, precision=highest, preferred_element_type=jnp.float32))
    act = low(jax.nn.gelu(pre, approximate=False))
    mlp = jnp.zeros((length, D), jnp.float32)
    for shard in range(N_MP):
        lo_unit = shard * unit_part
        mlp = mlp + low(jnp.dot(act[:, lo_unit:lo_unit + unit_part], return_weight[lo_unit:lo_unit + unit_part], precision=highest, preferred_element_type=jnp.float32))
    mlp = low_back(mlp)
    return hidden_in + mlp

def to_blocks(matrix):
    row_count, col_count = matrix.shape
    tiles = matrix.reshape(row_count // BLK, BLK, col_count // BLK, BLK)
    return tiles.transpose(0, 2, 1, 3).reshape(-1, BLK, BLK)

def make_blocks(grads, owner_list):
    model_part = D // N_MP
    unit_part = FF // N_MP
    per_shard = []
    for shard in range(N_MP):
        lo_col = shard * model_part
        lo_unit = shard * unit_part
        pieces = [to_blocks(grads[0][:, lo_col:lo_col + model_part]), to_blocks(grads[1][:, lo_col:lo_col + model_part]), to_blocks(grads[2][:, lo_col:lo_col + model_part]), to_blocks(grads[3][lo_col:lo_col + model_part, :]), to_blocks(grads[4][:, lo_unit:lo_unit + unit_part]), to_blocks(grads[5][lo_unit:lo_unit + unit_part, :])]
        local_blocks = jnp.concatenate(pieces, axis=0)
        per_shard.append(jnp.take(local_blocks, owner_list.astype(jnp.int32), axis=0))
    return jnp.stack(per_shard, axis=1)

def reflect_left(matrix, vector):
    coef = 2.0 / lax.optimization_barrier(jnp.sum(vector * vector, axis=-1))
    proj = jnp.einsum('sr,src->sc', vector, matrix, precision=lax.Precision.HIGHEST)
    return matrix - coef[:, None, None] * vector[:, :, None] * proj[:, None, :]

def reflect_right(matrix, vector):
    coef = 2.0 / lax.optimization_barrier(jnp.sum(vector * vector, axis=-1))
    proj = jnp.einsum('src,sc->sr', matrix, vector, precision=lax.Precision.HIGHEST)
    return matrix - coef[:, None, None] * proj[:, :, None] * vector[:, None, :]

def soap_update(grads, first, second, master, left_vec, right_vec, step_value):
    rotated = reflect_right(reflect_left(grads, left_vec), right_vec)
    new_first = beta_one * first + (1.0 - beta_one) * rotated
    new_second = beta_two * second + (1.0 - beta_two) * rotated * rotated
    corr_one = 1.0 - jnp.power(beta_one, step_value)
    corr_two = 1.0 - jnp.power(beta_two, step_value)
    normal_step = new_first / corr_one / (jnp.sqrt(new_second / corr_two) + adam_eps)
    turned = reflect_right(reflect_left(normal_step, left_vec), right_vec)
    trust = jnp.sqrt(lax.optimization_barrier(jnp.mean(master * master, axis=(1, 2))) + trust_eps) / jnp.sqrt(lax.optimization_barrier(jnp.mean(turned * turned, axis=(1, 2))) + trust_eps)
    new_master = master - step_rate * trust[:, None, None] * turned
    return (new_first, new_second, new_master)

def reference(tokens, cotangent, segment_ids, table_index, group_count, owner_list, step_count, query_weight, key_weight, value_weight, output_weight, hidden_weight, return_weight, norm_params, norm_first, norm_second, master_blocks, first_moment, second_moment, left_vector, right_vector):
    weights = tuple((w.astype(jnp.float32) for w in (query_weight, key_weight, value_weight, output_weight, hidden_weight, return_weight)))
    layer_in = tokens.astype(jnp.float32) + position_table(table_index)
    valid_row = (segment_ids >= 0).astype(jnp.float32)
    grad_in = cotangent.astype(jnp.float32) * valid_row[:, None]
    device_count = TOKENS // TOK_DEV

    def group_step(carry, data):
        inputs_g, grads_g, segs_g, count_g = data

        def apply_layer(inputs_x, weights_x, norms_x):
            return forward(inputs_x, weights_x, norms_x, segs_g)
        outputs_g, back_fn = jax.vjp(apply_layer, inputs_g, weights, norm_params)
        input_g, weight_g, norm_g = back_fn(grads_g)
        factor = count_g.astype(jnp.float32)
        new_weights = tuple((acc + factor * part for acc, part in zip(carry[0], weight_g)))
        return ((new_weights, carry[1] + factor * norm_g), (outputs_g, input_g))
    init = (tuple((jnp.zeros_like(w) for w in weights)), jnp.zeros_like(norm_params))
    (weight_sum, norm_sum), (outputs_all, inputs_all) = lax.scan(group_step, init, (layer_in.reshape(device_count, TOK_DEV, D), grad_in.reshape(device_count, TOK_DEV, D), segment_ids.reshape(device_count, TOK_DEV), group_count))
    count_total = jnp.sum(group_count.astype(jnp.float32))
    grads = [w / count_total for w in weight_sum]
    norm_grad = norm_sum / count_total
    blocks = make_blocks(grads, owner_list)
    total_sq = jnp.sum(blocks * blocks) + jnp.sum(norm_grad * norm_grad)
    clip_norm = jnp.sqrt(total_sq)
    factor = jnp.minimum(1.0, clip_max / clip_norm)
    block_grads = blocks * factor
    norm_clipped = norm_grad * factor
    step_value = step_count[0].astype(jnp.float32)
    flat = (NBLK * N_MP, BLK, BLK)
    new_first, new_second, new_master = soap_update(block_grads.reshape(flat), first_moment.reshape(flat), second_moment.reshape(flat), master_blocks.reshape(flat), left_vector.reshape(NBLK * N_MP, BLK), right_vector.reshape(NBLK * N_MP, BLK), step_value)
    shape_out = (NBLK, N_MP, BLK, BLK)
    new_first = new_first.reshape(shape_out)
    new_second = new_second.reshape(shape_out)
    new_master = new_master.reshape(shape_out)
    norm_m = beta_one * norm_first + (1.0 - beta_one) * norm_clipped
    norm_v = beta_two * norm_second + (1.0 - beta_two) * norm_clipped * norm_clipped
    corr_one = 1.0 - jnp.power(beta_one, step_value)
    corr_two = 1.0 - jnp.power(beta_two, step_value)
    norm_new = norm_params - step_rate * (norm_m / corr_one) / (jnp.sqrt(norm_v / corr_two) + adam_eps)
    norm_grads = jnp.stack([norm_clipped, norm_m], axis=0)
    return (outputs_all.reshape(TOKENS, D), inputs_all.reshape(TOKENS, D), block_grads, new_first, new_second, new_master, new_master.astype(jnp.bfloat16), norm_grads, norm_v, norm_new, clip_norm)
```

```python
import functools
import math

import jax
import jax.numpy as jnp
import numpy as np
from jax import lax
from jax.experimental import pallas as pl
from jax.experimental.pallas import tpu as pltpu
from jax.sharding import PartitionSpec as P

D = 1024
HEAD = 64
BLK = 128
LANES = 128
POS_ROWS = 64
SEG_ROWS = 32

clip_max = 1.0
beta_one = 0.5
beta_two = 0.5
adam_eps = 1e-08
step_rate = 0.25
norm_eps = 1e-06
trust_eps = 1e-06

F32 = jnp.float32
BF16 = jnp.bfloat16
VMEM_LIMIT = 48 * 1024 * 1024

ERF_P = 0.425
ERF_COEF = (
    0.11983931305209315,
    0.12092032287702306,
    0.10035292560006456,
    0.12754356284084392,
    -0.051626023300101125,
    0.20380940869554587,
    -0.1565787944569494,
    0.035739213095996265,
)


def position_rows():
    coords = np.concatenate(
        [1.75 * np.arange(8), 1.0 * np.arange(14), 0.5 * np.arange(28), np.zeros(POS_ROWS - 50)]
    )
    quarter = D // 4
    freqs = np.power(np.float32(10000.0), -np.arange(quarter, dtype=np.float32) / np.float32(quarter))
    args = (coords.astype(np.float32)[:, None] * freqs.astype(np.float32)[None, :]).astype(np.float64)
    table = np.concatenate([np.sin(args), np.cos(args)], axis=1).astype(np.float32)
    parts = []
    rest = table
    for _ in range(3):
        part = rest.astype(jnp.bfloat16)
        parts.append(part)
        rest = rest - part.astype(np.float32)
    return np.concatenate(parts, axis=0)


def dot_nn(left, right):
    return lax.dot_general(left, right, (((1,), (0,)), ((), ())), preferred_element_type=F32)


def dot_nt(left, right):
    return lax.dot_general(left, right, (((1,), (1,)), ((), ())), preferred_element_type=F32)


def dot_tn(left, right):
    return lax.dot_general(left, right, (((0,), (0,)), ((), ())), preferred_element_type=F32)


def norm_hat(values):
    center = values - jnp.mean(values, axis=-1, keepdims=True)
    inv_std = lax.rsqrt(jnp.mean(center * center, axis=-1, keepdims=True) + norm_eps)
    return (center * inv_std, inv_std)


def norm_back(grad_out, normal, inv_std, gain):
    scaled = grad_out * gain
    return inv_std * (
        scaled
        - jnp.mean(scaled, axis=-1, keepdims=True)
        - normal * jnp.mean(scaled * normal, axis=-1, keepdims=True)
    )


def gelu_parts(values):
    bell = jnp.exp(-0.5 * values * values)
    t = 1.0 / (1.0 + (ERF_P / math.sqrt(2.0)) * jnp.abs(values))
    poly = ERF_COEF[-1]
    for coef in ERF_COEF[-2::-1]:
        poly = poly * t + coef
    tail = poly * t * bell
    dist = jnp.where(values >= 0.0, 1.0 - tail, tail)
    return (values * dist, dist + values * ((1.0 / math.sqrt(2.0 * math.pi)) * bell))


def item_rows(seg_row):
    rows = lax.broadcasted_iota(jnp.int32, (SEG_ROWS, seg_row.shape[1]), 0)
    return jnp.where(rows == seg_row, 1.0, 0.0).astype(BF16)


def head_lanes(rows, head):
    lanes = lax.broadcasted_iota(jnp.int32, (rows, LANES), 1)
    return (lanes < HEAD) if head == 0 else (lanes >= HEAD)


def forward_kernel(
    me_ref,
    tok_ref,
    index_ref,
    seg_ref,
    table_ref,
    norm_ref,
    wq_ref,
    wk_ref,
    wv_ref,
    wo_ref,
    layer_ref,
    normed_ref,
    q_ref,
    k_ref,
    v_ref,
    mixed_ref,
    lse_ref,
    bias_ref,
    keep_ref,
    send_ref,
    part_ref,
):
    length = tok_ref.shape[0]
    index = index_ref[...]
    big = index >= 260
    mid = index >= 64
    offset = jnp.where(big, 260, jnp.where(mid, 64, 0))
    base = jnp.where(big, 22, jnp.where(mid, 8, 0))
    side = jnp.where(big, 28, jnp.where(mid, 14, 8))
    local = index - offset
    inv_side = jnp.where(big, 1.0 / 28.0, jnp.where(mid, 1.0 / 14.0, 1.0 / 8.0)).astype(F32)
    row = jnp.floor((local.astype(F32) + 0.5) * inv_side).astype(jnp.int32)
    col = local - row * side
    rows_iota = lax.broadcasted_iota(jnp.int32, (3 * POS_ROWS, length), 0)
    rows_iota = rows_iota & (POS_ROWS - 1)
    row_hot = jnp.where(rows_iota == base + row, 1.0, 0.0).astype(BF16)
    col_hot = jnp.where(rows_iota == base + col, 1.0, 0.0).astype(BF16)
    table = table_ref[...]
    items = item_rows(seg_ref[...])
    same = dot_tn(items, items)
    diag = lax.broadcasted_iota(jnp.int32, (length, length), 0) == lax.broadcasted_iota(
        jnp.int32, (length, length), 1
    )
    bias_ref[...] = jnp.where((same > 0.5) | diag, 0.0, -1e30)
    half = D // 2
    layer_ref[:, :half] = dot_tn(row_hot, table) + tok_ref[:, :half].astype(F32)
    layer_ref[:, half:] = dot_tn(col_hot, table) + tok_ref[:, half:].astype(F32)
    step = 128
    for at in range(0, length, step):
        rows = slice(at, at + step)
        hat, _ = norm_hat(layer_ref[rows, :])
        normed_ref[rows, :] = (hat * norm_ref[0:1, :] + norm_ref[1:2, :]).astype(BF16)
    normed = normed_ref[...]
    q_ref[...] = dot_nn(normed, wq_ref[...]).astype(BF16)
    k_ref[...] = dot_nn(normed, wk_ref[...]).astype(BF16)
    v_ref[...] = dot_nn(normed, wv_ref[...]).astype(BF16)
    scale = 1.0 / math.sqrt(HEAD)
    for pair in range(q_ref.shape[1] // LANES):
        cols = slice(pair * LANES, (pair + 1) * LANES)
        keys = k_ref[:, cols]
        vals = v_ref[:, cols]
        for at in range(0, length, step):
            rows = slice(at, at + step)
            query = q_ref[rows, cols] * scale
            outs = []
            for head in range(2):
                here = head_lanes(step, head)
                scores = dot_nt(jnp.where(here, query, 0.0).astype(BF16), keys) + bias_ref[rows, :]
                peak = jnp.max(scores, axis=-1, keepdims=True)
                expon = jnp.exp(scores - peak)
                total = jnp.sum(expon, axis=-1, keepdims=True)
                outs.append(dot_nn(expon.astype(BF16), vals) * (1.0 / total))
                number = pair * 2 + head
                lse_ref[rows, number : number + 1] = peak + jnp.log(total)
            mixed_ref[rows, cols] = jnp.where(head_lanes(step, 0), outs[0], outs[1]).astype(BF16)
    part_ref[...] = dot_nn(mixed_ref[...], wo_ref[...]).astype(BF16)
    split_halves(me_ref, part_ref, keep_ref, send_ref)


def split_halves(me_ref, part_ref, keep_ref, send_ref):
    half = keep_ref.shape[0]
    bit = me_ref[1] & 1
    keep_ref[...] = part_ref[pl.ds(pl.multiple_of(bit * half, half), half), :]
    send_ref[...] = part_ref[pl.ds(pl.multiple_of((1 - bit) * half, half), half), :]


def grad_out_kernel(cot_ref, seg_ref, wr_ref, gout_ref, gact_ref):
    items = item_rows(seg_ref[...])
    valid = dot_tn(items, jnp.ones((SEG_ROWS, LANES), BF16))
    for at in range(0, D, LANES):
        cols = slice(at, at + LANES)
        gout_ref[:, cols] = (cot_ref[:, cols].astype(F32) * valid).astype(BF16)
    gact_ref[...] = dot_nt(gout_ref[...], wr_ref[...])


def feed_kernel(
    me_ref,
    own_ref,
    other_ref,
    layer_ref,
    norm_ref,
    wh_ref,
    gact_ref,
    hid_ref,
    second_ref,
    act_ref,
    gpre_ref,
    keep_ref,
    send_ref,
    pre_ref,
):
    half = own_ref.shape[0]
    bit = me_ref[1] & 1
    step = 64
    for part_ref, which, out_ref in ((other_ref, 1 - bit, send_ref), (own_ref, bit, keep_ref)):
        start = pl.multiple_of(which * half, half)

        @pl.loop(0, half // step)
        def _(i, part_ref=part_ref, start=start):
            at = pl.multiple_of(i * step, step)
            rows = pl.ds(pl.multiple_of(start + at, step), step)
            hid = layer_ref[rows, :] + part_ref[pl.ds(at, step), :].astype(F32)
            hid_ref[rows, :] = hid
            hat, _ = norm_hat(hid)
            second_ref[rows, :] = (hat * norm_ref[2:3, :] + norm_ref[3:4, :]).astype(BF16)

        rows = pl.ds(start, half)
        pre_ref[...] = dot_nn(second_ref[rows, :], wh_ref[...])

        @pl.loop(0, half // 32)
        def _(i, start=start):
            at = pl.multiple_of(i * 32, 32)
            rows = pl.ds(pl.multiple_of(start + at, 32), 32)
            act, slope = gelu_parts(pre_ref[pl.ds(at, 32), :])
            act_ref[rows, :] = act.astype(BF16)
            gpre_ref[rows, :] = (gact_ref[rows, :] * slope).astype(BF16)

        out_ref[...] = dot_nt(gpre_ref[rows, :], wh_ref[...]).astype(BF16)


def store_blocks(nat_ref, base, left_ref, right_ref, weight):
    width = right_ref.shape[1]
    across = width // BLK
    wide = 256
    left = left_ref[...]
    for at in range(0, width, wide):
        grad = (dot_tn(left, right_ref[:, at : at + wide]) * weight).astype(BF16)
        for i in range(left_ref.shape[1] // BLK):
            for j in range(wide // BLK):
                nat_ref[base + i * across + at // BLK + j] = grad[
                    i * BLK : (i + 1) * BLK, j * BLK : (j + 1) * BLK
                ]


def feed_grad_kernel(
    me_ref,
    scal_ref,
    act_ref,
    gout_ref,
    second_ref,
    gpre_ref,
    wr_ref,
    nat_ref,
    keep_ref,
    send_ref,
    part_ref,
):
    weight = scal_ref[0]
    store_blocks(nat_ref, 0, second_ref, gpre_ref, weight)
    store_blocks(nat_ref, 64, act_ref, gout_ref, weight)
    part_ref[...] = dot_nn(act_ref[...], wr_ref[...]).astype(BF16)
    split_halves(me_ref, part_ref, keep_ref, send_ref)


def bit_reverse(value, bits):
    out = 0
    for i in range(bits):
        out |= ((value >> i) & 1) << (bits - 1 - i)
    return out


def backward_kernel(
    chunks,
    n_dp,
    me_ref,
    owner_ref,
    scal_ref,
    own_ref,
    other_ref,
    hid_ref,
    gout_ref,
    norm_ref,
    normed_ref,
    q_ref,
    k_ref,
    v_ref,
    mixed_ref,
    lse_ref,
    bias_ref,
    wo_ref,
    early_ref,
    *rest,
):
    ghid_ref, gq_ref, gk_ref, gv_ref = rest[:4]
    chunk_refs = rest[4 : 4 + 2 * len(chunks)]
    gattn_ref, gmix_ref, late_ref = rest[4 + 2 * len(chunks) :]
    half = own_ref.shape[0]
    length = 2 * half
    bit = me_ref[1] & 1
    weight = scal_ref[0]
    step = 64
    for part_ref, which in ((other_ref, 1 - bit), (own_ref, bit)):
        start = pl.multiple_of(which * half, half)

        @pl.loop(0, half // step)
        def _(i, part_ref=part_ref, start=start):
            at = pl.multiple_of(i * step, step)
            rows = pl.ds(pl.multiple_of(start + at, step), step)
            hat, inv_std = norm_hat(hid_ref[rows, :])
            grad = part_ref[pl.ds(at, step), :].astype(F32)
            ghid = gout_ref[rows, :].astype(F32) + norm_back(grad, hat, inv_std, norm_ref[2:3, :])
            ghid_ref[rows, :] = ghid
            gattn_ref[rows, :] = ghid.astype(BF16)

    gmix_ref[...] = dot_nt(gattn_ref[...], wo_ref[...]).astype(BF16)
    scale = 1.0 / math.sqrt(HEAD)
    step = 128
    for pair in range(q_ref.shape[1] // LANES):
        cols = slice(pair * LANES, (pair + 1) * LANES)
        keys = k_ref[:, cols]
        vals = v_ref[:, cols]
        grad_keys = [None, None]
        grad_vals = [None, None]
        for at in range(0, length, step):
            rows = slice(at, at + step)
            query = q_ref[rows, cols] * scale
            gmix = gmix_ref[rows, cols]
            grad_query = []
            for head in range(2):
                here = head_lanes(step, head)
                number = pair * 2 + head
                scores = dot_nt(jnp.where(here, query, 0.0).astype(BF16), keys) + bias_ref[rows, :]
                probs = jnp.exp(scores - lse_ref[rows, number : number + 1])
                grad_probs = dot_nt(jnp.where(here, gmix, 0.0).astype(BF16), vals)
                grad_scores = (
                    probs * (grad_probs - jnp.sum(probs * grad_probs, axis=-1, keepdims=True))
                ).astype(BF16)
                gv = dot_tn(probs.astype(BF16), gmix)
                gk = dot_tn(grad_scores, query)
                grad_vals[head] = gv if at == 0 else grad_vals[head] + gv
                grad_keys[head] = gk if at == 0 else grad_keys[head] + gk
                grad_query.append(dot_nn(grad_scores, keys))
            first = head_lanes(step, 0)
            gq_ref[rows, cols] = (jnp.where(first, grad_query[0], grad_query[1]) * scale).astype(
                BF16
            )
        first = head_lanes(length, 0)
        gk_ref[:, cols] = jnp.where(first, grad_keys[0], grad_keys[1]).astype(BF16)
        gv_ref[:, cols] = jnp.where(first, grad_vals[0], grad_vals[1]).astype(BF16)
    store_blocks(late_ref, 0, normed_ref, gq_ref, weight)
    store_blocks(late_ref, 16, normed_ref, gk_ref, weight)
    store_blocks(late_ref, 32, normed_ref, gv_ref, weight)
    store_blocks(late_ref, 48, mixed_ref, gattn_ref, weight)
    slots = sum(chunks)
    bits = n_dp.bit_length() - 1
    offset = 0
    for number, count in enumerate(chunks):
        for order in range(n_dp):
            dest = me_ref[0] ^ bit_reverse(order, bits)
            out_ref = chunk_refs[2 * number + (0 if order < n_dp // 2 else 1)]
            at = (order % (n_dp // 2)) * count
            for j in range(count):
                block = owner_ref[dest * slots + offset + j]
                out_ref[at + j] = jnp.where(
                    block < late_ref.shape[0],
                    late_ref[jnp.minimum(block, late_ref.shape[0] - 1)],
                    early_ref[jnp.maximum(block - late_ref.shape[0], 0)],
                )
        offset += count


def normed_grad_kernel(
    me_ref, gq_ref, gk_ref, gv_ref, wq_ref, wk_ref, wv_ref, keep_ref, send_ref, part_ref
):
    part_ref[...] = (
        dot_nt(gq_ref[...], wq_ref[...])
        + dot_nt(gk_ref[...], wk_ref[...])
        + dot_nt(gv_ref[...], wv_ref[...])
    ).astype(BF16)
    split_halves(me_ref, part_ref, keep_ref, send_ref)


def finish_kernel(
    me_ref,
    scal_ref,
    normed_own_ref,
    normed_other_ref,
    mlp_own_ref,
    mlp_other_ref,
    second_own_ref,
    second_other_ref,
    layer_ref,
    hid_ref,
    ghid_ref,
    norm_ref,
    out_ref,
    gin_ref,
    sums_ref,
):
    half = mlp_own_ref.shape[0]
    bit = me_ref[1] & 1
    weight = scal_ref[0]
    step = 32
    sums_ref[...] = jnp.zeros_like(sums_ref)
    for first_ref, mlp_ref, second_ref, which in (
        (normed_other_ref, mlp_other_ref, second_other_ref, 1 - bit),
        (normed_own_ref, mlp_own_ref, second_own_ref, bit),
    ):
        start = pl.multiple_of(which * half, half)

        @pl.loop(0, half // step)
        def _(i, first_ref=first_ref, mlp_ref=mlp_ref, second_ref=second_ref, start=start):
            at = pl.multiple_of(i * step, step)
            here = pl.ds(at, step)
            rows = pl.ds(pl.multiple_of(start + at, step), step)
            hid = hid_ref[rows, :]
            out_ref[rows, :] = hid + mlp_ref[here, :].astype(F32)
            hat, inv_std = norm_hat(layer_ref[rows, :])
            grad = first_ref[here, :].astype(F32)
            gin_ref[rows, :] = ghid_ref[rows, :] + norm_back(grad, hat, inv_std, norm_ref[0:1, :])
            hat2, _ = norm_hat(hid)
            grad2 = second_ref[here, :].astype(F32)
            sums_ref[0:8, :] += jnp.sum((grad * hat).reshape(step // 8, 8, D), axis=0)
            sums_ref[8:16, :] += jnp.sum(grad.reshape(step // 8, 8, D), axis=0)
            sums_ref[16:24, :] += jnp.sum((grad2 * hat2).reshape(step // 8, 8, D), axis=0)
            sums_ref[24:32, :] += jnp.sum(grad2.reshape(step // 8, 8, D), axis=0)

    total = [
        jnp.sum(sums_ref[8 * i : 8 * i + 8, :], axis=0, keepdims=True) * weight for i in range(4)
    ]
    total.append(jnp.full((1, D), weight, F32))
    total.append(jnp.zeros((3, D), F32))
    sums_ref[0:8, :] = jnp.concatenate(total, axis=0)


def reflect(matrix, left, right):
    coef_left = 2.0 / jnp.sum(left[:, 0:1] * left[:, 0:1])
    coef_right = 2.0 / jnp.sum(right * right)
    matrix = matrix - (coef_left * left) * jnp.sum(left * matrix, axis=0, keepdims=True)
    return matrix - (coef_right * right) * jnp.sum(matrix * right, axis=1, keepdims=True)


def column(row):
    return jnp.transpose(jnp.broadcast_to(row, (BLK, BLK)))


def rotate_kernel(chunks, norm_ref, left_ref, right_ref, *rest):
    parts = rest[: 2 * len(chunks)]
    grad_ref, rot_ref, square_ref = rest[2 * len(chunks) :]
    inverse = 1.0 / norm_ref[4:5, 0:BLK]
    slot = 0
    square = jnp.zeros((8, BLK), F32)
    for number, count in enumerate(chunks):
        keep_ref, recv_ref = parts[2 * number : 2 * number + 2]
        for j in range(count):
            grad = (keep_ref[j].astype(F32) + recv_ref[j].astype(F32)) * inverse
            grad_ref[slot] = grad
            square = square + jnp.sum((grad * grad).reshape(BLK // 8, 8, BLK), axis=0)
            rot_ref[slot] = reflect(
                grad, column(left_ref[slot : slot + 1, :]), right_ref[slot : slot + 1, :]
            )
            slot += 1
    square_ref[...] = jnp.full((8, BLK), jnp.sum(square), F32)


def update_kernel(
    group,
    scal_ref,
    square_ref,
    sums_ref,
    norm_ref,
    norm_first_ref,
    norm_second_ref,
    left_ref,
    right_ref,
    grad_ref,
    rot_ref,
    first_ref,
    second_ref,
    master_ref,
    out_grad_ref,
    out_first_ref,
    out_second_ref,
    out_master_ref,
    out_copy_ref,
    norm_pair_ref,
    norm_square_ref,
    norm_value_ref,
    clip_ref,
):
    inv_one = 1.0 / scal_ref[1]
    inv_two = 1.0 / scal_ref[2]
    norm_grad = sums_ref[0:4, :] * (1.0 / sums_ref[4:5, :])
    total = square_ref[0:1, :] + jnp.sum(norm_grad * norm_grad)
    clip_norm = jnp.sqrt(total)
    factor = jnp.minimum(1.0, clip_max / clip_norm)
    at = pl.program_id(0)

    @pl.when(at == 0)
    def _():
        clip_ref[...] = jnp.broadcast_to(clip_norm, clip_ref.shape)
        clipped = norm_grad * factor[:, 0:1]
        first = beta_one * norm_first_ref[...] + (1.0 - beta_one) * clipped
        second = beta_two * norm_second_ref[...] + (1.0 - beta_two) * clipped * clipped
        norm_pair_ref[0] = clipped
        norm_pair_ref[1] = first
        norm_square_ref[...] = second
        norm_value_ref[...] = norm_ref[...] - step_rate * (first * inv_one) / (
            jnp.sqrt(second * inv_two) + adam_eps
        )

    for i in range(group):
        slot = at * group + i
        left = column(left_ref[pl.ds(slot, 1), :])
        right = right_ref[pl.ds(slot, 1), :]
        out_grad_ref[i] = grad_ref[i] * factor
        rotated = rot_ref[i] * factor
        first = beta_one * first_ref[i] + (1.0 - beta_one) * rotated
        second = beta_two * second_ref[i] + (1.0 - beta_two) * rotated * rotated
        out_first_ref[i] = first
        out_second_ref[i] = second
        normal = (first * inv_one) / (jnp.sqrt(second * inv_two) + adam_eps)
        turned = reflect(normal, left, right)
        master = master_ref[i]
        entries = 1.0 / (BLK * BLK)
        trust = jnp.sqrt(jnp.sum(master * master) * entries + trust_eps) / jnp.sqrt(
            jnp.sum(turned * turned) * entries + trust_eps
        )
        fresh = master - (step_rate * trust) * turned
        out_master_ref[i] = fresh
        out_copy_ref[i] = fresh.astype(BF16)


def vmem():
    return pl.BlockSpec(memory_space=pltpu.VMEM)


def smem():
    return pl.BlockSpec(memory_space=pltpu.SMEM)


def call(kernel, name, n_smem, ins, outs, scratch=(), flops=0):
    return pl.pallas_call(
        kernel,
        name=name,
        out_shape=[jax.ShapeDtypeStruct(shape, kind) for shape, kind in outs],
        in_specs=[smem()] * n_smem + [vmem()] * (len(ins) - n_smem),
        out_specs=[vmem()] * len(outs),
        scratch_shapes=[pltpu.VMEM(shape, kind) for shape, kind in scratch],
        compiler_params=pltpu.CompilerParams(vmem_limit_bytes=VMEM_LIMIT),
        cost_estimate=pl.CostEstimate(flops=int(flops), bytes_accessed=4 << 20, transcendentals=0),
    )(*ins)


def swap(value, axis, bit):
    count = lax.axis_size(axis)
    return lax.ppermute(value, axis, [(i, i ^ bit) for i in range(count)])


def plus(left, right):
    return (left.astype(F32) + right.astype(F32)).astype(BF16)


def mp_sum(keep, send):
    total = plus(keep, swap(send, "mp", 1))
    bit = 2
    while bit < lax.axis_size("mp"):
        total = plus(total, swap(total, "mp", bit))
        bit *= 2
    return (total, swap(total, "mp", 1))


def split_counts(slots):
    if slots >= 12:
        tail = slots // 6
        head = (slots - tail) // 2
        return (slots - tail - head, head, tail)
    return (1,) * slots if slots <= 3 else (slots - slots // 2, slots // 2)


def shards(
    tokens,
    cotangent,
    segment_ids,
    table_index,
    group_count,
    owner_list,
    step_count,
    query_weight,
    key_weight,
    value_weight,
    output_weight,
    hidden_weight,
    return_weight,
    norm_params,
    norm_first,
    norm_second,
    master_blocks,
    first_moment,
    second_moment,
    left_vector,
    right_vector,
):
    length = tokens.shape[0]
    half = length // 2
    width = query_weight.shape[1]
    units = hidden_weight.shape[1]
    slots = master_blocks.shape[0]
    blocks = owner_list.shape[0]
    n_dp = lax.axis_size("dp")
    me = jnp.stack([lax.axis_index("dp"), lax.axis_index("mp")]).astype(jnp.int32)
    step_value = step_count[0].astype(F32)
    scal = jnp.stack(
        [
            group_count[0].astype(F32),
            1.0 - jnp.power(beta_one, step_value),
            1.0 - jnp.power(beta_two, step_value),
        ]
    )
    seg_row = segment_ids.reshape(1, length)
    index_row = table_index.reshape(1, length)
    table = jnp.asarray(position_rows())
    rows_d = (length, D)
    half_d = (half, D)
    unit = 2 * length * D * D

    layer_in, normed, q, k, v, mixed, lse, bias, keep, send = call(
        forward_kernel,
        "attention_forward",
        1,
        (
            me,
            tokens,
            index_row,
            seg_row,
            table,
            norm_params,
            query_weight,
            key_weight,
            value_weight,
            output_weight,
        ),
        [
            (rows_d, F32),
            (rows_d, BF16),
            ((length, width), BF16),
            ((length, width), BF16),
            ((length, width), BF16),
            ((length, width), BF16),
            ((length, width // HEAD), F32),
            ((length, length), F32),
            (half_d, BF16),
            (half_d, BF16),
        ],
        [(rows_d, BF16)],
        flops=5 * unit,
    )
    attn_own, attn_other = mp_sum(keep, send)
    grad_out, grad_act = call(
        grad_out_kernel,
        "grad_of_act",
        0,
        (cotangent, seg_row, return_weight),
        [(rows_d, BF16), ((length, units), F32)],
        flops=2 * unit,
    )
    hidden_in, second, act, grad_pre, keep, send = call(
        feed_kernel,
        "feed_forward",
        1,
        (me, attn_own, attn_other, layer_in, norm_params, hidden_weight, grad_act),
        [
            (rows_d, F32),
            (rows_d, BF16),
            ((length, units), BF16),
            ((length, units), BF16),
            (half_d, BF16),
            (half_d, BF16),
        ],
        [((half, units), F32)],
        flops=8 * unit,
    )
    second_own, second_other = mp_sum(keep, send)
    nat, keep, send = call(
        feed_grad_kernel,
        "feed_weight_grads",
        2,
        (me, scal, act, grad_out, second, grad_pre, return_weight),
        [((blocks - blocks // 3, BLK, BLK), BF16), (half_d, BF16), (half_d, BF16)],
        [(rows_d, BF16)],
        flops=6 * unit,
    )
    mlp_own, mlp_other = mp_sum(keep, send)
    chunks = split_counts(slots)
    chunk_shapes = []
    for count in chunks:
        chunk_shapes += [((n_dp // 2 * count, BLK, BLK), BF16)] * 2
    ins = (
        me,
        owner_list,
        scal,
        second_own,
        second_other,
        hidden_in,
        grad_out,
        norm_params,
        normed,
        q,
        k,
        v,
        mixed,
        lse,
        bias,
        output_weight,
        nat,
    )
    outs = call(
        functools.partial(backward_kernel, chunks, n_dp),
        "attention_backward",
        3,
        ins,
        [
            (rows_d, F32),
            ((length, width), BF16),
            ((length, width), BF16),
            ((length, width), BF16),
        ]
        + chunk_shapes,
        [(rows_d, BF16), ((length, width), BF16), ((blocks // 3, BLK, BLK), BF16)],
        flops=10 * unit,
    )
    grad_hid, gq, gk, gv = outs[:4]
    chunk_arrays = outs[4:]
    keep, send = call(
        normed_grad_kernel,
        "grad_of_normed",
        1,
        (me, gq, gk, gv, query_weight, key_weight, value_weight),
        [(half_d, BF16), (half_d, BF16)],
        [(rows_d, BF16)],
        flops=unit,
    )
    normed_own, normed_other = mp_sum(keep, send)

    state = [(chunk_arrays[2 * i], chunk_arrays[2 * i + 1]) for i in range(len(chunks))]
    pending = []
    for keep, send in state:
        bit = 1
        while True:
            got = swap(send, "dp", bit)
            bit *= 2
            if bit >= n_dp:
                break
            n = keep.shape[0] // 2
            keep, send = plus(keep[:n], got[:n]), plus(keep[n:], got[n:])
        pending += [keep, got]

    out, input_grad, sums = call(
        finish_kernel,
        "layer_outputs",
        2,
        (
            me,
            scal,
            normed_own,
            normed_other,
            mlp_own,
            mlp_other,
            second_own,
            second_other,
            layer_in,
            hidden_in,
            grad_hid,
            norm_params,
        ),
        [(rows_d, F32), (rows_d, F32), ((32, D), F32)],
        flops=2 * unit,
    )
    sums = sums[0:8]
    bit = 1
    while bit < n_dp:
        sums = sums + swap(sums, "dp", bit)
        bit *= 2
    left = left_vector.reshape(slots, BLK)
    right = right_vector.reshape(slots, BLK)
    grads, rotated, square = call(
        functools.partial(rotate_kernel, chunks),
        "rotate",
        0,
        (sums, left, right, *pending),
        [((slots, BLK, BLK), F32), ((slots, BLK, BLK), F32), ((8, BLK), F32)],
        flops=unit,
    )
    for axis in ("mp", "dp"):
        bit = 1
        while bit < lax.axis_size(axis):
            square = square + swap(square, axis, bit)
            bit *= 2
    group = max(g for g in range(1, 7) if slots % g == 0)
    block_spec = pl.BlockSpec((group, BLK, BLK), lambda i: (i, 0, 0))

    def whole(shape):
        return pl.BlockSpec(shape, lambda i: (0,) * len(shape))

    shape_block = jax.ShapeDtypeStruct((slots, BLK, BLK), F32)
    new = pl.pallas_call(
        functools.partial(update_kernel, group),
        name="update",
        grid=(slots // group,),
        out_shape=[shape_block] * 4
        + [
            jax.ShapeDtypeStruct((slots, BLK, BLK), BF16),
            jax.ShapeDtypeStruct((2, 4, D), F32),
            jax.ShapeDtypeStruct((4, D), F32),
            jax.ShapeDtypeStruct((4, D), F32),
            jax.ShapeDtypeStruct((8, BLK), F32),
        ],
        in_specs=[
            smem(),
            whole((8, BLK)),
            whole((8, D)),
            whole((4, D)),
            whole((4, D)),
            whole((4, D)),
            whole((slots, BLK)),
            whole((slots, BLK)),
        ]
        + [block_spec] * 5,
        out_specs=[block_spec] * 5
        + [whole((2, 4, D)), whole((4, D)), whole((4, D)), whole((8, BLK))],
        compiler_params=pltpu.CompilerParams(vmem_limit_bytes=VMEM_LIMIT),
    )(
        scal,
        square,
        sums,
        norm_params,
        norm_first,
        norm_second,
        left,
        right,
        grads,
        rotated,
        first_moment.reshape(slots, BLK, BLK),
        second_moment.reshape(slots, BLK, BLK),
        master_blocks.reshape(slots, BLK, BLK),
    )
    shard_shape = (slots, 1, BLK, BLK)
    return (
        out,
        input_grad,
        new[0].reshape(shard_shape),
        new[1].reshape(shard_shape),
        new[2].reshape(shard_shape),
        new[3].reshape(shard_shape),
        new[4].reshape(shard_shape),
        new[5],
        new[6],
        new[7],
        new[8][0, 0],
    )


def solution(mesh):
    placed = (
        P("dp", None),
        P("dp", None),
        P("dp"),
        P("dp"),
        P("dp"),
        P(),
        P(),
        P(None, "mp"),
        P(None, "mp"),
        P(None, "mp"),
        P("mp", None),
        P(None, "mp"),
        P("mp", None),
        P(),
        P(),
        P(),
        P("dp", "mp", None, None),
        P("dp", "mp", None, None),
        P("dp", "mp", None, None),
        P("dp", "mp", None),
        P("dp", "mp", None),
    )
    return jax.shard_map(
        shards,
        mesh=mesh,
        in_specs=placed,
        out_specs=(
            P("dp", None),
            P("dp", None),
            P("dp", "mp", None, None),
            P("dp", "mp", None, None),
            P("dp", "mp", None, None),
            P("dp", "mp", None, None),
            P("dp", "mp", None, None),
            P(),
            P(),
            P(),
            P(),
        ),
        check_vma=False,
    )
```

```python
import functools
import math

import jax
import jax.numpy as jnp
import numpy as np
from jax import lax
from jax.experimental import pallas as pl
from jax.experimental.pallas import tpu as pltpu
from jax.sharding import PartitionSpec as P

D = 1024
HEAD = 64
BLK = 128
LANES = 128
POS_ROWS = 64
SEG_ROWS = 32

clip_max = 1.0
beta_one = 0.5
beta_two = 0.5
adam_eps = 1e-08
step_rate = 0.25
norm_eps = 1e-06
trust_eps = 1e-06

F32 = jnp.float32
BF16 = jnp.bfloat16
MIB = 1024 * 1024
VMEM_LIMIT = 60 * MIB

ERF_P = 0.425
ERF_COEF = (
    0.11983931305209315,
    0.12092032287702306,
    0.10035292560006456,
    0.12754356284084392,
    -0.051626023300101125,
    0.20380940869554587,
    -0.1565787944569494,
    0.035739213095996265,
)


def position_rows():
    coords = np.concatenate(
        [1.75 * np.arange(8), 1.0 * np.arange(14), 0.5 * np.arange(28), np.zeros(POS_ROWS - 50)]
    )
    quarter = D // 4
    freqs = np.power(np.float32(10000.0), -np.arange(quarter, dtype=np.float32) / np.float32(quarter))
    args = (coords.astype(np.float32)[:, None] * freqs.astype(np.float32)[None, :]).astype(np.float64)
    table = np.concatenate([np.sin(args), np.cos(args)], axis=1).astype(np.float32)
    parts = []
    rest = table
    for _ in range(3):
        part = rest.astype(jnp.bfloat16)
        parts.append(part)
        rest = rest - part.astype(np.float32)
    return np.concatenate(parts, axis=0)


def dot_nn(left, right):
    return lax.dot_general(left, right, (((1,), (0,)), ((), ())), preferred_element_type=F32)


def dot_nt(left, right):
    return lax.dot_general(left, right, (((1,), (1,)), ((), ())), preferred_element_type=F32)


def dot_tn(left, right):
    return lax.dot_general(left, right, (((0,), (0,)), ((), ())), preferred_element_type=F32)


def norm_hat(values):
    center = values - jnp.mean(values, axis=-1, keepdims=True)
    inv_std = lax.rsqrt(jnp.mean(center * center, axis=-1, keepdims=True) + norm_eps)
    return (center * inv_std, inv_std)


def norm_back(grad_out, normal, inv_std, gain):
    scaled = grad_out * gain
    return inv_std * (
        scaled
        - jnp.mean(scaled, axis=-1, keepdims=True)
        - normal * jnp.mean(scaled * normal, axis=-1, keepdims=True)
    )


def gelu_parts(values):
    bell = jnp.exp(-0.5 * values * values)
    t = 1.0 / (1.0 + (ERF_P / math.sqrt(2.0)) * jnp.abs(values))
    poly = ERF_COEF[-1]
    for coef in ERF_COEF[-2::-1]:
        poly = poly * t + coef
    tail = poly * t * bell
    dist = jnp.where(values >= 0.0, 1.0 - tail, tail)
    return (values * dist, dist + values * ((1.0 / math.sqrt(2.0 * math.pi)) * bell))


def item_rows(seg_row):
    rows = lax.broadcasted_iota(jnp.int32, (SEG_ROWS, seg_row.shape[1]), 0)
    return jnp.where(rows == seg_row, 1.0, 0.0).astype(BF16)


def head_lanes(rows, head):
    lanes = lax.broadcasted_iota(jnp.int32, (rows, LANES), 1)
    return (lanes < HEAD) if head == 0 else (lanes >= HEAD)


def position_hots(index):
    length = index.shape[1]
    big = index >= 260
    mid = index >= 64
    offset = jnp.where(big, 260, jnp.where(mid, 64, 0))
    base = jnp.where(big, 22, jnp.where(mid, 8, 0))
    side = jnp.where(big, 28, jnp.where(mid, 14, 8))
    inv_side = jnp.where(big, 1.0 / 28.0, jnp.where(mid, 1.0 / 14.0, 1.0 / 8.0)).astype(F32)
    local = index - offset
    row = jnp.floor((local.astype(F32) + 0.5) * inv_side).astype(jnp.int32)
    col = local - row * side
    rows = lax.broadcasted_iota(jnp.int32, (3 * POS_ROWS, length), 0) & (POS_ROWS - 1)
    row_hot = jnp.where(rows == base + row, 1.0, 0.0).astype(BF16)
    col_hot = jnp.where(rows == base + col, 1.0, 0.0).astype(BF16)
    return (row_hot, col_hot)


def fill_layer(out_ref, index_row, table, tok_ref, sum_ref=None):
    half = D // 2
    for hot, cols in zip(position_hots(index_row), (slice(0, half), slice(half, D))):
        value = dot_tn(hot, table) + tok_ref[:, cols].astype(F32)
        if sum_ref is not None:
            value = value + sum_ref[:, cols].astype(F32)
        out_ref[:, cols] = value


def fill_bias(bias_ref, seg_row):
    length = seg_row.shape[1]
    items = item_rows(seg_row)
    same = dot_tn(items, items)
    diag = lax.broadcasted_iota(jnp.int32, (length, length), 0) == lax.broadcasted_iota(
        jnp.int32, (length, length), 1
    )
    bias_ref[...] = jnp.where((same > 0.5) | diag, 0.0, -1e30)


def attend(q_ref, k_ref, v_ref, bias_ref, mixed_ref, lse_ref):
    count = q_ref.shape[0]
    scale = 1.0 / math.sqrt(HEAD)
    step = 512
    for pair in range(q_ref.shape[1] // LANES):
        cols = slice(pair * LANES, (pair + 1) * LANES)
        keys = k_ref[:, cols]
        vals = v_ref[:, cols]
        for at in range(0, count, step):
            rows = slice(at, at + step)
            query = q_ref[rows, cols] * scale
            outs = []
            for head in range(2):
                here = head_lanes(step, head)
                scores = dot_nt(jnp.where(here, query, 0.0).astype(BF16), keys) + bias_ref[rows, :]
                peak = jnp.max(scores, axis=-1, keepdims=True)
                expon = jnp.exp(scores - peak)
                total = jnp.sum(expon, axis=-1, keepdims=True)
                outs.append(dot_nn(expon.astype(BF16), vals) * (1.0 / total))
                number = pair * 2 + head
                lse_ref[rows, number : number + 1] = peak + jnp.log(total)
            mixed_ref[rows, cols] = jnp.where(
                head_lanes(step, 0), outs[0], outs[1]
            ).astype(BF16)


class Load:
    def __init__(self, ref):
        self.ref = ref
        self.copies = []

    def __call__(self):
        for copy in self.copies:
            copy.wait()
        self.copies = []
        return self.ref


class Store:
    def __init__(self, ref, target, sem, running):
        self.ref = ref
        self.target = target
        self.sem = sem
        self.running = running
        self.sent = 0

    def send(self, rows=None):
        source = self.ref if rows is None else self.ref.at[rows]
        target = self.target if rows is None else self.target.at[rows]
        copy = pltpu.make_async_copy(source, target, self.sem.at[self.sent])
        copy.start()
        self.sent += 1
        self.running.append(copy)


    def send_if(self, flag, source):
        @pl.when(flag)
        def _():
            copy = pltpu.make_async_copy(source, self.target, self.sem.at[0])
            copy.start()
            copy.wait()


class Split:
    def __init__(self, ref, keep, send, sem, running, bit):
        self.ref = ref
        self.targets = ((send, 1 - bit), (keep, bit))
        self.sem = sem
        self.running = running

    def send(self):
        half = self.ref.shape[0] // 2
        for i, (target, which) in enumerate(self.targets):
            rows = pl.ds(pl.multiple_of(which * half, half), half)
            copy = pltpu.make_async_copy(self.ref.at[rows], target, self.sem.at[i])
            copy.start()
            self.running.append(copy)


class Rows:
    def __init__(self, array, first, count):
        self.array = array
        self.first = first
        self.count = count


class Into:
    def __init__(self, array, first):
        self.array = array
        self.first = first


class Pair:
    def __init__(self, own, other, first=0, count=None):
        self.own = own
        self.other = other
        self.first = first
        self.count = own.shape[0] if count is None else count


SEMS = 24


def call(kernel, name, scalars, ins, outs, scratch=(), flops=0, after=None):
    operands = []
    shapes = []
    for entry in ins:
        if isinstance(entry, Pair):
            operands += [entry.own, entry.other]
            shapes.append(((2 * entry.count,) + entry.own.shape[1:], entry.own.dtype))
        elif isinstance(entry, Into):
            operands.append(entry.array)
            rows = entry.first + entry.array.shape[0]
            shapes.append(((rows,) + entry.array.shape[1:], entry.array.dtype))
        elif isinstance(entry, Rows):
            operands.append(entry.array)
            shapes.append(((entry.count,) + entry.array.shape[1:], entry.array.dtype))
        else:
            operands.append(entry)
            shapes.append((entry.shape, entry.dtype))
    if after is not None:
        operands.append(after)
    results = []
    for shape, kind, *split in outs:
        if split:
            results += [jax.ShapeDtypeStruct((shape[0] // 2,) + shape[1:], kind)] * 2
        else:
            results.append(jax.ShapeDtypeStruct(shape, kind))
    n_scalar, n_in, n_out = len(scalars), len(operands), len(results)

    def body(*refs):
        smem_refs = refs[:n_scalar]
        sources = list(refs[n_scalar : n_scalar + n_in])
        targets = list(refs[n_scalar + n_in : n_scalar + n_in + n_out])
        rest = list(refs[n_scalar + n_in + n_out :])
        in_refs, rest = rest[: len(ins)], rest[len(ins) :]
        out_refs, rest = rest[: len(outs)], rest[len(outs) :]
        in_sem, out_sem = rest[:2]
        bit = smem_refs[0][1] & 1
        loads = []
        number = 0
        for entry, ref in zip(ins, in_refs):
            load = Load(ref)
            if isinstance(entry, Pair):
                half = ref.shape[0] // 2
                moves = []
                for which in (bit, 1 - bit):
                    rows = pl.ds(pl.multiple_of(which * half, half), half)
                    part = sources.pop(0).at[entry.first : entry.first + entry.count]
                    moves.append((part, ref.at[rows]))
            elif isinstance(entry, Into):
                moves = [(sources.pop(0), ref.at[entry.first : ref.shape[0]])]
            elif isinstance(entry, Rows):
                moves = [(sources.pop(0).at[entry.first : entry.first + entry.count], ref)]
            else:
                moves = [(sources.pop(0), ref)]
            for source, target in moves:
                copy = pltpu.make_async_copy(source, target, in_sem.at[number])
                copy.start()
                load.copies.append(copy)
                number += 1
            loads.append(load)
        running = []
        stores = []
        for i, (entry, ref) in enumerate(zip(outs, out_refs)):
            if len(entry) > 2:
                keep, send = targets.pop(0), targets.pop(0)
                stores.append(Split(ref, keep, send, out_sem.at[i], running, bit))
            else:
                stores.append(Store(ref, targets.pop(0), out_sem.at[i], running))
        kernel(*smem_refs, loads, stores, *rest[2:])
        for load in loads:
            load()
        for copy in running:
            copy.wait()

    hbm = pl.BlockSpec(memory_space=pltpu.HBM)
    return pl.pallas_call(
        body,
        name=name,
        out_shape=results,
        in_specs=[pl.BlockSpec(memory_space=pltpu.SMEM)] * n_scalar + [hbm] * n_in,
        out_specs=[hbm] * n_out,
        scratch_shapes=[pltpu.VMEM(shape, kind) for shape, kind in shapes]
        + [pltpu.VMEM(shape, kind) for shape, kind, *_ in outs]
        + [pltpu.SemaphoreType.DMA((max(n_in, 1),)), pltpu.SemaphoreType.DMA((len(outs), SEMS))]
        + [pltpu.VMEM(shape, kind) for shape, kind in scratch],
        compiler_params=pltpu.CompilerParams(vmem_limit_bytes=VMEM_LIMIT),
        cost_estimate=pl.CostEstimate(flops=int(flops), bytes_accessed=0, transcendentals=0),
    )(*scalars, *operands)


def forward_kernel(me_ref, loads, stores, layer_ref, bias_ref):
    index, table, tokens, seg, norm, wq, wk, wv, wo = loads
    normed, q, k, v, mixed, lse, first, last = stores
    length = tokens.ref.shape[0]
    half = length // 2
    index_row = index()[...]
    rows_of = table()[...]
    tok_ref = tokens()
    fill_layer(layer_ref, index_row, rows_of, tok_ref)
    fill_bias(bias_ref, seg()[...])
    norm_ref = norm()
    step = 128
    for at in range(0, length, step):
        rows = slice(at, at + step)
        hat, _ = norm_hat(layer_ref[rows, :])
        normed.ref[rows, :] = (hat * norm_ref[0:1, :] + norm_ref[1:2, :]).astype(BF16)
    normed.send()
    left = normed.ref[...]
    for weight, out in ((wq, q), (wk, k), (wv, v)):
        out.ref[...] = dot_nn(left, weight()[...]).astype(BF16)
        out.send()
    attend(q.ref, k.ref, v.ref, bias_ref, mixed.ref, lse.ref)
    mixed.send()
    lse.send()
    wo_ref = wo()
    for at, out in ((0, first), (half, last)):
        out.ref[...] = dot_nn(mixed.ref[at : at + half, :], wo_ref[...]).astype(BF16)
        out.send()


def grad_out_kernel(me_ref, loads, stores):
    seg, cotangent, return_weight = loads
    gout, gact = stores
    items = item_rows(seg()[...])
    valid = dot_tn(items, jnp.ones((SEG_ROWS, LANES), BF16))
    cot_ref = cotangent()
    for at in range(0, D, LANES):
        cols = slice(at, at + LANES)
        gout.ref[:, cols] = (cot_ref[:, cols].astype(F32) * valid).astype(BF16)
    gout.send()
    weight = return_weight()[...]
    half = gact.ref.shape[0] // 2
    for at in (0, half):
        rows = slice(at, at + half)
        gact.ref[rows, :] = dot_nt(gout.ref[rows, :], weight)
        gact.send(rows)


def feed_kernel(row0, me_ref, loads, stores, pre_ref):
    index, table, tokens, sums, norm, hidden_weight, gact = loads
    second, act, gpre, part = stores
    length = tokens.ref.shape[0]
    index_row = index()[:, row0 : row0 + length]
    rows_of = table()[...]
    tok_ref = tokens()
    fill_layer(pre_ref, index_row, rows_of, tok_ref, sums())
    norm_ref = norm()
    step = 64
    for at in range(0, length, step):
        rows = slice(at, at + step)
        hat, _ = norm_hat(pre_ref[rows, :])
        second.ref[rows, :] = (hat * norm_ref[2:3, :] + norm_ref[3:4, :]).astype(BF16)
    second.send()
    weight_ref = hidden_weight()
    pre_ref[...] = dot_nn(second.ref[...], weight_ref[...])
    gact_ref = gact()
    step = 32

    @pl.loop(0, length // step)
    def _(i):
        rows = pl.ds(pl.multiple_of(i * step, step), step)
        value, slope = gelu_parts(pre_ref[rows, :])
        act.ref[rows, :] = value.astype(BF16)
        gpre.ref[rows, :] = (gact_ref[rows, :] * slope).astype(BF16)

    act.send()
    gpre.send()
    part.ref[...] = dot_nt(gpre.ref[...], weight_ref[...]).astype(BF16)
    part.send()


def store_blocks(nat_ref, base, pairs, weight):
    width = pairs[0][1].shape[1]
    across = width // BLK
    wide = 256
    for at in range(0, width, wide):
        grad = None
        for left_ref, right_ref in pairs:
            part = dot_tn(left_ref[...], right_ref[:, at : at + wide])
            grad = part if grad is None else grad + part
        grad = (grad * weight).astype(BF16)
        for i in range(grad.shape[0] // BLK):
            for j in range(wide // BLK):
                nat_ref[base + i * across + at // BLK + j] = grad[
                    i * BLK : (i + 1) * BLK, j * BLK : (j + 1) * BLK
                ]


def relative(order, bits):
    out = 0
    for i, bit in enumerate(bits):
        if (order >> (len(bits) - 1 - i)) & 1:
            out |= bit
    return out


def gather_blocks(me_ref, source_ref, positions, first, count, bits, keep_ref, send_ref, block_at):
    owners = 2 ** len(bits)
    for order in range(owners):
        dest = me_ref[0] ^ relative(order, bits)
        out_ref = keep_ref if order < owners // 2 else send_ref
        at = (order % (owners // 2)) * count
        for j in range(count):
            out_ref[at + j] = block_at(source_ref[dest * positions + first + j])


def feed_grad_kernel(
    bits, early_slots, positions, late_count, me_ref, source_ref, scal_ref, loads, stores, nat_ref
):
    second_a, gpre_a, second_b, gpre_b, act_a, act_b, gout = loads
    rest = stores[0]
    weight = scal_ref[0]
    half = act_a.ref.shape[0]
    store_blocks(nat_ref, 0, ((second_a(), gpre_a()), (second_b(), gpre_b())), weight)
    gout_ref = gout()
    top, low = gout_ref.at[0:half, :], gout_ref.at[half : 2 * half, :]
    store_blocks(nat_ref, 64, ((act_a(), top), (act_b(), low)), weight)

    def block_at(block):
        return nat_ref[jnp.maximum(block - late_count, 0)]

    if early_slots:
        keep, send = stores[1:]
        gather_blocks(
            me_ref, source_ref, positions, 0, early_slots, bits, keep.ref, send.ref, block_at
        )
        send.send()
        keep.send()
    for i in range(rest.ref.shape[0]):
        rest.ref[i] = block_at(source_ref[2 ** len(bits) * positions + i])
    rest.send()


def backward_kernel(
    chunks,
    first,
    positions,
    late_count,
    me_ref,
    source_ref,
    scal_ref,
    loads,
    stores,
    gattn_ref,
    gmix_ref,
    gq_ref,
    gk_ref,
    gv_ref,
    hid_ref,
    bias_ref,
):
    index, table, tokens, attn_a, attn_b, norm, sum_a, gout, sum_b = loads[:9]
    wo, seg, q, k, v, lse, normed, mixed, rest = loads[9:18]
    wq, wk, wv, act_a, act_b, return_weight = loads[18:]
    late, parts = stores[:2]
    chunk_stores = stores[2:]
    half = attn_a.ref.shape[0]
    length = 2 * half
    weight = scal_ref[0]
    step = 64
    index_row = index()[...]
    rows_of = table()[...]
    tok_ref = tokens()
    for row0, attn, sums in ((0, attn_a, sum_a), (half, attn_b, sum_b)):
        part = slice(row0, row0 + half)
        fill_layer(hid_ref, index_row[:, part], rows_of, tok_ref.at[part, :], attn())
        norm_ref, gout_ref, sum_ref = norm(), gout(), sums()
        for at in range(0, half, step):
            here = slice(at, at + step)
            there = slice(row0 + at, row0 + at + step)
            hat, inv_std = norm_hat(hid_ref[here, :])
            grad = sum_ref[here, :].astype(F32)
            value = gout_ref[there, :].astype(F32) + norm_back(grad, hat, inv_std, norm_ref[2:3, :])
            gattn_ref[there, :] = value.astype(BF16)
    fill_bias(bias_ref, seg()[...])
    gmix_ref[...] = dot_nt(gattn_ref[...], wo()[...]).astype(BF16)
    scale = 1.0 / math.sqrt(HEAD)
    step = 512
    q_ref, k_ref, v_ref, lse_ref = q(), k(), v(), lse()
    for pair in range(q_ref.shape[1] // LANES):
        cols = slice(pair * LANES, (pair + 1) * LANES)
        keys = k_ref[:, cols]
        vals = v_ref[:, cols]
        grad_keys = [None, None]
        grad_vals = [None, None]
        for at in range(0, length, step):
            rows = slice(at, at + step)
            query = q_ref[rows, cols] * scale
            gmix = gmix_ref[rows, cols]
            grad_query = []
            for head in range(2):
                here = head_lanes(step, head)
                number = pair * 2 + head
                scores = dot_nt(jnp.where(here, query, 0.0).astype(BF16), keys) + bias_ref[rows, :]
                probs = jnp.exp(scores - lse_ref[rows, number : number + 1])
                grad_probs = dot_nt(jnp.where(here, gmix, 0.0).astype(BF16), vals)
                grad_scores = (
                    probs * (grad_probs - jnp.sum(probs * grad_probs, axis=-1, keepdims=True))
                ).astype(BF16)
                value_part = dot_tn(probs.astype(BF16), gmix)
                key_part = dot_tn(grad_scores, query)
                grad_vals[head] = value_part if at == 0 else grad_vals[head] + value_part
                grad_keys[head] = key_part if at == 0 else grad_keys[head] + key_part
                grad_query.append(dot_nn(grad_scores, keys))
            first_head = head_lanes(step, 0)
            gq_ref[rows, cols] = (
                jnp.where(first_head, grad_query[0], grad_query[1]) * scale
            ).astype(BF16)
        first_head = head_lanes(length, 0)
        gk_ref[:, cols] = jnp.where(first_head, grad_keys[0], grad_keys[1]).astype(BF16)
        gv_ref[:, cols] = jnp.where(first_head, grad_vals[0], grad_vals[1]).astype(BF16)
    pairs = ((gq_ref, wq()), (gk_ref, wk()), (gv_ref, wv()))
    return_ref = return_weight()
    for i, act in enumerate((act_a, act_b)):
        rows = slice(i * half, (i + 1) * half)
        total = sum(dot_nt(grad[rows, :], weights[...]) for grad, weights in pairs)
        parts.ref[2 * i * half : (2 * i + 1) * half, :] = total.astype(BF16)
        parts.ref[(2 * i + 1) * half : (2 * i + 2) * half, :] = dot_nn(
            act()[...], return_ref[...]
        ).astype(BF16)
    parts.send()
    normed_ref = normed()
    pool_ref = rest.ref
    store_blocks(pool_ref, 0, ((normed_ref, gq_ref),), weight)
    store_blocks(pool_ref, 16, ((normed_ref, gk_ref),), weight)
    store_blocks(pool_ref, 32, ((normed_ref, gv_ref),), weight)
    store_blocks(pool_ref, 48, ((mixed(), gattn_ref),), weight)
    rest()
    for number, (count, bits) in enumerate(chunks):
        keep, send = chunk_stores[2 * number : 2 * number + 2]
        gather_blocks(
            me_ref,
            source_ref,
            positions,
            first,
            count,
            bits,
            keep.ref,
            send.ref,
            lambda place: pool_ref[place],
        )
        send.send()
        keep.send()
        first += count
    late.send_if(scal_ref[3] > 0.5, pool_ref.at[0:late_count])


def overflow_kernel(first, count, bits, positions, me_ref, source_ref, loads, stores):
    (late,) = loads
    keep, send = stores
    late_ref = late()
    last = late_ref.shape[0] - 1
    gather_blocks(
        me_ref,
        source_ref,
        positions,
        first,
        count,
        bits,
        keep.ref,
        send.ref,
        lambda place: late_ref[jnp.minimum(place, last)],
    )
    keep.send()
    send.send()


def add_rows(acc_ref, at, values):
    acc_ref[at : at + 8, :] += jnp.sum(values.reshape(values.shape[0] // 8, 8, D), axis=0)


def finish_kernel(me_ref, scal_ref, loads, stores, layer_ref, acc_ref):
    index, table, tokens, attn_a, attn_b, norm, outputs, second_a, second_b, gout = loads
    out, gin, sums = stores
    half = attn_a.ref.shape[0]
    weight = scal_ref[0]
    step = 32
    acc_ref[...] = jnp.zeros_like(acc_ref)
    index_row = index()[...]
    rows_of = table()[...]
    tok_ref = tokens()
    for row0, attn, second in ((0, attn_a, second_a), (half, attn_b, second_b)):
        part = slice(row0, row0 + half)
        fill_layer(layer_ref, index_row[:, part], rows_of, tok_ref.at[part, :])
        attn_ref, norm_ref, second_ref, gout_ref, both_ref = (
            attn(),
            norm(),
            second(),
            gout(),
            outputs(),
        )
        for at in range(0, half, step):
            here = slice(at, at + step)
            rows = slice(row0 + at, row0 + at + step)
            first_at = 2 * row0 + at
            layer = layer_ref[here, :]
            hat, inv_std = norm_hat(layer)
            hid = layer + attn_ref[here, :].astype(F32)
            mlp = both_ref[first_at + half : first_at + half + step, :].astype(F32)
            out.ref[rows, :] = hid + mlp
            hat2, inv_std2 = norm_hat(hid)
            grad2 = second_ref[here, :].astype(F32)
            ghid = gout_ref[rows, :].astype(F32) + norm_back(
                grad2, hat2, inv_std2, norm_ref[2:3, :]
            )
            add_rows(acc_ref, 16, grad2 * hat2)
            add_rows(acc_ref, 24, grad2)
            grad = both_ref[first_at : first_at + step, :].astype(F32)
            gin.ref[rows, :] = ghid + norm_back(grad, hat, inv_std, norm_ref[0:1, :])
            add_rows(acc_ref, 0, grad * hat)
            add_rows(acc_ref, 8, grad)
        out.send(part)
        gin.send(part)
    for i in range(4):
        sums.ref[i : i + 1, :] = (
            jnp.sum(acc_ref[8 * i : 8 * i + 8, :], axis=0, keepdims=True) * weight
        )
    sums.ref[4:5, :] = jnp.full((1, D), weight, F32)
    sums.ref[5:8, :] = jnp.zeros((3, D), F32)
    sums.send()


def columns(rows):
    count = rows.shape[0]
    if count % 8:
        return jnp.stack(
            [jnp.transpose(jnp.broadcast_to(rows[i : i + 1], (BLK, BLK)))[:, 0:1] for i in range(count)]
        )
    turned = jnp.transpose(rows)
    return jnp.stack([turned[:, i : i + 1] for i in range(count)])


def reflect(blocks, left, right, coef_left, coef_right):
    along = jnp.sum(left * blocks, axis=1, keepdims=True) * coef_left
    blocks = blocks - left * along
    across = jnp.sum(blocks * right, axis=2, keepdims=True) * coef_right
    return blocks - across * right


def reflectors(left_ref, right_ref):
    left, right = left_ref[...], right_ref[...]
    coef_left = (2.0 / jnp.sum(left * left, axis=1, keepdims=True))[:, :, None]
    coef_right = (2.0 / jnp.sum(right * right, axis=1, keepdims=True))[:, :, None]
    return (columns(left), right[:, None, :], coef_left, coef_right)


def rotate_kernel(counts, group, me_ref, place_ref, loads, stores, found_ref):
    left, right = loads[:2]
    grads, turned, total = stores
    parts = reflectors(left(), right())
    at = 0
    for number, count in enumerate(counts):
        keep, got = loads[2 + 2 * number : 4 + 2 * number]
        found_ref[at : at + count] = keep()[...].astype(F32) + got()[...].astype(F32)
        at += count
    slots = grads.ref.shape[0]
    for slot in range(slots):
        grads.ref[slot] = found_ref[place_ref[me_ref[0] * slots + slot]]
    grads.send()
    square = jnp.zeros((8, BLK), F32)
    for at in range(0, slots, group):
        rows = slice(at, at + group)
        grad = grads.ref[rows]
        square = square + jnp.sum((grad * grad).reshape(group * BLK // 8, 8, BLK), axis=0)
        turned.ref[rows] = reflect(grad, *(part[rows] for part in parts))
        turned.send(rows)
    total.ref[...] = jnp.full((8, BLK), jnp.sum(square), F32)
    total.send()


def inverse(value):
    guess = pl.reciprocal(value, approx=True)
    return guess * (2.0 - value * guess)


def update_kernel(group, me_ref, scal_ref, loads, stores):
    sums, norm, norm_first, norm_second, left, right = loads[:6]
    grads, turned_grads, old_first, old_second, old_master = loads[6:]
    out_grad, out_first, out_second, out_master, out_copy = stores[:5]
    norm_pair, norm_square, norm_value, clip_out = stores[5:]
    inv_one = 1.0 / scal_ref[1]
    inv_two = 1.0 / scal_ref[2]
    sums_ref = sums()
    share = 1.0 / sums_ref[4:5, 0:BLK]
    norm_grad = sums_ref[0:4, :] * share[:, 0:1]
    total = sums_ref[5:6, 0:BLK] * (share * share) + jnp.sum(norm_grad * norm_grad)
    clip_norm = jnp.sqrt(total)
    clip = jnp.minimum(1.0, clip_max / clip_norm)
    factor = (share * clip)[:, None, :]
    parts = reflectors(left(), right())
    slots = left.ref.shape[0]
    entries = 1.0 / (BLK * BLK)
    for at in range(0, slots, group):
        rows = slice(at, at + group)
        out_grad.ref[rows] = grads()[rows] * factor
        rotated = turned_grads()[rows] * factor
        first = beta_one * old_first()[rows] + (1.0 - beta_one) * rotated
        second = beta_two * old_second()[rows] + (1.0 - beta_two) * rotated * rotated
        out_first.ref[rows] = first
        out_second.ref[rows] = second
        spread = second * inv_two
        normal = (first * inv_one) * inverse(spread * lax.rsqrt(spread) + adam_eps)
        turned = reflect(normal, *(part[rows] for part in parts))
        master = old_master()[rows]
        size = jnp.sum(jnp.sum(master * master, axis=1, keepdims=True), axis=2, keepdims=True)
        move = jnp.sum(jnp.sum(turned * turned, axis=1, keepdims=True), axis=2, keepdims=True)
        trust = jnp.sqrt(size * entries + trust_eps) / jnp.sqrt(move * entries + trust_eps)
        fresh = master - (step_rate * trust) * turned
        out_master.ref[rows] = fresh
        out_copy.ref[rows] = fresh.astype(BF16)
        for out in (out_grad, out_first, out_second, out_master, out_copy):
            out.send(rows)
    clip_out.ref[...] = jnp.broadcast_to(clip_norm, clip_out.ref.shape)
    clip_out.send()
    clipped = norm_grad * clip[:, 0:1]
    first = beta_one * norm_first()[...] + (1.0 - beta_one) * clipped
    second = beta_two * norm_second()[...] + (1.0 - beta_two) * clipped * clipped
    norm_pair.ref[0] = clipped
    norm_pair.ref[1] = first
    norm_pair.send()
    norm_square.ref[...] = second
    norm_square.send()
    norm_value.ref[...] = norm()[...] - step_rate * (first * inv_one) / (
        jnp.sqrt(second * inv_two) + adam_eps
    )
    norm_value.send()


def swap(value, axis, bit):
    count = lax.axis_size(axis)
    return lax.ppermute(value, axis, [(i, i ^ bit) for i in range(count)])


def plus(left, right):
    return (left.astype(F32) + right.astype(F32)).astype(BF16)


def after(value, *others):
    return lax.optimization_barrier((value, *others))[0]


def mp_far(total, wait=None):
    bit = 2
    while bit < lax.axis_size("mp"):
        got = swap(total, "mp", bit)
        total = plus(total, got if wait is None else after(got, wait))
        bit *= 2
    return total


def mp_sum(keep, send):
    total = mp_far(plus(keep, swap(send, "mp", 1)))
    return (total, swap(total, "mp", 1))


def early_count(slots):
    return slots // 3 if slots >= 24 else 0


def split_counts(slots, bits):
    if slots >= 8:
        last = slots // 4
        head = (slots - last + 2) // 2
        crossed = (bits[1], bits[0]) + bits[2:]
        return ((head, bits), (slots - last - head, bits), (last, crossed))
    return ((1, bits),) * slots if slots <= 3 else ((slots - slots // 2, bits), (slots // 2, bits))


def exclusive_sum(values):
    size = values.shape[-1]
    before = jnp.asarray(np.tril(np.ones((size, size), np.int32), -1))
    return jnp.sum(values[..., None, :] * before, axis=-1)


def rest_count(blocks, late_count, n_dp, slots, early_slots):
    total = blocks - late_count
    full, over = divmod(total, slots)
    return total - full * early_slots - min(over, early_slots)


def slot_tables(owner_list, n_dp, slots, early_slots, late_count):
    blocks = owner_list.shape[0]
    owned = owner_list.reshape(n_dp, slots)
    early = (owned >= late_count).astype(jnp.int32)
    if early_slots:
        goes = early * (exclusive_sum(early) < early_slots).astype(jnp.int32)
        place = jnp.where(goes == 1, exclusive_sum(early), early_slots + exclusive_sum(1 - goes))
        positions = slots + early_slots
        hit = place[:, None, :] == jnp.arange(positions, dtype=jnp.int32)[None, :, None]
        source = jnp.sum(jnp.where(hit, owned[:, None, :], 0), axis=2)
        short = jnp.any(jnp.sum(early, axis=1) < early_slots)
    else:
        place = jnp.broadcast_to(jnp.arange(slots, dtype=jnp.int32), (n_dp, slots))
        source, short = owned, jnp.zeros((), bool)
    later = source[:, early_slots:].reshape(-1)
    is_rest = (later >= late_count).astype(jnp.int32)
    order = exclusive_sum(is_rest)
    count = rest_count(blocks, late_count, n_dp, slots, early_slots)
    hit = (order[None, :] == jnp.arange(count, dtype=jnp.int32)[:, None]) & (is_rest[None, :] == 1)
    rest = jnp.sum(jnp.where(hit, later[None, :], 0), axis=1)
    later = jnp.where(is_rest == 1, late_count + order, later)
    source = jnp.concatenate([source[:, :early_slots], later.reshape(n_dp, -1)], axis=1)
    return (jnp.concatenate([source.reshape(-1), rest]), place.reshape(-1), short)


def shards(
    tokens,
    cotangent,
    segment_ids,
    table_index,
    group_count,
    owner_list,
    step_count,
    query_weight,
    key_weight,
    value_weight,
    output_weight,
    hidden_weight,
    return_weight,
    norm_params,
    norm_first,
    norm_second,
    master_blocks,
    first_moment,
    second_moment,
    left_vector,
    right_vector,
):
    length = tokens.shape[0]
    half = length // 2
    width = query_weight.shape[1]
    heads = width // HEAD
    units = hidden_weight.shape[1]
    slots = master_blocks.shape[0]
    blocks = owner_list.shape[0]
    late_count = blocks // 3
    n_dp = lax.axis_size("dp")
    natural = tuple(1 << i for i in range(n_dp.bit_length() - 1))
    early_slots = early_count(slots)
    positions = slots + early_slots
    me = jnp.stack([lax.axis_index("dp"), lax.axis_index("mp")]).astype(jnp.int32)
    step_value = step_count[0].astype(F32)
    source, place, short = slot_tables(owner_list, n_dp, slots, early_slots, late_count)
    scal = jnp.stack(
        [
            group_count[0].astype(F32),
            1.0 - jnp.power(beta_one, step_value),
            1.0 - jnp.power(beta_two, step_value),
            short.astype(F32),
        ]
    )
    seg_row = segment_ids.reshape(1, length)
    index_row = table_index.reshape(1, length)
    table = jnp.asarray(position_rows())
    rows_d = (length, D)
    half_d = (half, D)
    unit = 2 * length * D * D
    wide = ((length, width), BF16)

    normed, q, k, v, mixed, lse, keep_a, send_a, keep_b, send_b = call(
        forward_kernel,
        "attention_forward",
        (me,),
        (
            index_row,
            table,
            tokens,
            seg_row,
            norm_params,
            query_weight,
            key_weight,
            value_weight,
            output_weight,
        ),
        [
            (rows_d, BF16),
            wide,
            wide,
            wide,
            wide,
            ((length, heads), F32),
            (half_d, BF16, True),
            (half_d, BF16, True),
        ],
        [(rows_d, F32), ((length, length), F32)],
        flops=5 * unit,
    )
    near_a = plus(keep_a, swap(send_a, "mp", 1))
    near_b = plus(keep_b, swap(send_b, "mp", 1))
    token = near_b
    grad_out, grad_act = call(
        grad_out_kernel,
        "grad_of_act",
        (me,),
        (seg_row, cotangent, return_weight),
        [(rows_d, BF16), ((length, units), F32)],
        flops=2 * unit,
        after=token,
    )

    far_a = mp_far(near_a, grad_act)
    attn_a = Pair(far_a, swap(far_a, "mp", 1))
    far_b = mp_far(near_b)
    attn_b = Pair(far_b, swap(far_b, "mp", 1))

    def feed(row0, name, sums, token):
        return call(
            functools.partial(feed_kernel, row0),
            name,
            (me,),
            (
                index_row,
                table,
                Rows(tokens, row0, half),
                sums,
                norm_params,
                hidden_weight,
                Rows(grad_act, row0, half),
            ),
            [
                (half_d, BF16),
                ((half, units), BF16),
                ((half, units), BF16),
                (half_d, BF16, True),
            ],
            [((half, units), F32)],
            flops=4 * unit,
            after=token,
        )

    second_a, act_a, gpre_a, keep_a, send_a = feed(0, "feed_forward_a", attn_a, None)
    second_b, act_b, gpre_b, keep_b, send_b = feed(half, "feed_forward_b", attn_b, keep_a)
    near_a = plus(keep_a, swap(send_a, "mp", 1))
    near_b = plus(keep_b, swap(send_b, "mp", 1))
    far_a = mp_far(near_a, near_b)
    chunk_e = [((n_dp // 2 * early_slots, BLK, BLK), BF16)] * 2 if early_slots else []
    count = rest_count(blocks, late_count, n_dp, slots, early_slots)
    rest, *chunk_e = call(
        functools.partial(feed_grad_kernel, natural, early_slots, positions, late_count),
        "feed_weight_grads",
        (me, source, scal),
        (second_a, gpre_a, second_b, gpre_b, act_a, act_b, grad_out),
        [((count, BLK, BLK), BF16)] + chunk_e,
        [((blocks - late_count, BLK, BLK), BF16)],
        flops=4 * unit,
        after=near_b,
    )
    far_b = mp_far(near_b, rest)
    sum_a = Pair(far_a, swap(far_a, "mp", 1))
    sum_b = Pair(far_b, swap(far_b, "mp", 1))
    got_e = swap(chunk_e[1], "dp", 1) if early_slots else None
    chunks = split_counts(slots - early_slots, natural)
    chunk_shapes = []
    for count, _ in chunks:
        chunk_shapes += [((n_dp // 2 * count, BLK, BLK), BF16)] * 2
    outs = call(
        functools.partial(backward_kernel, chunks, early_slots, positions, late_count),
        "attention_backward",
        (me, source, scal),
        (
            index_row,
            table,
            tokens,
            attn_a,
            attn_b,
            norm_params,
            sum_a,
            grad_out,
            sum_b,
            output_weight,
            seg_row,
            q,
            k,
            v,
            lse,
            normed,
            mixed,
            Into(rest, late_count),
            query_weight,
            key_weight,
            value_weight,
            act_a,
            act_b,
            return_weight,
        ),
        [((late_count, BLK, BLK), BF16), ((2 * length, D), BF16, True)] + chunk_shapes,
        [(rows_d, BF16)]
        + [((length, width), BF16)] * 4
        + [(half_d, F32), ((length, length), F32)],
        flops=10 * unit,
    )
    late, keep, send = outs[:3]
    queue = [(outs[3 + 2 * i], outs[4 + 2 * i]) for i in range(len(chunks))]
    counts = [count for count, _ in chunks]
    orders = [bits for _, bits in chunks]

    stages = len(natural)
    state = [(first, swap(second, "dp", bits[0])) for (first, second), bits in zip(queue, orders)]
    if early_slots:
        state.insert(0, (chunk_e[0], after(got_e, keep)))
        counts.insert(0, early_slots)
        orders.insert(0, natural)
    level = [0] * len(state)
    last = []

    def in_turn(got):
        got = after(got, *last)
        last[:] = [got]
        return got

    def halve(number):
        keep, got = state[number]
        got = in_turn(got)
        if level[number] < stages - 1:
            n = keep.shape[0] // 2
            keep, send = plus(keep[:n], got[:n]), plus(keep[n:], got[n:])
            got = swap(send, "dp", orders[number][level[number] + 1])
            last.append(send)
        level[number] += 1
        state[number] = (keep, got)

    def mp_first(keep, send):
        return plus(keep, in_turn(swap(send, "mp", 1)))

    def mp_rest(near):
        bit = 2
        while bit < lax.axis_size("mp"):
            near = plus(near, in_turn(swap(near, "mp", bit)))
            bit *= 2
        return Pair(near, swap(near, "mp", 1))

    if early_slots:
        halve(0)
    def finish(both):
        outputs = call(
            finish_kernel,
            "layer_outputs",
            (me, scal),
            (
                index_row,
                table,
                tokens,
                attn_a,
                attn_b,
                norm_params,
                both,
                sum_a,
                sum_b,
                grad_out,
            ),
            [(rows_d, F32), (rows_d, F32), ((8, D), F32)],
            [(half_d, F32), ((32, D), F32)],
            flops=2 * unit,
        )
        last.append(outputs[2])
        return outputs

    plan = ["near", "far", "finish"]
    if early_slots and stages == 3:
        plan = ["near", (3, 0), (1, 0), (0, 1), (2, 0), "far", (1, 1), (0, 2), (3, 1), (2, 1), (1, 2)]
        plan += ["finish"]
    plan += [(i, d - i) for d in range(len(state) + stages) for i in range(len(state))]
    for entry in plan:
        if entry == "near":
            near = plus(keep, in_turn(swap(send, "mp", 1)))
        elif entry == "far":
            bit = 2
            while bit < lax.axis_size("mp"):
                near = plus(near, in_turn(swap(near, "mp", bit)))
                bit *= 2
            both = Pair(near, swap(near, "mp", 1))
        elif entry == "finish":
            out, input_grad, sums = finish(both)
        elif level[entry[0]] == entry[1] < stages:
            halve(entry[0])
    pending = [array for pair in state for array in pair]

    if early_slots:
        shape = (n_dp // 2 * early_slots, BLK, BLK)

        def exchange(late):
            keep, send = call(
                functools.partial(overflow_kernel, slots, early_slots, natural, positions),
                "overflow",
                (me, source),
                (late,),
                [(shape, BF16), (shape, BF16)],
            )
            bit = 1
            while True:
                got = swap(send, "dp", bit)
                bit *= 2
                if bit >= n_dp:
                    return (keep, got)
                n = keep.shape[0] // 2
                keep, send = plus(keep[:n], got[:n]), plus(keep[n:], got[n:])

        def nothing(late):
            zero = jnp.zeros((early_slots, BLK, BLK), BF16)
            return (zero, zero)

        pending += list(lax.cond(short, exchange, nothing, late))
        counts.append(early_slots)

    left = left_vector.reshape(slots, BLK)
    right = right_vector.reshape(slots, BLK)
    block_f32 = ((slots, BLK, BLK), F32)
    group = 4 if slots % 4 == 0 else 1
    grads, rotated, square = call(
        functools.partial(rotate_kernel, counts, group),
        "rotate",
        (me, place),
        (left, right, *pending),
        [block_f32, block_f32, ((8, BLK), F32)],
        [((sum(counts), BLK, BLK), F32)],
        flops=unit,
    )
    bit = 1
    while bit < lax.axis_size("mp"):
        square = square + swap(square, "mp", bit)
        bit *= 2
    sums = sums + jnp.pad(square[0:1], ((5, 2), (0, D - BLK)))
    bit = 1
    while bit < n_dp:
        sums = sums + swap(sums, "dp", bit)
        bit *= 2
    new = call(
        functools.partial(update_kernel, group),
        "update",
        (me, scal),
        (
            sums,
            norm_params,
            norm_first,
            norm_second,
            left,
            right,
            grads,
            rotated,
            first_moment.reshape(slots, BLK, BLK),
            second_moment.reshape(slots, BLK, BLK),
            master_blocks.reshape(slots, BLK, BLK),
        ),
        [block_f32] * 4
        + [
            ((slots, BLK, BLK), BF16),
            ((2, 4, D), F32),
            ((4, D), F32),
            ((4, D), F32),
            ((8, BLK), F32),
        ],
        flops=unit,
    )
    shard_shape = (slots, 1, BLK, BLK)
    return (
        out,
        input_grad,
        new[0].reshape(shard_shape),
        new[1].reshape(shard_shape),
        new[2].reshape(shard_shape),
        new[3].reshape(shard_shape),
        new[4].reshape(shard_shape),
        new[5],
        new[6],
        new[7],
        new[8][0, 0],
    )


def solution(mesh):
    placed = (
        P("dp", None),
        P("dp", None),
        P("dp"),
        P("dp"),
        P("dp"),
        P(),
        P(),
        P(None, "mp"),
        P(None, "mp"),
        P(None, "mp"),
        P("mp", None),
        P(None, "mp"),
        P("mp", None),
        P(),
        P(),
        P(),
        P("dp", "mp", None, None),
        P("dp", "mp", None, None),
        P("dp", "mp", None, None),
        P("dp", "mp", None),
        P("dp", "mp", None),
    )
    return jax.shard_map(
        shards,
        mesh=mesh,
        in_specs=placed,
        out_specs=(
            P("dp", None),
            P("dp", None),
            P("dp", "mp", None, None),
            P("dp", "mp", None, None),
            P("dp", "mp", None, None),
            P("dp", "mp", None, None),
            P("dp", "mp", None, None),
            P(),
            P(),
            P(),
            P(),
        ),
        check_vma=False,
    )
```

```python
import functools
import math

import jax
import jax.numpy as jnp
import numpy as np
from jax import lax
from jax.experimental import pallas as pl
from jax.experimental.pallas import tpu as pltpu
from jax.sharding import PartitionSpec as P

D = 1024
HEAD = 64
BLK = 128
LANES = 128
POS_ROWS = 64
SEG_ROWS = 32

clip_max = 1.0
beta_one = 0.5
beta_two = 0.5
adam_eps = 1e-08
step_rate = 0.25
norm_eps = 1e-06
trust_eps = 1e-06

F32 = jnp.float32
BF16 = jnp.bfloat16
MIB = 1024 * 1024
VMEM_LIMIT = 60 * MIB

ERF_P = 0.425
ERF_COEF = (
    0.11983931305209315,
    0.12092032287702306,
    0.10035292560006456,
    0.12754356284084392,
    -0.051626023300101125,
    0.20380940869554587,
    -0.1565787944569494,
    0.035739213095996265,
)


def position_rows():
    coords = np.concatenate(
        [1.75 * np.arange(8), 1.0 * np.arange(14), 0.5 * np.arange(28), np.zeros(POS_ROWS - 50)]
    )
    quarter = D // 4
    freqs = np.power(np.float32(10000.0), -np.arange(quarter, dtype=np.float32) / np.float32(quarter))
    args = (coords.astype(np.float32)[:, None] * freqs.astype(np.float32)[None, :]).astype(np.float64)
    table = np.concatenate([np.sin(args), np.cos(args)], axis=1).astype(np.float32)
    parts = []
    rest = table
    for _ in range(3):
        part = rest.astype(jnp.bfloat16)
        parts.append(part)
        rest = rest - part.astype(np.float32)
    return np.concatenate(parts, axis=0)


def dot_nn(left, right):
    return lax.dot_general(left, right, (((1,), (0,)), ((), ())), preferred_element_type=F32)


def dot_nt(left, right):
    return lax.dot_general(left, right, (((1,), (1,)), ((), ())), preferred_element_type=F32)


def dot_tn(left, right):
    return lax.dot_general(left, right, (((0,), (0,)), ((), ())), preferred_element_type=F32)


def norm_hat(values):
    center = values - jnp.mean(values, axis=-1, keepdims=True)
    inv_std = lax.rsqrt(jnp.mean(center * center, axis=-1, keepdims=True) + norm_eps)
    return (center * inv_std, inv_std)


def norm_back(grad_out, normal, inv_std, gain):
    scaled = grad_out * gain
    return inv_std * (
        scaled
        - jnp.mean(scaled, axis=-1, keepdims=True)
        - normal * jnp.mean(scaled * normal, axis=-1, keepdims=True)
    )


def gelu_parts(values):
    bell = jnp.exp(-0.5 * values * values)
    t = 1.0 / (1.0 + (ERF_P / math.sqrt(2.0)) * jnp.abs(values))
    poly = ERF_COEF[-1]
    for coef in ERF_COEF[-2::-1]:
        poly = poly * t + coef
    tail = poly * t * bell
    dist = jnp.where(values >= 0.0, 1.0 - tail, tail)
    return (values * dist, dist + values * ((1.0 / math.sqrt(2.0 * math.pi)) * bell))


def item_rows(seg_row):
    rows = lax.broadcasted_iota(jnp.int32, (SEG_ROWS, seg_row.shape[1]), 0)
    return jnp.where(rows == seg_row, 1.0, 0.0).astype(BF16)


def head_lanes(rows, head):
    lanes = lax.broadcasted_iota(jnp.int32, (rows, LANES), 1)
    return (lanes // HEAD) == head


def position_hots(index):
    length = index.shape[1]
    big = index >= 260
    mid = index >= 64
    offset = jnp.where(big, 260, jnp.where(mid, 64, 0))
    base = jnp.where(big, 22, jnp.where(mid, 8, 0))
    side = jnp.where(big, 28, jnp.where(mid, 14, 8))
    inv_side = jnp.where(big, 1.0 / 28.0, jnp.where(mid, 1.0 / 14.0, 1.0 / 8.0)).astype(F32)
    local = index - offset
    row = jnp.floor((local.astype(F32) + 0.5) * inv_side).astype(jnp.int32)
    col = local - row * side
    rows = lax.broadcasted_iota(jnp.int32, (3 * POS_ROWS, length), 0) & (POS_ROWS - 1)
    row_hot = jnp.where(rows == base + row, 1.0, 0.0).astype(BF16)
    col_hot = jnp.where(rows == base + col, 1.0, 0.0).astype(BF16)
    return (row_hot, col_hot)


def fill_layer(out_ref, index_row, table, tok_ref, sum_ref=None):
    half = D // 2
    for hot, cols in zip(position_hots(index_row), (slice(0, half), slice(half, D))):
        value = dot_tn(hot, table) + tok_ref[:, cols].astype(F32)
        if sum_ref is not None:
            value = value + sum_ref[:, cols].astype(F32)
        out_ref[:, cols] = value


def fill_bias(bias_ref, seg_row):
    length = seg_row.shape[1]
    items = item_rows(seg_row)
    same = dot_tn(items, items)
    diag = lax.broadcasted_iota(jnp.int32, (length, length), 0) == lax.broadcasted_iota(
        jnp.int32, (length, length), 1
    )
    bias_ref[...] = jnp.where((same > 0.5) | diag, 0.0, -1e30)


def lane_of(values, number):
    lanes = lax.broadcasted_iota(jnp.int32, values.shape, 1)
    return jnp.sum(jnp.where(lanes == number, values, 0.0), axis=1, keepdims=True)


def head_columns(number):
    return pl.ds(pl.multiple_of((number // 2) * LANES, LANES), LANES)


def attend(q_ref, k_ref, v_ref, bias_ref, mixed_ref, lse_ref):
    count = q_ref.shape[0]
    scale = 1.0 / math.sqrt(HEAD)
    step = 512
    for pair in range(q_ref.shape[1] // LANES):
        cols = slice(pair * LANES, (pair + 1) * LANES)
        keys = k_ref[:, cols]
        vals = v_ref[:, cols]
        for at in range(0, count, step):
            rows = slice(at, at + step)
            query = q_ref[rows, cols] * scale
            outs = []
            for head in range(2):
                here = head_lanes(step, head)
                scores = dot_nt(jnp.where(here, query, 0.0).astype(BF16), keys) + bias_ref[rows, :]
                peak = jnp.max(scores, axis=-1, keepdims=True)
                expon = jnp.exp(scores - peak)
                total = jnp.sum(expon, axis=-1, keepdims=True)
                outs.append(dot_nn(expon.astype(BF16), vals) * (1.0 / total))
                number = pair * 2 + head
                lse_ref[rows, number : number + 1] = peak + jnp.log(total)
            mixed_ref[rows, cols] = jnp.where(
                head_lanes(step, 0), outs[0], outs[1]
            ).astype(BF16)


class Load:
    def __init__(self, ref):
        self.ref = ref
        self.copies = []

    def __call__(self):
        for copy in self.copies:
            copy.wait()
        self.copies = []
        return self.ref


class Store:
    def __init__(self, ref, target, sem, running):
        self.ref = ref
        self.target = target
        self.sem = sem
        self.running = running
        self.sent = 0

    def send(self, rows=None):
        source = self.ref if rows is None else self.ref.at[rows]
        target = self.target if rows is None else self.target.at[rows]
        copy = pltpu.make_async_copy(source, target, self.sem.at[self.sent])
        copy.start()
        self.sent += 1
        self.running.append(copy)


    def send_if(self, flag, source):
        @pl.when(flag)
        def _():
            copy = pltpu.make_async_copy(source, self.target, self.sem.at[0])
            copy.start()
            copy.wait()


class Split:
    def __init__(self, ref, keep, send, sem, running, bit):
        self.ref = ref
        self.targets = ((send, 1 - bit), (keep, bit))
        self.sem = sem
        self.running = running

    def send(self):
        half = self.ref.shape[0] // 2
        for i, (target, which) in enumerate(self.targets):
            rows = pl.ds(pl.multiple_of(which * half, half), half)
            copy = pltpu.make_async_copy(self.ref.at[rows], target, self.sem.at[i])
            copy.start()
            self.running.append(copy)


class Rows:
    def __init__(self, array, first, count):
        self.array = array
        self.first = first
        self.count = count


class Into:
    def __init__(self, array, first):
        self.array = array
        self.first = first


class Pair:
    def __init__(self, own, other, first=0, count=None):
        self.own = own
        self.other = other
        self.first = first
        self.count = own.shape[0] if count is None else count


class Stack:
    def __init__(self, *parts):
        self.parts = parts


SEMS = 24


def row_moves(entry, sources, ref, first, bit):
    if isinstance(entry, Stack):
        moves = []
        for part in entry.parts:
            more, first = row_moves(part, sources, ref, first, bit)
            moves += more
        return (moves, first)
    if isinstance(entry, Pair):
        moves = []
        for which in (bit, 1 - bit):
            rows = pl.ds(pl.multiple_of(first + which * entry.count, entry.count), entry.count)
            part = sources.pop(0).at[entry.first : entry.first + entry.count]
            moves.append((part, ref.at[rows]))
        return (moves, first + 2 * entry.count)
    count = entry.count if isinstance(entry, Rows) else entry.shape[0]
    source = sources.pop(0)
    if isinstance(entry, Rows):
        source = source.at[entry.first : entry.first + count]
    whole = count == ref.shape[0]
    return ([(source, ref if whole else ref.at[first : first + count])], first + count)


def flat(entry):
    if isinstance(entry, Stack):
        parts = [flat(part) for part in entry.parts]
        return (sum((p[0] for p in parts), []), sum(p[1] for p in parts), parts[0][2])
    if isinstance(entry, Pair):
        return ([entry.own, entry.other], 2 * entry.count, entry.own)
    if isinstance(entry, Rows):
        return ([entry.array], entry.count, entry.array)
    if isinstance(entry, Into):
        return ([entry.array], entry.first + entry.array.shape[0], entry.array)
    return ([entry], entry.shape[0], entry)


def call(kernel, name, scalars, ins, outs, scratch=(), flops=0, after=None):
    operands = []
    shapes = []
    for entry in ins:
        arrays, rows, like = flat(entry)
        operands += arrays
        shapes.append(((rows,) + like.shape[1:], like.dtype))
    if after is not None:
        operands.append(after)
    results = []
    for shape, kind, *split in outs:
        if split:
            results += [jax.ShapeDtypeStruct((shape[0] // 2,) + shape[1:], kind)] * 2
        else:
            results.append(jax.ShapeDtypeStruct(shape, kind))
    n_scalar, n_in, n_out = len(scalars), len(operands), len(results)

    def body(*refs):
        smem_refs = refs[:n_scalar]
        sources = list(refs[n_scalar : n_scalar + n_in])
        targets = list(refs[n_scalar + n_in : n_scalar + n_in + n_out])
        rest = list(refs[n_scalar + n_in + n_out :])
        in_refs, rest = rest[: len(ins)], rest[len(ins) :]
        out_refs, rest = rest[: len(outs)], rest[len(outs) :]
        in_sem, out_sem = rest[:2]
        bit = smem_refs[0][1] & 1
        loads = []
        number = 0
        for entry, ref in zip(ins, in_refs):
            load = Load(ref)
            if isinstance(entry, Into):
                moves = [(sources.pop(0), ref.at[entry.first : ref.shape[0]])]
            else:
                moves, _ = row_moves(entry, sources, ref, 0, bit)
            for source, target in moves:
                copy = pltpu.make_async_copy(source, target, in_sem.at[number])
                copy.start()
                load.copies.append(copy)
                number += 1
            loads.append(load)
        running = []
        stores = []
        for i, (entry, ref) in enumerate(zip(outs, out_refs)):
            if len(entry) > 2:
                keep, send = targets.pop(0), targets.pop(0)
                stores.append(Split(ref, keep, send, out_sem.at[i], running, bit))
            else:
                stores.append(Store(ref, targets.pop(0), out_sem.at[i], running))
        kernel(*smem_refs, loads, stores, *rest[2:])
        for load in loads:
            load()
        for copy in running:
            copy.wait()

    hbm = pl.BlockSpec(memory_space=pltpu.HBM)
    return pl.pallas_call(
        body,
        name=name,
        out_shape=results,
        in_specs=[pl.BlockSpec(memory_space=pltpu.SMEM)] * n_scalar + [hbm] * n_in,
        out_specs=[hbm] * n_out,
        scratch_shapes=[pltpu.VMEM(shape, kind) for shape, kind in shapes]
        + [pltpu.VMEM(shape, kind) for shape, kind, *_ in outs]
        + [pltpu.SemaphoreType.DMA((max(n_in, 1),)), pltpu.SemaphoreType.DMA((len(outs), SEMS))]
        + [pltpu.VMEM(shape, kind) for shape, kind in scratch],
        compiler_params=pltpu.CompilerParams(vmem_limit_bytes=VMEM_LIMIT),
        cost_estimate=pl.CostEstimate(flops=int(flops), bytes_accessed=0, transcendentals=0),
    )(*scalars, *operands)


def forward_kernel(me_ref, loads, stores, layer_ref, bias_ref):
    index, table, tokens, seg, norm, wq, wk, wv, wo = loads
    normed, q, k, v, mixed, lse, first, last = stores
    length = tokens.ref.shape[0]
    half = length // 2
    index_row = index()[...]
    rows_of = table()[...]
    tok_ref = tokens()
    fill_layer(layer_ref, index_row, rows_of, tok_ref)
    fill_bias(bias_ref, seg()[...])
    norm_ref = norm()
    step = 128
    for at in range(0, length, step):
        rows = slice(at, at + step)
        hat, _ = norm_hat(layer_ref[rows, :])
        normed.ref[rows, :] = (hat * norm_ref[0:1, :] + norm_ref[1:2, :]).astype(BF16)
    normed.send()
    left = normed.ref[...]
    for weight, out in ((wq, q), (wk, k), (wv, v)):
        out.ref[...] = dot_nn(left, weight()[...]).astype(BF16)
        out.send()
    attend(q.ref, k.ref, v.ref, bias_ref, mixed.ref, lse.ref)
    mixed.send()
    lse.send()
    wo_ref = wo()
    for at, out in ((0, first), (half, last)):
        out.ref[...] = dot_nn(mixed.ref[at : at + half, :], wo_ref[...]).astype(BF16)
        out.send()


def grad_out_kernel(me_ref, loads, stores):
    seg, cotangent, return_weight = loads
    gout, gact = stores
    items = item_rows(seg()[...])
    valid = dot_tn(items, jnp.ones((SEG_ROWS, LANES), BF16))
    cot_ref = cotangent()
    for at in range(0, D, LANES):
        cols = slice(at, at + LANES)
        gout.ref[:, cols] = (cot_ref[:, cols].astype(F32) * valid).astype(BF16)
    gout.send()
    weight = return_weight()[...]
    half = gact.ref.shape[0] // 2
    for at in (0, half):
        rows = slice(at, at + half)
        gact.ref[rows, :] = dot_nt(gout.ref[rows, :], weight)
        gact.send(rows)


def feed_kernel(row0, me_ref, loads, stores, pre_ref):
    index, table, tokens, sums, norm, hidden_weight, gact = loads
    second, act, gpre, part = stores
    length = tokens.ref.shape[0]
    index_row = index()[:, row0 : row0 + length]
    rows_of = table()[...]
    tok_ref = tokens()
    fill_layer(pre_ref, index_row, rows_of, tok_ref, sums())
    norm_ref = norm()
    step = 64
    for at in range(0, length, step):
        rows = slice(at, at + step)
        hat, _ = norm_hat(pre_ref[rows, :])
        second.ref[rows, :] = (hat * norm_ref[2:3, :] + norm_ref[3:4, :]).astype(BF16)
    second.send()
    weight_ref = hidden_weight()
    pre_ref[...] = dot_nn(second.ref[...], weight_ref[...])
    gact_ref = gact()
    step = 32

    @pl.loop(0, length // step)
    def _(i):
        rows = pl.ds(pl.multiple_of(i * step, step), step)
        value, slope = gelu_parts(pre_ref[rows, :])
        act.ref[rows, :] = value.astype(BF16)
        gpre.ref[rows, :] = (gact_ref[rows, :] * slope).astype(BF16)

    act.send()
    gpre.send()
    part.ref[...] = dot_nt(gpre.ref[...], weight_ref[...]).astype(BF16)
    part.send()


def store_blocks(nat_ref, base, left, right_ref, weight):
    width = right_ref.shape[1]
    across = width // BLK
    wide = 256

    @pl.loop(0, width // wide)
    def _(step):
        cols = pl.ds(pl.multiple_of(step * wide, wide), wide)
        grad = (dot_tn(left, right_ref[:, cols]) * weight).astype(BF16)
        for i in range(grad.shape[0] // BLK):
            for j in range(wide // BLK):
                nat_ref[base + i * across + step * (wide // BLK) + j] = grad[
                    i * BLK : (i + 1) * BLK, j * BLK : (j + 1) * BLK
                ]


def relative(order, bits):
    out = 0
    for i, bit in enumerate(bits):
        if (order >> (len(bits) - 1 - i)) & 1:
            out |= bit
    return out


def gather_blocks(me_ref, source_ref, positions, first, count, bits, keep_ref, send_ref, block_at):
    owners = 2 ** len(bits)
    for order in range(owners):
        dest = me_ref[0] ^ relative(order, bits)
        out_ref = keep_ref if order < owners // 2 else send_ref
        at = (order % (owners // 2)) * count

        @pl.loop(0, count)
        def _(j, out_ref=out_ref, at=at, place=dest * positions + first):
            out_ref[at + j] = block_at(source_ref[place + j])


def feed_grad_kernel(
    bits, early_slots, positions, late_count, me_ref, source_ref, scal_ref, loads, stores, nat_ref
):
    second, gpre, act, gout = loads
    rest = stores[0]
    weight = scal_ref[0]
    store_blocks(nat_ref, 0, second()[...], gpre(), weight)
    store_blocks(nat_ref, 64, act()[...], gout(), weight)

    def block_at(block):
        return nat_ref[jnp.maximum(block - late_count, 0)]

    if early_slots:
        keep, send = stores[1:]
        gather_blocks(
            me_ref, source_ref, positions, 0, early_slots, bits, keep.ref, send.ref, block_at
        )
        send.send()
        keep.send()

    @pl.loop(0, rest.ref.shape[0])
    def _(i):
        rest.ref[i] = block_at(source_ref[2 ** len(bits) * positions + i])

    rest.send()


def backward_kernel(
    chunks,
    first,
    positions,
    late_count,
    me_ref,
    source_ref,
    scal_ref,
    loads,
    stores,
    gattn_ref,
    gmix_ref,
    grads_ref,
    hid_ref,
    bias_ref,
):
    index, table, tokens, attn, norm, sums, gout = loads[:7]
    wo, seg, q, k, v, lse, normed, mixed, rest, qkv_weight, act, return_weight = loads[7:]
    late, parts = stores[:2]
    chunk_stores = stores[2:]
    length = tokens.ref.shape[0]
    half = length // 2
    width = q.ref.shape[1]
    weight = scal_ref[0]
    step = 64
    index_row, rows_of, tok_ref = index()[...], table()[...], tokens()
    fill_layer(hid_ref, index_row, rows_of, tok_ref, attn())
    norm_ref, gout_ref, sum_ref = norm(), gout(), sums()

    @pl.loop(0, length // step, unroll=2)
    def _(i):
        rows = pl.ds(pl.multiple_of(i * step, step), step)
        hat, inv_std = norm_hat(hid_ref[rows, :])
        grad = sum_ref[rows, :].astype(F32)
        value = gout_ref[rows, :].astype(F32) + norm_back(grad, hat, inv_std, norm_ref[2:3, :])
        gattn_ref[rows, :] = value.astype(BF16)

    fill_bias(bias_ref, seg()[...])
    gmix_ref[...] = dot_nt(gattn_ref[...], wo()[...]).astype(BF16)
    scale = 1.0 / math.sqrt(HEAD)
    q_ref, k_ref, v_ref, lse_ref = q(), k(), v(), lse()

    @pl.loop(0, q_ref.shape[1] // HEAD)
    def _(number):
        cols = head_columns(number)
        here = head_lanes(length, number % 2)
        keys, vals = k_ref[:, cols], v_ref[:, cols]
        query = q_ref[:, cols] * scale
        gmix = gmix_ref[:, cols]
        scores = dot_nt(jnp.where(here, query, 0.0).astype(BF16), keys) + bias_ref[...]
        probs = jnp.exp(scores - lane_of(lse_ref[...], number))
        grad_probs = dot_nt(jnp.where(here, gmix, 0.0).astype(BF16), vals)
        grad_scores = (
            probs * (grad_probs - jnp.sum(probs * grad_probs, axis=-1, keepdims=True))
        ).astype(BF16)
        for place, value in (
            (2, dot_tn(probs.astype(BF16), gmix)),
            (1, dot_tn(grad_scores, query)),
            (0, dot_nn(grad_scores, keys) * scale),
        ):
            old = grads_ref[place, :, cols]
            grads_ref[place, :, cols] = jnp.where(here, value.astype(BF16), old)

    weights_ref, act_ref, return_ref = qkv_weight(), act(), return_weight()

    @pl.loop(0, 2)
    def _(i):
        rows = pl.ds(pl.multiple_of(i * half, half), half)
        total = sum(
            dot_nt(grads_ref[place, rows, :], weights_ref[place * D : (place + 1) * D, :])
            for place in range(3)
        )
        parts.ref[pl.ds(pl.multiple_of(2 * i * half, half), half), :] = total.astype(BF16)
        parts.ref[pl.ds(pl.multiple_of((2 * i + 1) * half, half), half), :] = dot_nn(
            act_ref[rows, :], return_ref[...]
        ).astype(BF16)

    parts.send()
    pool_ref = rest.ref
    left = normed()[...]
    share = D // BLK * (width // BLK)

    @pl.loop(0, 3)
    def _(place):
        store_blocks(pool_ref, place * share, left, grads_ref.at[place], weight)

    store_blocks(pool_ref, 3 * share, mixed()[...], gattn_ref, weight)
    rest()
    for number, (count, bits) in enumerate(chunks):
        keep, send = chunk_stores[2 * number : 2 * number + 2]
        gather_blocks(
            me_ref,
            source_ref,
            positions,
            first,
            count,
            bits,
            keep.ref,
            send.ref,
            lambda place: pool_ref[place],
        )
        send.send()
        keep.send()
        first += count
    late.send_if(scal_ref[3] > 0.5, pool_ref.at[0:late_count])


def overflow_kernel(first, count, bits, positions, me_ref, source_ref, loads, stores):
    (late,) = loads
    keep, send = stores
    late_ref = late()
    last = late_ref.shape[0] - 1
    gather_blocks(
        me_ref,
        source_ref,
        positions,
        first,
        count,
        bits,
        keep.ref,
        send.ref,
        lambda place: late_ref[jnp.minimum(place, last)],
    )
    keep.send()
    send.send()


def add_rows(acc_ref, at, values):
    acc_ref[at : at + 8, :] += jnp.sum(values.reshape(values.shape[0] // 8, 8, D), axis=0)


def finish_kernel(me_ref, scal_ref, loads, stores, layer_ref, acc_ref):
    index, table, tokens, attn_a, attn_b, norm, outputs, second_a, second_b, gout = loads
    out, gin, sums = stores
    half = attn_a.ref.shape[0]
    weight = scal_ref[0]
    step = 64
    acc_ref[...] = jnp.zeros_like(acc_ref)
    index_row = index()[...]
    rows_of = table()[...]
    tok_ref = tokens()
    for row0, attn, second in ((0, attn_a, second_a), (half, attn_b, second_b)):
        part = slice(row0, row0 + half)
        fill_layer(layer_ref, index_row[:, part], rows_of, tok_ref.at[part, :])
        attn_ref, norm_ref, second_ref, gout_ref, both_ref = (
            attn(),
            norm(),
            second(),
            gout(),
            outputs(),
        )
        @pl.loop(0, half // step)
        def _(
            i,
            row0=row0,
            attn_ref=attn_ref,
            norm_ref=norm_ref,
            second_ref=second_ref,
            gout_ref=gout_ref,
            both_ref=both_ref,
        ):
            at = pl.multiple_of(i * step, step)
            here = pl.ds(at, step)
            rows = pl.ds(pl.multiple_of(row0 + at, step), step)
            first_at = pl.multiple_of(2 * row0 + at, step)
            layer = layer_ref[here, :]
            hat, inv_std = norm_hat(layer)
            hid = layer + attn_ref[here, :].astype(F32)
            mlp = both_ref[pl.ds(first_at + half, step), :].astype(F32)
            out.ref[rows, :] = hid + mlp
            hat2, inv_std2 = norm_hat(hid)
            grad2 = second_ref[here, :].astype(F32)
            ghid = gout_ref[rows, :].astype(F32) + norm_back(
                grad2, hat2, inv_std2, norm_ref[2:3, :]
            )
            add_rows(acc_ref, 16, grad2 * hat2)
            add_rows(acc_ref, 24, grad2)
            grad = both_ref[pl.ds(first_at, step), :].astype(F32)
            gin.ref[rows, :] = ghid + norm_back(grad, hat, inv_std, norm_ref[0:1, :])
            add_rows(acc_ref, 0, grad * hat)
            add_rows(acc_ref, 8, grad)

        out.send(part)
        gin.send(part)
    for i in range(4):
        sums.ref[i : i + 1, :] = (
            jnp.sum(acc_ref[8 * i : 8 * i + 8, :], axis=0, keepdims=True) * weight
        )
    sums.ref[4:5, :] = jnp.full((1, D), weight, F32)
    sums.ref[5:8, :] = jnp.zeros((3, D), F32)
    sums.send()


def columns(rows):
    count = rows.shape[0]
    if count % 8:
        return jnp.stack(
            [jnp.transpose(jnp.broadcast_to(rows[i : i + 1], (BLK, BLK)))[:, 0:1] for i in range(count)]
        )
    turned = jnp.transpose(rows)
    return jnp.stack([turned[:, i : i + 1] for i in range(count)])


def reflect(blocks, left, right, coef_left, coef_right):
    along = jnp.sum(left * blocks, axis=1, keepdims=True) * coef_left
    blocks = blocks - left * along
    across = jnp.sum(blocks * right, axis=2, keepdims=True) * coef_right
    return blocks - across * right


def reflectors(left_ref, right_ref):
    left, right = left_ref[...], right_ref[...]
    coef_left = (2.0 / jnp.sum(left * left, axis=1, keepdims=True))[:, :, None]
    coef_right = (2.0 / jnp.sum(right * right, axis=1, keepdims=True))[:, :, None]
    return (columns(left), right[:, None, :], coef_left, coef_right)


def rotate_kernel(counts, group, me_ref, place_ref, loads, stores, found_ref):
    left, right = loads[:2]
    grads, turned, total = stores
    parts = reflectors(left(), right())
    at = 0
    for number, count in enumerate(counts):
        keep, got = loads[2 + 2 * number : 4 + 2 * number]
        found_ref[at : at + count] = keep()[...].astype(F32) + got()[...].astype(F32)
        at += count
    slots = grads.ref.shape[0]
    for slot in range(slots):
        grads.ref[slot] = found_ref[place_ref[me_ref[0] * slots + slot]]
    grads.send()
    square = jnp.zeros((8, BLK), F32)
    for at in range(0, slots, group):
        rows = slice(at, at + group)
        grad = grads.ref[rows]
        square = square + jnp.sum((grad * grad).reshape(group * BLK // 8, 8, BLK), axis=0)
        turned.ref[rows] = reflect(grad, *(part[rows] for part in parts))
        turned.send(rows)
    total.ref[...] = jnp.full((8, BLK), jnp.sum(square), F32)
    total.send()


def inverse(value):
    guess = pl.reciprocal(value, approx=True)
    return guess * (2.0 - value * guess)


def update_kernel(group, me_ref, scal_ref, loads, stores):
    sums, norm, norm_first, norm_second, left, right = loads[:6]
    grads, turned_grads, old_first, old_second, old_master = loads[6:]
    out_grad, out_first, out_second, out_master, out_copy = stores[:5]
    norm_pair, norm_square, norm_value, clip_out = stores[5:]
    inv_one = 1.0 / scal_ref[1]
    inv_two = 1.0 / scal_ref[2]
    sums_ref = sums()
    share = 1.0 / sums_ref[4:5, 0:BLK]
    norm_grad = sums_ref[0:4, :] * share[:, 0:1]
    total = sums_ref[5:6, 0:BLK] * (share * share) + jnp.sum(norm_grad * norm_grad)
    clip_norm = jnp.sqrt(total)
    clip = jnp.minimum(1.0, clip_max / clip_norm)
    factor = (share * clip)[:, None, :]
    parts = reflectors(left(), right())
    slots = left.ref.shape[0]
    entries = 1.0 / (BLK * BLK)
    for at in range(0, slots, group):
        rows = slice(at, at + group)
        out_grad.ref[rows] = grads()[rows] * factor
        rotated = turned_grads()[rows] * factor
        first = beta_one * old_first()[rows] + (1.0 - beta_one) * rotated
        second = beta_two * old_second()[rows] + (1.0 - beta_two) * rotated * rotated
        out_first.ref[rows] = first
        out_second.ref[rows] = second
        spread = second * inv_two
        normal = (first * inv_one) * inverse(spread * lax.rsqrt(spread) + adam_eps)
        turned = reflect(normal, *(part[rows] for part in parts))
        master = old_master()[rows]
        size = jnp.sum(jnp.sum(master * master, axis=1, keepdims=True), axis=2, keepdims=True)
        move = jnp.sum(jnp.sum(turned * turned, axis=1, keepdims=True), axis=2, keepdims=True)
        trust = jnp.sqrt(size * entries + trust_eps) / jnp.sqrt(move * entries + trust_eps)
        fresh = master - (step_rate * trust) * turned
        out_master.ref[rows] = fresh
        out_copy.ref[rows] = fresh.astype(BF16)
        for out in (out_grad, out_first, out_second, out_master, out_copy):
            out.send(rows)
    clip_out.ref[...] = jnp.broadcast_to(clip_norm, clip_out.ref.shape)
    clip_out.send()
    clipped = norm_grad * clip[:, 0:1]
    first = beta_one * norm_first()[...] + (1.0 - beta_one) * clipped
    second = beta_two * norm_second()[...] + (1.0 - beta_two) * clipped * clipped
    norm_pair.ref[0] = clipped
    norm_pair.ref[1] = first
    norm_pair.send()
    norm_square.ref[...] = second
    norm_square.send()
    norm_value.ref[...] = norm()[...] - step_rate * (first * inv_one) / (
        jnp.sqrt(second * inv_two) + adam_eps
    )
    norm_value.send()


def swap(value, axis, bit):
    count = lax.axis_size(axis)
    return lax.ppermute(value, axis, [(i, i ^ bit) for i in range(count)])


def plus(left, right):
    return (left.astype(F32) + right.astype(F32)).astype(BF16)


def after(value, *others):
    return lax.optimization_barrier((value, *others))[0]


def mp_far(total, wait=None):
    bit = 2
    while bit < lax.axis_size("mp"):
        got = swap(total, "mp", bit)
        total = plus(total, got if wait is None else after(got, wait))
        bit *= 2
    return total


def mp_sum(keep, send):
    total = mp_far(plus(keep, swap(send, "mp", 1)))
    return (total, swap(total, "mp", 1))


def early_count(slots):
    return slots // 3 if slots >= 24 else 0


def split_counts(slots, bits):
    if slots >= 8:
        last = slots // 4
        head = (slots - last + 2) // 2
        crossed = (bits[1], bits[0]) + bits[2:]
        return ((head, bits), (slots - last - head, bits), (last, crossed))
    return ((1, bits),) * slots if slots <= 3 else ((slots - slots // 2, bits), (slots // 2, bits))


def exclusive_sum(values):
    size = values.shape[-1]
    before = jnp.asarray(np.tril(np.ones((size, size), np.int32), -1))
    return jnp.sum(values[..., None, :] * before, axis=-1)


def rest_count(blocks, late_count, n_dp, slots, early_slots):
    total = blocks - late_count
    full, over = divmod(total, slots)
    return total - full * early_slots - min(over, early_slots)


def slot_tables(owner_list, n_dp, slots, early_slots, late_count):
    blocks = owner_list.shape[0]
    owned = owner_list.reshape(n_dp, slots)
    early = (owned >= late_count).astype(jnp.int32)
    if early_slots:
        goes = early * (exclusive_sum(early) < early_slots).astype(jnp.int32)
        place = jnp.where(goes == 1, exclusive_sum(early), early_slots + exclusive_sum(1 - goes))
        positions = slots + early_slots
        hit = place[:, None, :] == jnp.arange(positions, dtype=jnp.int32)[None, :, None]
        source = jnp.sum(jnp.where(hit, owned[:, None, :], 0), axis=2)
        short = jnp.any(jnp.sum(early, axis=1) < early_slots)
    else:
        place = jnp.broadcast_to(jnp.arange(slots, dtype=jnp.int32), (n_dp, slots))
        source, short = owned, jnp.zeros((), bool)
    later = source[:, early_slots:].reshape(-1)
    is_rest = (later >= late_count).astype(jnp.int32)
    order = exclusive_sum(is_rest)
    count = rest_count(blocks, late_count, n_dp, slots, early_slots)
    hit = (order[None, :] == jnp.arange(count, dtype=jnp.int32)[:, None]) & (is_rest[None, :] == 1)
    rest = jnp.sum(jnp.where(hit, later[None, :], 0), axis=1)
    later = jnp.where(is_rest == 1, late_count + order, later)
    source = jnp.concatenate([source[:, :early_slots], later.reshape(n_dp, -1)], axis=1)
    return (jnp.concatenate([source.reshape(-1), rest]), place.reshape(-1), short)


def shards(
    tokens,
    cotangent,
    segment_ids,
    table_index,
    group_count,
    owner_list,
    step_count,
    query_weight,
    key_weight,
    value_weight,
    output_weight,
    hidden_weight,
    return_weight,
    norm_params,
    norm_first,
    norm_second,
    master_blocks,
    first_moment,
    second_moment,
    left_vector,
    right_vector,
):
    length = tokens.shape[0]
    half = length // 2
    width = query_weight.shape[1]
    heads = width // HEAD
    units = hidden_weight.shape[1]
    slots = master_blocks.shape[0]
    blocks = owner_list.shape[0]
    late_count = blocks // 3
    n_dp = lax.axis_size("dp")
    natural = tuple(1 << i for i in range(n_dp.bit_length() - 1))
    early_slots = early_count(slots)
    positions = slots + early_slots
    me = jnp.stack([lax.axis_index("dp"), lax.axis_index("mp")]).astype(jnp.int32)
    step_value = step_count[0].astype(F32)
    source, place, short = slot_tables(owner_list, n_dp, slots, early_slots, late_count)
    scal = jnp.stack(
        [
            group_count[0].astype(F32),
            1.0 - jnp.power(beta_one, step_value),
            1.0 - jnp.power(beta_two, step_value),
            short.astype(F32),
        ]
    )
    seg_row = segment_ids.reshape(1, length)
    index_row = table_index.reshape(1, length)
    table = jnp.asarray(position_rows())
    rows_d = (length, D)
    half_d = (half, D)
    unit = 2 * length * D * D
    wide = ((length, width), BF16)

    normed, q, k, v, mixed, lse, keep_a, send_a, keep_b, send_b = call(
        forward_kernel,
        "attention_forward",
        (me,),
        (
            index_row,
            table,
            tokens,
            seg_row,
            norm_params,
            query_weight,
            key_weight,
            value_weight,
            output_weight,
        ),
        [
            (rows_d, BF16),
            wide,
            wide,
            wide,
            wide,
            ((length, heads), F32),
            (half_d, BF16, True),
            (half_d, BF16, True),
        ],
        [(rows_d, F32), ((length, length), F32)],
        flops=5 * unit,
    )
    near_a = plus(keep_a, swap(send_a, "mp", 1))
    near_b = plus(keep_b, swap(send_b, "mp", 1))
    token = near_b
    grad_out, grad_act = call(
        grad_out_kernel,
        "grad_of_act",
        (me,),
        (seg_row, cotangent, return_weight),
        [(rows_d, BF16), ((length, units), F32)],
        flops=2 * unit,
        after=token,
    )

    far_a = mp_far(near_a, grad_act)
    attn_a = Pair(far_a, swap(far_a, "mp", 1))
    def feed(row0, name, sums, token):
        return call(
            functools.partial(feed_kernel, row0),
            name,
            (me,),
            (
                index_row,
                table,
                Rows(tokens, row0, half),
                sums,
                norm_params,
                hidden_weight,
                Rows(grad_act, row0, half),
            ),
            [
                (half_d, BF16),
                ((half, units), BF16),
                ((half, units), BF16),
                (half_d, BF16, True),
            ],
            [((half, units), F32)],
            flops=4 * unit,
            after=token,
        )

    second_a, act_a, gpre_a, keep_a, send_a = feed(0, "feed_forward_a", attn_a, None)
    far_b = mp_far(near_b, keep_a)
    attn_b = Pair(far_b, swap(far_b, "mp", 1))
    second_b, act_b, gpre_b, keep_b, send_b = feed(half, "feed_forward_b", attn_b, keep_a)
    near_a = plus(keep_a, swap(send_a, "mp", 1))
    near_b = plus(keep_b, swap(send_b, "mp", 1))
    far_a = mp_far(near_a, near_b)
    chunk_e = [((n_dp // 2 * early_slots, BLK, BLK), BF16)] * 2 if early_slots else []
    count = rest_count(blocks, late_count, n_dp, slots, early_slots)
    rest, *chunk_e = call(
        functools.partial(feed_grad_kernel, natural, early_slots, positions, late_count),
        "feed_weight_grads",
        (me, source, scal),
        (Stack(second_a, second_b), Stack(gpre_a, gpre_b), Stack(act_a, act_b), grad_out),
        [((count, BLK, BLK), BF16)] + chunk_e,
        [((blocks - late_count, BLK, BLK), BF16)],
        flops=4 * unit,
        after=near_b,
    )
    far_b = mp_far(near_b, rest)
    sum_a = Pair(far_a, swap(far_a, "mp", 1))
    sum_b = Pair(far_b, swap(far_b, "mp", 1))
    got_e = swap(chunk_e[1], "dp", 1) if early_slots else None
    chunks = split_counts(slots - early_slots, natural)
    chunk_shapes = []
    for count, _ in chunks:
        chunk_shapes += [((n_dp // 2 * count, BLK, BLK), BF16)] * 2
    outs = call(
        functools.partial(backward_kernel, chunks, early_slots, positions, late_count),
        "attention_backward",
        (me, source, scal),
        (
            index_row,
            table,
            tokens,
            Stack(attn_a, attn_b),
            norm_params,
            Stack(sum_a, sum_b),
            grad_out,
            output_weight,
            seg_row,
            q,
            k,
            v,
            lse,
            normed,
            mixed,
            Into(rest, late_count),
            Stack(query_weight, key_weight, value_weight),
            Stack(act_a, act_b),
            return_weight,
        ),
        [((late_count, BLK, BLK), BF16), ((2 * length, D), BF16, True)] + chunk_shapes,
        [(rows_d, BF16)]
        + [((length, width), BF16), ((3, length, width), BF16)]
        + [(rows_d, F32), ((length, length), F32)],
        flops=10 * unit,
    )
    late, keep, send = outs[:3]
    queue = [(outs[3 + 2 * i], outs[4 + 2 * i]) for i in range(len(chunks))]
    counts = [count for count, _ in chunks]
    orders = [bits for _, bits in chunks]

    stages = len(natural)
    state = [(first, swap(second, "dp", bits[0])) for (first, second), bits in zip(queue, orders)]
    if early_slots:
        state.insert(0, (chunk_e[0], after(got_e, keep)))
        counts.insert(0, early_slots)
        orders.insert(0, natural)
    level = [0] * len(state)
    last = []

    def in_turn(got):
        got = after(got, *last)
        last[:] = [got]
        return got

    def halve(number):
        keep, got = state[number]
        got = in_turn(got)
        if level[number] < stages - 1:
            n = keep.shape[0] // 2
            keep, send = plus(keep[:n], got[:n]), plus(keep[n:], got[n:])
            got = swap(send, "dp", orders[number][level[number] + 1])
            last.append(send)
        level[number] += 1
        state[number] = (keep, got)

    def mp_first(keep, send):
        return plus(keep, in_turn(swap(send, "mp", 1)))

    def mp_rest(near):
        bit = 2
        while bit < lax.axis_size("mp"):
            near = plus(near, in_turn(swap(near, "mp", bit)))
            bit *= 2
        return Pair(near, swap(near, "mp", 1))

    if early_slots:
        halve(0)
    def finish(both):
        outputs = call(
            finish_kernel,
            "layer_outputs",
            (me, scal),
            (
                index_row,
                table,
                tokens,
                attn_a,
                attn_b,
                norm_params,
                both,
                sum_a,
                sum_b,
                grad_out,
            ),
            [(rows_d, F32), (rows_d, F32), ((8, D), F32)],
            [(half_d, F32), ((32, D), F32)],
            flops=2 * unit,
        )
        last.append(outputs[2])
        return outputs

    plan = ["near", "far", "finish"]
    if early_slots and stages == 3:
        plan = ["near",(3,0),(1,0),(0,1),(2,0),(1,1),(3,1),(0,2),(2,1),(1,2),"far","finish"]
    plan += [(i, d - i) for d in range(len(state) + stages) for i in range(len(state))]
    for entry in plan:
        if entry == "near":
            near = plus(keep, in_turn(swap(send, "mp", 1)))
        elif entry == "far":
            bit = 2
            while bit < lax.axis_size("mp"):
                near = plus(near, in_turn(swap(near, "mp", bit)))
                bit *= 2
            both = Pair(near, swap(near, "mp", 1))
        elif entry == "finish":
            out, input_grad, sums = finish(both)
        elif level[entry[0]] == entry[1] < stages:
            halve(entry[0])
    pending = [array for pair in state for array in pair]

    if early_slots:
        shape = (n_dp // 2 * early_slots, BLK, BLK)

        def exchange(late):
            keep, send = call(
                functools.partial(overflow_kernel, slots, early_slots, natural, positions),
                "overflow",
                (me, source),
                (late,),
                [(shape, BF16), (shape, BF16)],
            )
            bit = 1
            while True:
                got = swap(send, "dp", bit)
                bit *= 2
                if bit >= n_dp:
                    return (keep, got)
                n = keep.shape[0] // 2
                keep, send = plus(keep[:n], got[:n]), plus(keep[n:], got[n:])

        def nothing(late):
            zero = jnp.zeros((early_slots, BLK, BLK), BF16)
            return (zero, zero)

        pending += list(lax.cond(short, exchange, nothing, late))
        counts.append(early_slots)

    left = left_vector.reshape(slots, BLK)
    right = right_vector.reshape(slots, BLK)
    block_f32 = ((slots, BLK, BLK), F32)
    group = 4 if slots % 4 == 0 else 1
    grads, rotated, square = call(
        functools.partial(rotate_kernel, counts, group),
        "rotate",
        (me, place),
        (left, right, *pending),
        [block_f32, block_f32, ((8, BLK), F32)],
        [((sum(counts), BLK, BLK), F32)],
        flops=unit,
    )
    bit = 1
    while bit < lax.axis_size("mp"):
        square = square + swap(square, "mp", bit)
        bit *= 2
    sums = sums + jnp.pad(square[0:1], ((5, 2), (0, D - BLK)))
    bit = 1
    while bit < n_dp:
        sums = sums + swap(sums, "dp", bit)
        bit *= 2
    new = call(
        functools.partial(update_kernel, group),
        "update",
        (me, scal),
        (
            sums,
            norm_params,
            norm_first,
            norm_second,
            left,
            right,
            grads,
            rotated,
            first_moment.reshape(slots, BLK, BLK),
            second_moment.reshape(slots, BLK, BLK),
            master_blocks.reshape(slots, BLK, BLK),
        ),
        [block_f32] * 4
        + [
            ((slots, BLK, BLK), BF16),
            ((2, 4, D), F32),
            ((4, D), F32),
            ((4, D), F32),
            ((8, BLK), F32),
        ],
        flops=unit,
    )
    shard_shape = (slots, 1, BLK, BLK)
    return (
        out,
        input_grad,
        new[0].reshape(shard_shape),
        new[1].reshape(shard_shape),
        new[2].reshape(shard_shape),
        new[3].reshape(shard_shape),
        new[4].reshape(shard_shape),
        new[5],
        new[6],
        new[7],
        new[8][0, 0],
    )


def solution(mesh):
    placed = (
        P("dp", None),
        P("dp", None),
        P("dp"),
        P("dp"),
        P("dp"),
        P(),
        P(),
        P(None, "mp"),
        P(None, "mp"),
        P(None, "mp"),
        P("mp", None),
        P(None, "mp"),
        P("mp", None),
        P(),
        P(),
        P(),
        P("dp", "mp", None, None),
        P("dp", "mp", None, None),
        P("dp", "mp", None, None),
        P("dp", "mp", None),
        P("dp", "mp", None),
    )
    return jax.shard_map(
        shards,
        mesh=mesh,
        in_specs=placed,
        out_specs=(
            P("dp", None),
            P("dp", None),
            P("dp", "mp", None, None),
            P("dp", "mp", None, None),
            P("dp", "mp", None, None),
            P("dp", "mp", None, None),
            P("dp", "mp", None, None),
            P(),
            P(),
            P(),
            P(),
        ),
        check_vma=False,
    )
```

```python
import functools
import math

import jax
import jax.numpy as jnp
import numpy as np
from jax import lax
from jax.experimental import pallas as pl
from jax.experimental.pallas import tpu as pltpu
from jax.sharding import PartitionSpec as P

D = 1024
HEAD = 64
BLK = 128
LANES = 128
POS_ROWS = 64
SEG_ROWS = 32

clip_max = 1.0
beta_one = 0.5
beta_two = 0.5
adam_eps = 1e-08
step_rate = 0.25
norm_eps = 1e-06
trust_eps = 1e-06

F32 = jnp.float32
BF16 = jnp.bfloat16
MIB = 1024 * 1024
VMEM_LIMIT = 60 * MIB

ERF_P = 0.425
ERF_COEF = (
    0.11983931305209315,
    0.12092032287702306,
    0.10035292560006456,
    0.12754356284084392,
    -0.051626023300101125,
    0.20380940869554587,
    -0.1565787944569494,
    0.035739213095996265,
)


def position_rows():
    coords = np.concatenate(
        [1.75 * np.arange(8), 1.0 * np.arange(14), 0.5 * np.arange(28), np.zeros(POS_ROWS - 50)]
    )
    quarter = D // 4
    freqs = np.power(np.float32(10000.0), -np.arange(quarter, dtype=np.float32) / np.float32(quarter))
    args = (coords.astype(np.float32)[:, None] * freqs.astype(np.float32)[None, :]).astype(np.float64)
    table = np.concatenate([np.sin(args), np.cos(args)], axis=1).astype(np.float32)
    parts = []
    rest = table
    for _ in range(3):
        part = rest.astype(jnp.bfloat16)
        parts.append(part)
        rest = rest - part.astype(np.float32)
    return np.concatenate(parts, axis=0)


def dot_nn(left, right):
    return lax.dot_general(left, right, (((1,), (0,)), ((), ())), preferred_element_type=F32)


def dot_nt(left, right):
    return lax.dot_general(left, right, (((1,), (1,)), ((), ())), preferred_element_type=F32)


def dot_tn(left, right):
    return lax.dot_general(left, right, (((0,), (0,)), ((), ())), preferred_element_type=F32)


def norm_hat(values):
    center = values - jnp.mean(values, axis=-1, keepdims=True)
    inv_std = lax.rsqrt(jnp.mean(center * center, axis=-1, keepdims=True) + norm_eps)
    return (center * inv_std, inv_std)


def norm_back(grad_out, normal, inv_std, gain):
    scaled = grad_out * gain
    return inv_std * (
        scaled
        - jnp.mean(scaled, axis=-1, keepdims=True)
        - normal * jnp.mean(scaled * normal, axis=-1, keepdims=True)
    )


def gelu_parts(values):
    bell = jnp.exp(-0.5 * values * values)
    t = 1.0 / (1.0 + (ERF_P / math.sqrt(2.0)) * jnp.abs(values))
    poly = ERF_COEF[-1]
    for coef in ERF_COEF[-2::-1]:
        poly = poly * t + coef
    tail = poly * t * bell
    dist = jnp.where(values >= 0.0, 1.0 - tail, tail)
    return (values * dist, dist + values * ((1.0 / math.sqrt(2.0 * math.pi)) * bell))


def item_rows(seg_row):
    rows = lax.broadcasted_iota(jnp.int32, (SEG_ROWS, seg_row.shape[1]), 0)
    return jnp.where(rows == seg_row, 1.0, 0.0).astype(BF16)


def head_lanes(rows, head):
    lanes = lax.broadcasted_iota(jnp.int32, (rows, LANES), 1)
    return (lanes // HEAD) == head


def position_hots(index):
    length = index.shape[1]
    big = index >= 260
    mid = index >= 64
    offset = jnp.where(big, 260, jnp.where(mid, 64, 0))
    base = jnp.where(big, 22, jnp.where(mid, 8, 0))
    side = jnp.where(big, 28, jnp.where(mid, 14, 8))
    inv_side = jnp.where(big, 1.0 / 28.0, jnp.where(mid, 1.0 / 14.0, 1.0 / 8.0)).astype(F32)
    local = index - offset
    row = jnp.floor((local.astype(F32) + 0.5) * inv_side).astype(jnp.int32)
    col = local - row * side
    rows = lax.broadcasted_iota(jnp.int32, (3 * POS_ROWS, length), 0) & (POS_ROWS - 1)
    row_hot = jnp.where(rows == base + row, 1.0, 0.0).astype(BF16)
    col_hot = jnp.where(rows == base + col, 1.0, 0.0).astype(BF16)
    return (row_hot, col_hot)


def fill_layer(out_ref, index_row, table, tok_ref, sum_ref=None):
    half = D // 2
    for hot, cols in zip(position_hots(index_row), (slice(0, half), slice(half, D))):
        value = dot_tn(hot, table) + tok_ref[:, cols].astype(F32)
        if sum_ref is not None:
            value = value + sum_ref[:, cols].astype(F32)
        out_ref[:, cols] = value


def fill_bias(bias_ref, seg_row):
    length = seg_row.shape[1]
    items = item_rows(seg_row)
    same = dot_tn(items, items)
    diag = lax.broadcasted_iota(jnp.int32, (length, length), 0) == lax.broadcasted_iota(
        jnp.int32, (length, length), 1
    )
    bias_ref[...] = jnp.where((same > 0.5) | diag, 0.0, -1e30)


def lane_of(values, number):
    lanes = lax.broadcasted_iota(jnp.int32, values.shape, 1)
    return jnp.sum(jnp.where(lanes == number, values, 0.0), axis=1, keepdims=True)


def head_columns(number):
    return pl.ds(pl.multiple_of((number // 2) * LANES, LANES), LANES)


def attend(q_ref, k_ref, v_ref, bias_ref, mixed_ref, lse_ref):
    count = q_ref.shape[0]
    scale = 1.0 / math.sqrt(HEAD)
    step = 512
    for pair in range(q_ref.shape[1] // LANES):
        cols = slice(pair * LANES, (pair + 1) * LANES)
        keys = k_ref[:, cols]
        vals = v_ref[:, cols]
        for at in range(0, count, step):
            rows = slice(at, at + step)
            query = q_ref[rows, cols] * scale
            outs = []
            for head in range(2):
                here = head_lanes(step, head)
                scores = dot_nt(jnp.where(here, query, 0.0).astype(BF16), keys) + bias_ref[rows, :]
                peak = jnp.max(scores, axis=-1, keepdims=True)
                expon = jnp.exp(scores - peak)
                total = jnp.sum(expon, axis=-1, keepdims=True)
                outs.append(dot_nn(expon.astype(BF16), vals) * (1.0 / total))
                number = pair * 2 + head
                lse_ref[rows, number : number + 1] = peak + jnp.log(total)
            mixed_ref[rows, cols] = jnp.where(
                head_lanes(step, 0), outs[0], outs[1]
            ).astype(BF16)


class Load:
    def __init__(self, ref):
        self.ref = ref
        self.copies = []

    def __call__(self):
        for copy in self.copies:
            copy.wait()
        self.copies = []
        return self.ref


class Store:
    def __init__(self, ref, target, sem, running):
        self.ref = ref
        self.target = target
        self.sem = sem
        self.running = running
        self.sent = 0

    def send(self, rows=None):
        source = self.ref if rows is None else self.ref.at[rows]
        target = self.target if rows is None else self.target.at[rows]
        copy = pltpu.make_async_copy(source, target, self.sem.at[self.sent])
        copy.start()
        self.sent += 1
        self.running.append(copy)


    def send_if(self, flag, source):
        @pl.when(flag)
        def _():
            copy = pltpu.make_async_copy(source, self.target, self.sem.at[0])
            copy.start()
            copy.wait()


class Split:
    def __init__(self, ref, keep, send, sem, running, bit):
        self.ref = ref
        self.targets = ((send, 1 - bit), (keep, bit))
        self.sem = sem
        self.running = running

    def send(self):
        half = self.ref.shape[0] // 2
        for i, (target, which) in enumerate(self.targets):
            rows = pl.ds(pl.multiple_of(which * half, half), half)
            copy = pltpu.make_async_copy(self.ref.at[rows], target, self.sem.at[i])
            copy.start()
            self.running.append(copy)


class Rows:
    def __init__(self, array, first, count):
        self.array = array
        self.first = first
        self.count = count


class Into:
    def __init__(self, array, first):
        self.array = array
        self.first = first


class Pair:
    def __init__(self, own, other, first=0, count=None):
        self.own = own
        self.other = other
        self.first = first
        self.count = own.shape[0] if count is None else count


class Stack:
    def __init__(self, *parts):
        self.parts = parts


SEMS = 24


def row_moves(entry, sources, ref, first, bit):
    if isinstance(entry, Stack):
        moves = []
        for part in entry.parts:
            more, first = row_moves(part, sources, ref, first, bit)
            moves += more
        return (moves, first)
    if isinstance(entry, Pair):
        moves = []
        for which in (bit, 1 - bit):
            rows = pl.ds(pl.multiple_of(first + which * entry.count, entry.count), entry.count)
            part = sources.pop(0).at[entry.first : entry.first + entry.count]
            moves.append((part, ref.at[rows]))
        return (moves, first + 2 * entry.count)
    count = entry.count if isinstance(entry, Rows) else entry.shape[0]
    source = sources.pop(0)
    if isinstance(entry, Rows):
        source = source.at[entry.first : entry.first + count]
    whole = count == ref.shape[0]
    return ([(source, ref if whole else ref.at[first : first + count])], first + count)


def flat(entry):
    if isinstance(entry, Stack):
        parts = [flat(part) for part in entry.parts]
        return (sum((p[0] for p in parts), []), sum(p[1] for p in parts), parts[0][2])
    if isinstance(entry, Pair):
        return ([entry.own, entry.other], 2 * entry.count, entry.own)
    if isinstance(entry, Rows):
        return ([entry.array], entry.count, entry.array)
    if isinstance(entry, Into):
        return ([entry.array], entry.first + entry.array.shape[0], entry.array)
    return ([entry], entry.shape[0], entry)


def call(kernel, name, scalars, ins, outs, scratch=(), flops=0, after=None):
    operands = []
    shapes = []
    for entry in ins:
        arrays, rows, like = flat(entry)
        operands += arrays
        shapes.append(((rows,) + like.shape[1:], like.dtype))
    if after is not None:
        operands.append(after)
    results = []
    for shape, kind, *split in outs:
        if split:
            results += [jax.ShapeDtypeStruct((shape[0] // 2,) + shape[1:], kind)] * 2
        else:
            results.append(jax.ShapeDtypeStruct(shape, kind))
    n_scalar, n_in, n_out = len(scalars), len(operands), len(results)

    def body(*refs):
        smem_refs = refs[:n_scalar]
        sources = list(refs[n_scalar : n_scalar + n_in])
        targets = list(refs[n_scalar + n_in : n_scalar + n_in + n_out])
        rest = list(refs[n_scalar + n_in + n_out :])
        in_refs, rest = rest[: len(ins)], rest[len(ins) :]
        out_refs, rest = rest[: len(outs)], rest[len(outs) :]
        in_sem, out_sem = rest[:2]
        bit = smem_refs[0][1] & 1
        loads = []
        number = 0
        for entry, ref in zip(ins, in_refs):
            load = Load(ref)
            if isinstance(entry, Into):
                moves = [(sources.pop(0), ref.at[entry.first : ref.shape[0]])]
            else:
                moves, _ = row_moves(entry, sources, ref, 0, bit)
            for source, target in moves:
                copy = pltpu.make_async_copy(source, target, in_sem.at[number])
                copy.start()
                load.copies.append(copy)
                number += 1
            loads.append(load)
        running = []
        stores = []
        for i, (entry, ref) in enumerate(zip(outs, out_refs)):
            if len(entry) > 2:
                keep, send = targets.pop(0), targets.pop(0)
                stores.append(Split(ref, keep, send, out_sem.at[i], running, bit))
            else:
                stores.append(Store(ref, targets.pop(0), out_sem.at[i], running))
        kernel(*smem_refs, loads, stores, *rest[2:])
        for load in loads:
            load()
        for copy in running:
            copy.wait()

    hbm = pl.BlockSpec(memory_space=pltpu.HBM)
    scalar = pl.BlockSpec(memory_space=pltpu.SMEM)
    return pl.pallas_call(
        body,
        name=name,
        out_shape=results,
        in_specs=[pl.BlockSpec(memory_space=pltpu.SMEM)] * n_scalar + [hbm] * n_in,
        out_specs=[scalar if r.shape == (1, 1) else hbm for r in results],
        scratch_shapes=[pltpu.VMEM(shape, kind) for shape, kind in shapes]
        + [pltpu.VMEM(shape, kind) for shape, kind, *_ in outs]
        + [pltpu.SemaphoreType.DMA((max(n_in, 1),)), pltpu.SemaphoreType.DMA((len(outs), SEMS))]
        + [pltpu.VMEM(shape, kind) for shape, kind in scratch],
        compiler_params=pltpu.CompilerParams(vmem_limit_bytes=VMEM_LIMIT),
        cost_estimate=pl.CostEstimate(flops=int(flops), bytes_accessed=0, transcendentals=0),
    )(*scalars, *operands)


def forward_kernel(me_ref, loads, stores, layer_ref, bias_ref):
    index, table, tokens, seg, norm, wq, wk, wv, wo = loads
    normed, q, k, v, mixed, lse, first, last = stores
    length = tokens.ref.shape[0]
    half = length // 2
    index_row = index()[...]
    rows_of = table()[...]
    tok_ref = tokens()
    fill_layer(layer_ref, index_row, rows_of, tok_ref)
    fill_bias(bias_ref, seg()[...])
    norm_ref = norm()
    step = 128
    for at in range(0, length, step):
        rows = slice(at, at + step)
        hat, _ = norm_hat(layer_ref[rows, :])
        normed.ref[rows, :] = (hat * norm_ref[0:1, :] + norm_ref[1:2, :]).astype(BF16)
    normed.send()
    left = normed.ref[...]
    for weight, out in ((wq, q), (wk, k), (wv, v)):
        out.ref[...] = dot_nn(left, weight()[...]).astype(BF16)
        out.send()
    attend(q.ref, k.ref, v.ref, bias_ref, mixed.ref, lse.ref)
    mixed.send()
    lse.send()
    wo_ref = wo()
    for at, out in ((0, first), (half, last)):
        out.ref[...] = dot_nn(mixed.ref[at : at + half, :], wo_ref[...]).astype(BF16)
        out.send()


def grad_out_kernel(me_ref, loads, stores):
    seg, cotangent, return_weight = loads
    gout, gact = stores
    items = item_rows(seg()[...])
    valid = dot_tn(items, jnp.ones((SEG_ROWS, LANES), BF16))
    cot_ref = cotangent()
    for at in range(0, D, LANES):
        cols = slice(at, at + LANES)
        gout.ref[:, cols] = (cot_ref[:, cols].astype(F32) * valid).astype(BF16)
    gout.send()
    weight = return_weight()[...]
    half = gact.ref.shape[0] // 2
    for at in (0, half):
        rows = slice(at, at + half)
        gact.ref[rows, :] = dot_nt(gout.ref[rows, :], weight)
        gact.send(rows)


def feed_kernel(row0, me_ref, loads, stores, pre_ref):
    index, table, tokens, sums, norm, hidden_weight, gact = loads
    second, act, gpre, part = stores
    length = tokens.ref.shape[0]
    index_row = index()[:, row0 : row0 + length]
    rows_of = table()[...]
    tok_ref = tokens()
    fill_layer(pre_ref, index_row, rows_of, tok_ref, sums())
    norm_ref = norm()
    step = 64
    for at in range(0, length, step):
        rows = slice(at, at + step)
        hat, _ = norm_hat(pre_ref[rows, :])
        second.ref[rows, :] = (hat * norm_ref[2:3, :] + norm_ref[3:4, :]).astype(BF16)
    second.send()
    weight_ref = hidden_weight()
    pre_ref[...] = dot_nn(second.ref[...], weight_ref[...])
    gact_ref = gact()
    step = 32

    @pl.loop(0, length // step)
    def _(i):
        rows = pl.ds(pl.multiple_of(i * step, step), step)
        value, slope = gelu_parts(pre_ref[rows, :])
        act.ref[rows, :] = value.astype(BF16)
        gpre.ref[rows, :] = (gact_ref[rows, :] * slope).astype(BF16)

    act.send()
    gpre.send()
    part.ref[...] = dot_nt(gpre.ref[...], weight_ref[...]).astype(BF16)
    part.send()


def store_blocks(nat_ref, base, left, right_ref, weight, unroll=False):
    width = right_ref.shape[1]
    across = width // BLK
    wide = 256

    @pl.loop(0, width // wide, unroll=unroll)
    def _(step):
        cols = pl.ds(pl.multiple_of(step * wide, wide), wide)
        grad = (dot_tn(left, right_ref[:, cols]) * weight).astype(BF16)
        for i in range(grad.shape[0] // BLK):
            for j in range(wide // BLK):
                nat_ref[base + i * across + step * (wide // BLK) + j] = grad[
                    i * BLK : (i + 1) * BLK, j * BLK : (j + 1) * BLK
                ]


def relative(order, bits):
    out = 0
    for i, bit in enumerate(bits):
        if (order >> (len(bits) - 1 - i)) & 1:
            out |= bit
    return out


def gather_blocks(me_ref, source_ref, positions, first, count, bits, keep_ref, send_ref, block_at):
    owners = 2 ** len(bits)
    for order in range(owners):
        dest = me_ref[0] ^ relative(order, bits)
        out_ref = keep_ref if order < owners // 2 else send_ref
        at = (order % (owners // 2)) * count

        @pl.loop(0, count)
        def _(j, out_ref=out_ref, at=at, place=dest * positions + first):
            out_ref[at + j] = block_at(source_ref[place + j])


def feed_grad_kernel(
    bits, early_slots, positions, late_count, me_ref, source_ref, scal_ref, loads, stores, nat_ref
):
    second, gpre, act, gout = loads
    rest = stores[0]
    weight = scal_ref[0]
    store_blocks(nat_ref, 0, second()[...], gpre(), weight, True)
    store_blocks(nat_ref, 64, act()[...], gout(), weight, True)

    def block_at(block):
        return nat_ref[jnp.maximum(block - late_count, 0)]

    if early_slots:
        keep, send = stores[1:]
        gather_blocks(
            me_ref, source_ref, positions, 0, early_slots, bits, keep.ref, send.ref, block_at
        )
        send.send()
        keep.send()

    @pl.loop(0, rest.ref.shape[0])
    def _(i):
        rest.ref[i] = block_at(source_ref[2 ** len(bits) * positions + i])

    rest.send()


def backward_kernel(
    chunks,
    first,
    positions,
    late_count,
    me_ref,
    source_ref,
    scal_ref,
    loads,
    stores,
    gattn_ref,
    gmix_ref,
    grads_ref,
    hid_ref,
    bias_ref,
):
    index, table, tokens, attn, norm, sums, gout = loads[:7]
    wo, seg, q, k, v, lse, normed, mixed, rest, qkv_weight, act, return_weight = loads[7:]
    late, parts = stores[:2]
    chunk_stores = stores[2:]
    length = tokens.ref.shape[0]
    half = length // 2
    width = q.ref.shape[1]
    weight = scal_ref[0]
    step = 64
    index_row, rows_of, tok_ref = index()[...], table()[...], tokens()
    fill_layer(hid_ref, index_row, rows_of, tok_ref, attn())
    norm_ref, gout_ref, sum_ref = norm(), gout(), sums()

    @pl.loop(0, length // step, unroll=2)
    def _(i):
        rows = pl.ds(pl.multiple_of(i * step, step), step)
        hat, inv_std = norm_hat(hid_ref[rows, :])
        grad = sum_ref[rows, :].astype(F32)
        value = gout_ref[rows, :].astype(F32) + norm_back(grad, hat, inv_std, norm_ref[2:3, :])
        gattn_ref[rows, :] = value.astype(BF16)

    fill_bias(bias_ref, seg()[...])
    gmix_ref[...] = dot_nt(gattn_ref[...], wo()[...]).astype(BF16)
    scale = 1.0 / math.sqrt(HEAD)
    q_ref, k_ref, v_ref, lse_ref = q(), k(), v(), lse()

    @pl.loop(0, q_ref.shape[1] // HEAD)
    def _(number):
        cols = head_columns(number)
        here = head_lanes(length, number % 2)
        keys, vals = k_ref[:, cols], v_ref[:, cols]
        query = q_ref[:, cols] * scale
        gmix = gmix_ref[:, cols]
        scores = dot_nt(jnp.where(here, query, 0.0).astype(BF16), keys) + bias_ref[...]
        probs = jnp.exp(scores - lane_of(lse_ref[...], number))
        grad_probs = dot_nt(jnp.where(here, gmix, 0.0).astype(BF16), vals)
        grad_scores = (
            probs * (grad_probs - jnp.sum(probs * grad_probs, axis=-1, keepdims=True))
        ).astype(BF16)
        for place, value in (
            (2, dot_tn(probs.astype(BF16), gmix)),
            (1, dot_tn(grad_scores, query)),
            (0, dot_nn(grad_scores, keys) * scale),
        ):
            old = grads_ref[place, :, cols]
            grads_ref[place, :, cols] = jnp.where(here, value.astype(BF16), old)

    weights_ref, act_ref, return_ref = qkv_weight(), act(), return_weight()

    @pl.loop(0, 2)
    def _(i):
        rows = pl.ds(pl.multiple_of(i * half, half), half)
        total = sum(
            dot_nt(grads_ref[place, rows, :], weights_ref[place * D : (place + 1) * D, :])
            for place in range(3)
        )
        parts.ref[pl.ds(pl.multiple_of(2 * i * half, half), half), :] = total.astype(BF16)
        parts.ref[pl.ds(pl.multiple_of((2 * i + 1) * half, half), half), :] = dot_nn(
            act_ref[rows, :], return_ref[...]
        ).astype(BF16)

    parts.send()
    pool_ref = rest.ref
    left = normed()[...]
    share = D // BLK * (width // BLK)

    @pl.loop(0, 3)
    def _(place):
        store_blocks(pool_ref, place * share, left, grads_ref.at[place], weight)

    store_blocks(pool_ref, 3 * share, mixed()[...], gattn_ref, weight)
    rest()
    for number, (count, bits) in enumerate(chunks):
        keep, send = chunk_stores[2 * number : 2 * number + 2]
        gather_blocks(
            me_ref,
            source_ref,
            positions,
            first,
            count,
            bits,
            keep.ref,
            send.ref,
            lambda place: pool_ref[place],
        )
        send.send()
        keep.send()
        first += count
    late.send_if(scal_ref[3] > 0.5, pool_ref.at[0:late_count])


def overflow_kernel(first, count, bits, positions, me_ref, source_ref, loads, stores):
    (late,) = loads
    keep, send = stores
    late_ref = late()
    last = late_ref.shape[0] - 1
    gather_blocks(
        me_ref,
        source_ref,
        positions,
        first,
        count,
        bits,
        keep.ref,
        send.ref,
        lambda place: late_ref[jnp.minimum(place, last)],
    )
    keep.send()
    send.send()


def add_rows(acc_ref, at, values):
    acc_ref[at : at + 8, :] += jnp.sum(values.reshape(values.shape[0] // 8, 8, D), axis=0)


def finish_kernel(me_ref, scal_ref, loads, stores, layer_ref, acc_ref):
    index, table, tokens, attn_a, attn_b, norm, outputs, second_a, second_b, gout = loads
    out, gin, sums = stores
    half = attn_a.ref.shape[0]
    weight = scal_ref[0]
    step = 64
    acc_ref[...] = jnp.zeros_like(acc_ref)
    index_row = index()[...]
    rows_of = table()[...]
    tok_ref = tokens()
    for row0, attn, second in ((0, attn_a, second_a), (half, attn_b, second_b)):
        part = slice(row0, row0 + half)
        fill_layer(layer_ref, index_row[:, part], rows_of, tok_ref.at[part, :])
        attn_ref, norm_ref, second_ref, gout_ref, both_ref = (
            attn(),
            norm(),
            second(),
            gout(),
            outputs(),
        )
        @pl.loop(0, half // step)
        def _(
            i,
            row0=row0,
            attn_ref=attn_ref,
            norm_ref=norm_ref,
            second_ref=second_ref,
            gout_ref=gout_ref,
            both_ref=both_ref,
        ):
            at = pl.multiple_of(i * step, step)
            here = pl.ds(at, step)
            rows = pl.ds(pl.multiple_of(row0 + at, step), step)
            first_at = pl.multiple_of(2 * row0 + at, step)
            layer = layer_ref[here, :]
            hat, inv_std = norm_hat(layer)
            hid = layer + attn_ref[here, :].astype(F32)
            mlp = both_ref[pl.ds(first_at + half, step), :].astype(F32)
            out.ref[rows, :] = hid + mlp
            hat2, inv_std2 = norm_hat(hid)
            grad2 = second_ref[here, :].astype(F32)
            ghid = gout_ref[rows, :].astype(F32) + norm_back(
                grad2, hat2, inv_std2, norm_ref[2:3, :]
            )
            add_rows(acc_ref, 16, grad2 * hat2)
            add_rows(acc_ref, 24, grad2)
            grad = both_ref[pl.ds(first_at, step), :].astype(F32)
            gin.ref[rows, :] = ghid + norm_back(grad, hat, inv_std, norm_ref[0:1, :])
            add_rows(acc_ref, 0, grad * hat)
            add_rows(acc_ref, 8, grad)

        out.send(part)
        gin.send(part)
    for i in range(4):
        sums.ref[i : i + 1, :] = (
            jnp.sum(acc_ref[8 * i : 8 * i + 8, :], axis=0, keepdims=True) * weight
        )
    sums.ref[4:5, :] = jnp.full((1, D), weight, F32)
    sums.ref[5:8, :] = jnp.zeros((3, D), F32)
    sums.send()


def columns(rows):
    count = rows.shape[0]
    if count % 8:
        return jnp.stack(
            [jnp.transpose(jnp.broadcast_to(rows[i : i + 1], (BLK, BLK)))[:, 0:1] for i in range(count)]
        )
    turned = jnp.transpose(rows)
    return jnp.stack([turned[:, i : i + 1] for i in range(count)])


def reflect(blocks, left, right, coef_left, coef_right):
    along = jnp.sum(left * blocks, axis=1, keepdims=True) * coef_left
    blocks = blocks - left * along
    across = jnp.sum(blocks * right, axis=2, keepdims=True) * coef_right
    return blocks - across * right


def reflectors(left_ref, right_ref):
    left, right = left_ref[...], right_ref[...]
    coef_left = (2.0 / jnp.sum(left * left, axis=1, keepdims=True))[:, :, None]
    coef_right = (2.0 / jnp.sum(right * right, axis=1, keepdims=True))[:, :, None]
    return (columns(left), right[:, None, :], coef_left, coef_right)


def rotate_kernel(counts, group, me_ref, place_ref, loads, stores, found_ref):
    left, right = loads[:2]
    grads, turned, total = stores
    parts = reflectors(left(), right())
    at = 0
    for number, count in enumerate(counts):
        keep, got = loads[2 + 2 * number : 4 + 2 * number]
        found_ref[at : at + count] = keep()[...].astype(F32) + got()[...].astype(F32)
        at += count
    slots = grads.ref.shape[0]
    for slot in range(slots):
        grads.ref[slot] = found_ref[place_ref[me_ref[0] * slots + slot]]
    grads.send()
    square = jnp.zeros((8, BLK), F32)
    for at in range(0, slots, group):
        rows = slice(at, at + group)
        grad = grads.ref[rows]
        square = square + jnp.sum((grad * grad).reshape(group * BLK // 8, 8, BLK), axis=0)
        turned.ref[rows] = reflect(grad, *(part[rows] for part in parts))
        turned.send(rows)
    total.ref[...] = jnp.full((8, BLK), jnp.sum(square), F32)
    total.send()


def inverse(value):
    guess = pl.reciprocal(value, approx=True)
    return guess * (2.0 - value * guess)


def update_kernel(group, me_ref, scal_ref, loads, stores):
    sums, norm, norm_first, norm_second, left, right = loads[:6]
    grads, turned_grads, old_first, old_second, old_master = loads[6:]
    out_grad, out_first, out_second, out_master, out_copy = stores[:5]
    norm_pair, norm_square, norm_value, clip_out = stores[5:]
    inv_one = 1.0 / scal_ref[1]
    inv_two = 1.0 / scal_ref[2]
    sums_ref = sums()
    share = 1.0 / sums_ref[4:5, 0:BLK]
    norm_grad = sums_ref[0:4, :] * share[:, 0:1]
    total = sums_ref[5:6, 0:BLK] * (share * share) + jnp.sum(norm_grad * norm_grad)
    clip_norm = jnp.sqrt(total)
    clip = jnp.minimum(1.0, clip_max / clip_norm)
    factor = (share * clip)[:, None, :]
    parts = reflectors(left(), right())
    slots = left.ref.shape[0]
    entries = 1.0 / (BLK * BLK)
    for at in range(0, slots, group):
        rows = slice(at, at + group)
        out_grad.ref[rows] = grads()[rows] * factor
        rotated = turned_grads()[rows] * factor
        first = beta_one * old_first()[rows] + (1.0 - beta_one) * rotated
        second = beta_two * old_second()[rows] + (1.0 - beta_two) * rotated * rotated
        out_first.ref[rows] = first
        out_second.ref[rows] = second
        spread = second * inv_two
        normal = (first * inv_one) * inverse(spread * lax.rsqrt(spread) + adam_eps)
        turned = reflect(normal, *(part[rows] for part in parts))
        master = old_master()[rows]
        size = jnp.sum(jnp.sum(master * master, axis=1, keepdims=True), axis=2, keepdims=True)
        move = jnp.sum(jnp.sum(turned * turned, axis=1, keepdims=True), axis=2, keepdims=True)
        trust = jnp.sqrt(size * entries + trust_eps) / jnp.sqrt(move * entries + trust_eps)
        fresh = master - (step_rate * trust) * turned
        out_master.ref[rows] = fresh
        out_copy.ref[rows] = fresh.astype(BF16)
        for out in (out_grad, out_first, out_second, out_master, out_copy):
            out.send(rows)
    clip_out.target[0, 0] = clip_norm[0, 0]
    clipped = norm_grad * clip[:, 0:1]
    first = beta_one * norm_first()[...] + (1.0 - beta_one) * clipped
    second = beta_two * norm_second()[...] + (1.0 - beta_two) * clipped * clipped
    norm_pair.ref[0] = clipped
    norm_pair.ref[1] = first
    norm_pair.send()
    norm_square.ref[...] = second
    norm_square.send()
    norm_value.ref[...] = norm()[...] - step_rate * (first * inv_one) / (
        jnp.sqrt(second * inv_two) + adam_eps
    )
    norm_value.send()


def swap(value, axis, bit):
    count = lax.axis_size(axis)
    return lax.ppermute(value, axis, [(i, i ^ bit) for i in range(count)])


def plus(left, right):
    return (left.astype(F32) + right.astype(F32)).astype(BF16)


def after(value, *others):
    return lax.optimization_barrier((value, *others))[0]


def mp_far(total, wait=None):
    bit = 2
    while bit < lax.axis_size("mp"):
        got = swap(total, "mp", bit)
        total = plus(total, got if wait is None else after(got, wait))
        bit *= 2
    return total


def mp_sum(keep, send):
    total = mp_far(plus(keep, swap(send, "mp", 1)))
    return (total, swap(total, "mp", 1))


def early_count(slots):
    return slots // 3 if slots >= 24 else 0


def split_counts(slots, bits):
    if slots >= 8:
        last = slots // 4
        head = (slots - last + 2) // 2
        return ((head, bits), (slots - last - head, bits), (last, (bits[1], bits[0]) + bits[2:]))
    return ((1, bits),) * slots if slots <= 3 else ((slots - slots // 2, bits), (slots // 2, bits))


def exclusive_sum(values):
    size = values.shape[-1]
    before = jnp.asarray(np.tril(np.ones((size, size), np.int32), -1))
    return jnp.sum(values[..., None, :] * before, axis=-1)


def rest_count(blocks, late_count, n_dp, slots, early_slots):
    total = blocks - late_count
    full, over = divmod(total, slots)
    return total - full * early_slots - min(over, early_slots)


def slot_tables(owner_list, n_dp, slots, early_slots, late_count):
    blocks = owner_list.shape[0]
    owned = owner_list.reshape(n_dp, slots)
    early = (owned >= late_count).astype(jnp.int32)
    if early_slots:
        goes = early * (exclusive_sum(early) < early_slots).astype(jnp.int32)
        place = jnp.where(goes == 1, exclusive_sum(early), early_slots + exclusive_sum(1 - goes))
        positions = slots + early_slots
        hit = place[:, None, :] == jnp.arange(positions, dtype=jnp.int32)[None, :, None]
        source = jnp.sum(jnp.where(hit, owned[:, None, :], 0), axis=2)
        short = jnp.any(jnp.sum(early, axis=1) < early_slots)
    else:
        place = jnp.broadcast_to(jnp.arange(slots, dtype=jnp.int32), (n_dp, slots))
        source, short = owned, jnp.zeros((), bool)
    later = source[:, early_slots:].reshape(-1)
    is_rest = (later >= late_count).astype(jnp.int32)
    order = exclusive_sum(is_rest)
    count = rest_count(blocks, late_count, n_dp, slots, early_slots)
    hit = (order[None, :] == jnp.arange(count, dtype=jnp.int32)[:, None]) & (is_rest[None, :] == 1)
    rest = jnp.sum(jnp.where(hit, later[None, :], 0), axis=1)
    later = jnp.where(is_rest == 1, late_count + order, later)
    source = jnp.concatenate([source[:, :early_slots], later.reshape(n_dp, -1)], axis=1)
    return (jnp.concatenate([source.reshape(-1), rest]), place.reshape(-1), short)


def shards(
    tokens,
    cotangent,
    segment_ids,
    table_index,
    group_count,
    owner_list,
    step_count,
    query_weight,
    key_weight,
    value_weight,
    output_weight,
    hidden_weight,
    return_weight,
    norm_params,
    norm_first,
    norm_second,
    master_blocks,
    first_moment,
    second_moment,
    left_vector,
    right_vector,
):
    length = tokens.shape[0]
    half = length // 2
    width = query_weight.shape[1]
    heads = width // HEAD
    units = hidden_weight.shape[1]
    slots = master_blocks.shape[0]
    blocks = owner_list.shape[0]
    late_count = blocks // 3
    n_dp = lax.axis_size("dp")
    natural = tuple(1 << i for i in range(n_dp.bit_length() - 1))
    early_slots = early_count(slots)
    positions = slots + early_slots
    me = jnp.stack([lax.axis_index("dp"), lax.axis_index("mp")]).astype(jnp.int32)
    step_value = step_count[0].astype(F32)
    source, place, short = slot_tables(owner_list, n_dp, slots, early_slots, late_count)
    scal = jnp.stack(
        [
            group_count[0].astype(F32),
            1.0 - jnp.power(beta_one, step_value),
            1.0 - jnp.power(beta_two, step_value),
            short.astype(F32),
        ]
    )
    seg_row = segment_ids.reshape(1, length)
    index_row = table_index.reshape(1, length)
    table = jnp.asarray(position_rows())
    rows_d = (length, D)
    half_d = (half, D)
    unit = 2 * length * D * D
    wide = ((length, width), BF16)

    normed, q, k, v, mixed, lse, keep_a, send_a, keep_b, send_b = call(
        forward_kernel,
        "attention_forward",
        (me,),
        (
            index_row,
            table,
            tokens,
            seg_row,
            norm_params,
            query_weight,
            key_weight,
            value_weight,
            output_weight,
        ),
        [
            (rows_d, BF16),
            wide,
            wide,
            wide,
            wide,
            ((length, heads), F32),
            (half_d, BF16, True),
            (half_d, BF16, True),
        ],
        [(rows_d, F32), ((length, length), F32)],
        flops=5 * unit,
    )
    near_a = plus(keep_a, swap(send_a, "mp", 1))
    near_b = plus(keep_b, swap(send_b, "mp", 1))
    token = near_b
    grad_out, grad_act = call(
        grad_out_kernel,
        "grad_of_act",
        (me,),
        (seg_row, cotangent, return_weight),
        [(rows_d, BF16), ((length, units), F32)],
        flops=2 * unit,
        after=token,
    )

    far_a = mp_far(near_a, grad_act)
    attn_a = Pair(far_a, swap(far_a, "mp", 1))
    def feed(row0, name, sums, token):
        return call(
            functools.partial(feed_kernel, row0),
            name,
            (me,),
            (
                index_row,
                table,
                Rows(tokens, row0, half),
                sums,
                norm_params,
                hidden_weight,
                Rows(grad_act, row0, half),
            ),
            [
                (half_d, BF16),
                ((half, units), BF16),
                ((half, units), BF16),
                (half_d, BF16, True),
            ],
            [((half, units), F32)],
            flops=4 * unit,
            after=token,
        )

    second_a, act_a, gpre_a, keep_a, send_a = feed(0, "feed_forward_a", attn_a, None)
    far_b = mp_far(near_b, keep_a)
    attn_b = Pair(far_b, swap(far_b, "mp", 1))
    second_b, act_b, gpre_b, keep_b, send_b = feed(half, "feed_forward_b", attn_b, keep_a)
    near_a = plus(keep_a, swap(send_a, "mp", 1))
    near_b = plus(keep_b, swap(send_b, "mp", 1))
    chunk_e = [((n_dp // 2 * early_slots, BLK, BLK), BF16)] * 2 if early_slots else []
    count = rest_count(blocks, late_count, n_dp, slots, early_slots)
    rest, *chunk_e = call(
        functools.partial(feed_grad_kernel, natural, early_slots, positions, late_count),
        "feed_weight_grads",
        (me, source, scal),
        (Stack(second_a, second_b), Stack(gpre_a, gpre_b), Stack(act_a, act_b), grad_out),
        [((count, BLK, BLK), BF16)] + chunk_e,
        [((blocks - late_count, BLK, BLK), BF16)],
        flops=4 * unit,
        after=near_b,
    )
    far_a = mp_far(near_a, rest)
    far_b = mp_far(near_b, far_a)
    sum_a = Pair(far_a, swap(far_a, "mp", 1))
    sum_b = Pair(far_b, swap(far_b, "mp", 1))
    got_e = swap(chunk_e[1], "dp", 1) if early_slots else None
    chunks = split_counts(slots - early_slots, natural)
    chunk_shapes = []
    for count, _ in chunks:
        chunk_shapes += [((n_dp // 2 * count, BLK, BLK), BF16)] * 2
    outs = call(
        functools.partial(backward_kernel, chunks, early_slots, positions, late_count),
        "attention_backward",
        (me, source, scal),
        (
            index_row,
            table,
            tokens,
            Stack(attn_a, attn_b),
            norm_params,
            Stack(sum_a, sum_b),
            grad_out,
            output_weight,
            seg_row,
            q,
            k,
            v,
            lse,
            normed,
            mixed,
            Into(rest, late_count),
            Stack(query_weight, key_weight, value_weight),
            Stack(act_a, act_b),
            return_weight,
        ),
        [((late_count, BLK, BLK), BF16), ((2 * length, D), BF16, True)] + chunk_shapes,
        [(rows_d, BF16)]
        + [((length, width), BF16), ((3, length, width), BF16)]
        + [(rows_d, F32), ((length, length), F32)],
        flops=10 * unit,
    )
    late, keep, send = outs[:3]
    queue = [(outs[3 + 2 * i], outs[4 + 2 * i]) for i in range(len(chunks))]
    counts = [count for count, _ in chunks]
    orders = [bits for _, bits in chunks]

    stages = len(natural)
    state = [(first, swap(second, "dp", bits[0])) for (first, second), bits in zip(queue, orders)]
    if early_slots:
        state.insert(0, (chunk_e[0], after(got_e, keep)))
        counts.insert(0, early_slots)
        orders.insert(0, natural)
    level = [0] * len(state)
    last = []

    def in_turn(got):
        got = after(got, *last)
        last[:] = [got]
        return got

    def halve(number):
        keep, got = state[number]
        got = in_turn(got)
        if level[number] < stages - 1:
            n = keep.shape[0] // 2
            keep, send = plus(keep[:n], got[:n]), plus(keep[n:], got[n:])
            got = swap(send, "dp", orders[number][level[number] + 1])
            last.append(send)
        level[number] += 1
        state[number] = (keep, got)

    def mp_first(keep, send):
        return plus(keep, in_turn(swap(send, "mp", 1)))

    def mp_rest(near):
        bit = 2
        while bit < lax.axis_size("mp"):
            near = plus(near, in_turn(swap(near, "mp", bit)))
            bit *= 2
        return Pair(near, swap(near, "mp", 1))

    if early_slots:
        halve(0)
    def finish(both):
        outputs = call(
            finish_kernel,
            "layer_outputs",
            (me, scal),
            (
                index_row,
                table,
                tokens,
                attn_a,
                attn_b,
                norm_params,
                both,
                sum_a,
                sum_b,
                grad_out,
            ),
            [(rows_d, F32), (rows_d, F32), ((8, D), F32)],
            [(half_d, F32), ((32, D), F32)],
            flops=2 * unit,
        )
        last.append(outputs[2])
        return outputs

    overflow, early_done = [], []
    if early_slots:
        shape = (n_dp // 2 * early_slots, BLK, BLK)

        def exchange(late):
            keep, send = call(
                functools.partial(overflow_kernel, slots, early_slots, natural, positions),
                "overflow",
                (me, source),
                (late,),
                [(shape, BF16), (shape, BF16)],
            )
            bit = 1
            while True:
                got = swap(send, "dp", bit)
                bit *= 2
                if bit >= n_dp:
                    return (keep, got)
                n = keep.shape[0] // 2
                keep, send = plus(keep[:n], got[:n]), plus(keep[n:], got[n:])

        def nothing(late):
            zero = jnp.zeros((early_slots, BLK, BLK), BF16)
            return (zero, zero)

        overflow = list(lax.cond(short, exchange, nothing, late))
        early_done = [overflow[0], place]

    plan = ["near", "far", "finish"]
    if early_slots and stages == 3:
        plan = ["near",(3,0),(1,0),(0,1),(2,0),(1,1),(3,1),(0,2),(2,1),(1,2),"far","finish"]
    plan += [(i, d - i) for d in range(len(state) + stages) for i in range(len(state))]
    for entry in plan:
        if entry == "near":
            near = plus(keep, in_turn(swap(send, "mp", 1)))
            last += early_done
        elif entry == "far":
            bit = 2
            while bit < lax.axis_size("mp"):
                near = plus(near, in_turn(swap(near, "mp", bit)))
                bit *= 2
            both = Pair(near, swap(near, "mp", 1))
        elif entry == "finish":
            out, input_grad, sums = finish(both)
        elif level[entry[0]] == entry[1] < stages:
            halve(entry[0])
    pending = [array for pair in state for array in pair]

    pending += overflow
    counts += [early_slots] if early_slots else []
    left = left_vector.reshape(slots, BLK)
    right = right_vector.reshape(slots, BLK)
    block_f32 = ((slots, BLK, BLK), F32)
    group = 4 if slots % 4 == 0 else 1
    grads, rotated, square = call(
        functools.partial(rotate_kernel, counts, group),
        "rotate",
        (me, place),
        (left, right, *pending),
        [block_f32, block_f32, ((8, BLK), F32)],
        [((sum(counts), BLK, BLK), F32)],
        flops=unit,
    )
    bit = 1
    while bit < lax.axis_size("mp"):
        square = square + swap(square, "mp", bit)
        bit *= 2
    sums = sums + jnp.pad(square[0:1], ((5, 2), (0, D - BLK)))
    bit = 1
    while bit < n_dp:
        sums = sums + swap(sums, "dp", bit)
        bit *= 2
    new = call(
        functools.partial(update_kernel, group),
        "update",
        (me, scal),
        (
            sums,
            norm_params,
            norm_first,
            norm_second,
            left,
            right,
            grads,
            rotated,
            first_moment.reshape(slots, BLK, BLK),
            second_moment.reshape(slots, BLK, BLK),
            master_blocks.reshape(slots, BLK, BLK),
        ),
        [block_f32] * 4
        + [
            ((slots, BLK, BLK), BF16),
            ((2, 4, D), F32),
            ((4, D), F32),
            ((4, D), F32),
            ((1, 1), F32),
        ],
        flops=unit,
    )
    shard_shape = (slots, 1, BLK, BLK)
    return (
        out,
        input_grad,
        new[0].reshape(shard_shape),
        new[1].reshape(shard_shape),
        new[2].reshape(shard_shape),
        new[3].reshape(shard_shape),
        new[4].reshape(shard_shape),
        new[5],
        new[6],
        new[7],
        new[8].reshape(()),
    )


def solution(mesh):
    placed = (
        P("dp", None),
        P("dp", None),
        P("dp"),
        P("dp"),
        P("dp"),
        P(),
        P(),
        P(None, "mp"),
        P(None, "mp"),
        P(None, "mp"),
        P("mp", None),
        P(None, "mp"),
        P("mp", None),
        P(),
        P(),
        P(),
        P("dp", "mp", None, None),
        P("dp", "mp", None, None),
        P("dp", "mp", None, None),
        P("dp", "mp", None),
        P("dp", "mp", None),
    )
    return jax.shard_map(
        shards,
        mesh=mesh,
        in_specs=placed,
        out_specs=(
            P("dp", None),
            P("dp", None),
            P("dp", "mp", None, None),
            P("dp", "mp", None, None),
            P("dp", "mp", None, None),
            P("dp", "mp", None, None),
            P("dp", "mp", None, None),
            P(),
            P(),
            P(),
            P(),
        ),
        check_vma=False,
    )
```

```python
import functools
import math

import jax
import jax.numpy as jnp
import numpy as np
from jax import lax
from jax.experimental import pallas as pl
from jax.experimental.pallas import tpu as pltpu
from jax.sharding import PartitionSpec as P

D = 1024
HEAD = 64
BLK = 128
LANES = 128
POS_ROWS = 64
SEG_ROWS = 32

clip_max = 1.0
beta_one = 0.5
beta_two = 0.5
adam_eps = 1e-08
step_rate = 0.25
norm_eps = 1e-06
trust_eps = 1e-06

F32 = jnp.float32
BF16 = jnp.bfloat16
MIB = 1024 * 1024
VMEM_LIMIT = 60 * MIB

ERF_P = 0.425
ERF_COEF = (
    0.11983931305209315,
    0.12092032287702306,
    0.10035292560006456,
    0.12754356284084392,
    -0.051626023300101125,
    0.20380940869554587,
    -0.1565787944569494,
    0.035739213095996265,
)


def position_rows():
    coords = np.concatenate(
        [1.75 * np.arange(8), 1.0 * np.arange(14), 0.5 * np.arange(28), np.zeros(POS_ROWS - 50)]
    )
    quarter = D // 4
    freqs = np.power(np.float32(10000.0), -np.arange(quarter, dtype=np.float32) / np.float32(quarter))
    args = (coords.astype(np.float32)[:, None] * freqs.astype(np.float32)[None, :]).astype(np.float64)
    table = np.concatenate([np.sin(args), np.cos(args)], axis=1).astype(np.float32)
    parts = []
    rest = table
    for _ in range(3):
        part = rest.astype(jnp.bfloat16)
        parts.append(part)
        rest = rest - part.astype(np.float32)
    return np.concatenate(parts, axis=0)


def dot_nn(left, right):
    return lax.dot_general(left, right, (((1,), (0,)), ((), ())), preferred_element_type=F32)


def dot_nt(left, right):
    return lax.dot_general(left, right, (((1,), (1,)), ((), ())), preferred_element_type=F32)


def dot_tn(left, right):
    return lax.dot_general(left, right, (((0,), (0,)), ((), ())), preferred_element_type=F32)


def norm_hat(values):
    center = values - jnp.mean(values, axis=-1, keepdims=True)
    inv_std = lax.rsqrt(jnp.mean(center * center, axis=-1, keepdims=True) + norm_eps)
    return (center * inv_std, inv_std)


def norm_back(grad_out, normal, inv_std, gain):
    scaled = grad_out * gain
    return inv_std * (
        scaled
        - jnp.mean(scaled, axis=-1, keepdims=True)
        - normal * jnp.mean(scaled * normal, axis=-1, keepdims=True)
    )


def gelu_parts(values):
    bell = jnp.exp(-0.5 * values * values)
    t = 1.0 / (1.0 + (ERF_P / math.sqrt(2.0)) * jnp.abs(values))
    poly = ERF_COEF[-1]
    for coef in ERF_COEF[-2::-1]:
        poly = poly * t + coef
    tail = poly * t * bell
    dist = jnp.where(values >= 0.0, 1.0 - tail, tail)
    return (values * dist, dist + values * ((1.0 / math.sqrt(2.0 * math.pi)) * bell))


def item_rows(seg_row):
    rows = lax.broadcasted_iota(jnp.int32, (SEG_ROWS, seg_row.shape[1]), 0)
    return jnp.where(rows == seg_row, 1.0, 0.0).astype(BF16)


def head_lanes(rows, head):
    lanes = lax.broadcasted_iota(jnp.int32, (rows, LANES), 1)
    return (lanes // HEAD) == head


def position_hots(index):
    length = index.shape[1]
    big = index >= 260
    mid = index >= 64
    offset = jnp.where(big, 260, jnp.where(mid, 64, 0))
    base = jnp.where(big, 22, jnp.where(mid, 8, 0))
    side = jnp.where(big, 28, jnp.where(mid, 14, 8))
    inv_side = jnp.where(big, 1.0 / 28.0, jnp.where(mid, 1.0 / 14.0, 1.0 / 8.0)).astype(F32)
    local = index - offset
    row = jnp.floor((local.astype(F32) + 0.5) * inv_side).astype(jnp.int32)
    col = local - row * side
    rows = lax.broadcasted_iota(jnp.int32, (3 * POS_ROWS, length), 0) & (POS_ROWS - 1)
    row_hot = jnp.where(rows == base + row, 1.0, 0.0).astype(BF16)
    col_hot = jnp.where(rows == base + col, 1.0, 0.0).astype(BF16)
    return (row_hot, col_hot)


def fill_layer(out_ref, index_row, table, tok_ref, sum_ref=None):
    half = D // 2
    for hot, cols in zip(position_hots(index_row), (slice(0, half), slice(half, D))):
        value = dot_tn(hot, table) + tok_ref[:, cols].astype(F32)
        if sum_ref is not None:
            value = value + sum_ref[:, cols].astype(F32)
        out_ref[:, cols] = value


def fill_bias(bias_ref, seg_row):
    length = seg_row.shape[1]
    items = item_rows(seg_row)
    same = dot_tn(items, items)
    diag = lax.broadcasted_iota(jnp.int32, (length, length), 0) == lax.broadcasted_iota(
        jnp.int32, (length, length), 1
    )
    bias_ref[...] = jnp.where((same > 0.5) | diag, 0.0, -1e30)


def lane_of(values, number):
    lanes = lax.broadcasted_iota(jnp.int32, values.shape, 1)
    return jnp.sum(jnp.where(lanes == number, values, 0.0), axis=1, keepdims=True)


def head_columns(number):
    return pl.ds(pl.multiple_of((number // 2) * LANES, LANES), LANES)


def attend(q_ref, k_ref, v_ref, bias_ref, mixed_ref, lse_ref):
    count = q_ref.shape[0]
    scale = 1.0 / math.sqrt(HEAD)
    step = 512
    for pair in range(q_ref.shape[1] // LANES):
        cols = slice(pair * LANES, (pair + 1) * LANES)
        keys = k_ref[:, cols]
        vals = v_ref[:, cols]
        for at in range(0, count, step):
            rows = slice(at, at + step)
            query = q_ref[rows, cols] * scale
            outs = []
            for head in range(2):
                here = head_lanes(step, head)
                scores = dot_nt(jnp.where(here, query, 0.0).astype(BF16), keys) + bias_ref[rows, :]
                peak = jnp.max(scores, axis=-1, keepdims=True)
                expon = jnp.exp(scores - peak)
                total = jnp.sum(expon, axis=-1, keepdims=True)
                outs.append(dot_nn(expon.astype(BF16), vals) * (1.0 / total))
                number = pair * 2 + head
                lse_ref[rows, number : number + 1] = peak + jnp.log(total)
            mixed_ref[rows, cols] = jnp.where(
                head_lanes(step, 0), outs[0], outs[1]
            ).astype(BF16)


class Load:
    def __init__(self, ref):
        self.ref = ref
        self.copies = []

    def __call__(self):
        for copy in self.copies:
            copy.wait()
        self.copies = []
        return self.ref


class Store:
    def __init__(self, ref, target, sem, running):
        self.ref = ref
        self.target = target
        self.sem = sem
        self.running = running
        self.sent = 0

    def send(self, rows=None):
        source = self.ref if rows is None else self.ref.at[rows]
        target = self.target if rows is None else self.target.at[rows]
        copy = pltpu.make_async_copy(source, target, self.sem.at[self.sent])
        copy.start()
        self.sent += 1
        self.running.append(copy)


    def send_if(self, flag, source):
        @pl.when(flag)
        def _():
            copy = pltpu.make_async_copy(source, self.target, self.sem.at[0])
            copy.start()
            copy.wait()


class Split:
    def __init__(self, ref, keep, send, sem, running, bit):
        self.ref = ref
        self.targets = ((send, 1 - bit), (keep, bit))
        self.sem = sem
        self.running = running

    def send(self):
        half = self.ref.shape[0] // 2
        for i, (target, which) in enumerate(self.targets):
            rows = pl.ds(pl.multiple_of(which * half, half), half)
            copy = pltpu.make_async_copy(self.ref.at[rows], target, self.sem.at[i])
            copy.start()
            self.running.append(copy)


class Rows:
    def __init__(self, array, first, count):
        self.array = array
        self.first = first
        self.count = count


class Into:
    def __init__(self, array, first):
        self.array = array
        self.first = first


class Pair:
    def __init__(self, own, other, first=0, count=None):
        self.own = own
        self.other = other
        self.first = first
        self.count = own.shape[0] if count is None else count


class Stack:
    def __init__(self, *parts):
        self.parts = parts


SEMS = 24


def row_moves(entry, sources, ref, first, bit):
    if isinstance(entry, Stack):
        moves = []
        for part in entry.parts:
            more, first = row_moves(part, sources, ref, first, bit)
            moves += more
        return (moves, first)
    if isinstance(entry, Pair):
        moves = []
        for which in (bit, 1 - bit):
            rows = pl.ds(pl.multiple_of(first + which * entry.count, entry.count), entry.count)
            part = sources.pop(0).at[entry.first : entry.first + entry.count]
            moves.append((part, ref.at[rows]))
        return (moves, first + 2 * entry.count)
    count = entry.count if isinstance(entry, Rows) else entry.shape[0]
    source = sources.pop(0)
    if isinstance(entry, Rows):
        source = source.at[entry.first : entry.first + count]
    whole = count == ref.shape[0]
    return ([(source, ref if whole else ref.at[first : first + count])], first + count)


def flat(entry):
    if isinstance(entry, Stack):
        parts = [flat(part) for part in entry.parts]
        return (sum((p[0] for p in parts), []), sum(p[1] for p in parts), parts[0][2])
    if isinstance(entry, Pair):
        return ([entry.own, entry.other], 2 * entry.count, entry.own)
    if isinstance(entry, Rows):
        return ([entry.array], entry.count, entry.array)
    if isinstance(entry, Into):
        return ([entry.array], entry.first + entry.array.shape[0], entry.array)
    return ([entry], entry.shape[0], entry)


def call(kernel, name, scalars, ins, outs, scratch=(), flops=0, after=None, limit=VMEM_LIMIT):
    operands = []
    shapes = []
    for entry in ins:
        arrays, rows, like = flat(entry)
        operands += arrays
        shapes.append(((rows,) + like.shape[1:], like.dtype))
    if after is not None:
        operands.append(after)
    results = []
    for shape, kind, *split in outs:
        if split:
            results += [jax.ShapeDtypeStruct((shape[0] // 2,) + shape[1:], kind)] * 2
        else:
            results.append(jax.ShapeDtypeStruct(shape, kind))
    n_scalar, n_in, n_out = len(scalars), len(operands), len(results)

    def body(*refs):
        smem_refs = refs[:n_scalar]
        sources = list(refs[n_scalar : n_scalar + n_in])
        targets = list(refs[n_scalar + n_in : n_scalar + n_in + n_out])
        rest = list(refs[n_scalar + n_in + n_out :])
        in_refs, rest = rest[: len(ins)], rest[len(ins) :]
        out_refs, rest = rest[: len(outs)], rest[len(outs) :]
        in_sem, out_sem = rest[:2]
        bit = smem_refs[0][1] & 1
        loads = []
        number = 0
        for entry, ref in zip(ins, in_refs):
            load = Load(ref)
            if isinstance(entry, Into):
                moves = [(sources.pop(0), ref.at[entry.first : ref.shape[0]])]
            else:
                moves, _ = row_moves(entry, sources, ref, 0, bit)
            for source, target in moves:
                copy = pltpu.make_async_copy(source, target, in_sem.at[number])
                copy.start()
                load.copies.append(copy)
                number += 1
            loads.append(load)
        running = []
        stores = []
        for i, (entry, ref) in enumerate(zip(outs, out_refs)):
            if len(entry) > 2:
                keep, send = targets.pop(0), targets.pop(0)
                stores.append(Split(ref, keep, send, out_sem.at[i], running, bit))
            else:
                stores.append(Store(ref, targets.pop(0), out_sem.at[i], running))
        kernel(*smem_refs, loads, stores, *rest[2:])
        for load in loads:
            load()
        for copy in running:
            copy.wait()

    hbm = pl.BlockSpec(memory_space=pltpu.HBM)
    scalar = pl.BlockSpec(memory_space=pltpu.SMEM)
    return pl.pallas_call(
        body,
        name=name,
        out_shape=results,
        in_specs=[pl.BlockSpec(memory_space=pltpu.SMEM)] * n_scalar + [hbm] * n_in,
        out_specs=[scalar if r.shape == (1, 1) else hbm for r in results],
        scratch_shapes=[pltpu.VMEM(shape, kind) for shape, kind in shapes]
        + [pltpu.VMEM(shape, kind) for shape, kind, *_ in outs]
        + [pltpu.SemaphoreType.DMA((max(n_in, 1),)), pltpu.SemaphoreType.DMA((len(outs), SEMS))]
        + [pltpu.VMEM(shape, kind) for shape, kind in scratch],
        compiler_params=pltpu.CompilerParams(vmem_limit_bytes=limit),
        cost_estimate=pl.CostEstimate(flops=int(flops), bytes_accessed=0, transcendentals=0),
    )(*scalars, *operands)


def forward_kernel(me_ref, loads, stores, layer_ref, bias_ref):
    index, table, tokens, seg, norm, wq, wk, wv, wo = loads
    normed, q, k, v, mixed, lse, first, last = stores
    length = tokens.ref.shape[0]
    half = length // 2
    index_row = index()[...]
    rows_of = table()[...]
    tok_ref = tokens()
    fill_layer(layer_ref, index_row, rows_of, tok_ref)
    fill_bias(bias_ref, seg()[...])
    norm_ref = norm()
    step = 128
    for at in range(0, length, step):
        rows = slice(at, at + step)
        hat, _ = norm_hat(layer_ref[rows, :])
        normed.ref[rows, :] = (hat * norm_ref[0:1, :] + norm_ref[1:2, :]).astype(BF16)
    normed.send()
    left = normed.ref[...]
    for weight, out in ((wq, q), (wk, k), (wv, v)):
        out.ref[...] = dot_nn(left, weight()[...]).astype(BF16)
        out.send()
    attend(q.ref, k.ref, v.ref, bias_ref, mixed.ref, lse.ref)
    mixed.send()
    lse.send()
    wo_ref = wo()
    for at, out in ((0, first), (half, last)):
        out.ref[...] = dot_nn(mixed.ref[at : at + half, :], wo_ref[...]).astype(BF16)
        out.send()


def grad_out_kernel(me_ref, loads, stores):
    seg, cotangent, return_weight = loads
    gout, gact = stores
    items = item_rows(seg()[...])
    valid = dot_tn(items, jnp.ones((SEG_ROWS, LANES), BF16))
    cot_ref = cotangent()
    for at in range(0, D, LANES):
        cols = slice(at, at + LANES)
        gout.ref[:, cols] = (cot_ref[:, cols].astype(F32) * valid).astype(BF16)
    gout.send()
    weight = return_weight()[...]
    half = gact.ref.shape[0] // 2
    for at in (0, half):
        rows = slice(at, at + half)
        gact.ref[rows, :] = dot_nt(gout.ref[rows, :], weight)
        gact.send(rows)


def feed_kernel(row0, me_ref, loads, stores, pre_ref):
    index, table, tokens, sums, norm, hidden_weight, gact = loads
    second, act, gpre, part = stores
    length = tokens.ref.shape[0]
    index_row = index()[:, row0 : row0 + length]
    rows_of = table()[...]
    tok_ref = tokens()
    fill_layer(pre_ref, index_row, rows_of, tok_ref, sums())
    norm_ref = norm()
    step = 64
    for at in range(0, length, step):
        rows = slice(at, at + step)
        hat, _ = norm_hat(pre_ref[rows, :])
        second.ref[rows, :] = (hat * norm_ref[2:3, :] + norm_ref[3:4, :]).astype(BF16)
    second.send()
    weight_ref = hidden_weight()
    pre_ref[...] = dot_nn(second.ref[...], weight_ref[...])
    gact_ref = gact()
    step = 32

    @pl.loop(0, length // step)
    def _(i):
        rows = pl.ds(pl.multiple_of(i * step, step), step)
        value, slope = gelu_parts(pre_ref[rows, :])
        act.ref[rows, :] = value.astype(BF16)
        gpre.ref[rows, :] = (gact_ref[rows, :] * slope).astype(BF16)

    act.send()
    gpre.send()
    part.ref[...] = dot_nt(gpre.ref[...], weight_ref[...]).astype(BF16)
    part.send()


def store_blocks(nat_ref, base, left, right_ref, weight, unroll=False):
    width = right_ref.shape[1]
    across = width // BLK
    wide = 256

    @pl.loop(0, width // wide, unroll=unroll)
    def _(step):
        cols = pl.ds(pl.multiple_of(step * wide, wide), wide)
        grad = (dot_tn(left, right_ref[:, cols]) * weight).astype(BF16)
        for i in range(grad.shape[0] // BLK):
            for j in range(wide // BLK):
                nat_ref[base + i * across + step * (wide // BLK) + j] = grad[
                    i * BLK : (i + 1) * BLK, j * BLK : (j + 1) * BLK
                ]


def relative(order, bits):
    out = 0
    for i, bit in enumerate(bits):
        if (order >> (len(bits) - 1 - i)) & 1:
            out |= bit
    return out


def gather_blocks(me_ref, source_ref, positions, first, count, bits, keep_ref, send_ref, block_at):
    owners = 2 ** len(bits)
    for order in range(owners):
        dest = me_ref[0] ^ relative(order, bits)
        out_ref = keep_ref if order < owners // 2 else send_ref
        at = (order % (owners // 2)) * count

        @pl.loop(0, count)
        def _(j, out_ref=out_ref, at=at, place=dest * positions + first):
            out_ref[at + j] = block_at(source_ref[place + j])


def feed_grad_kernel(
    bits, early_slots, positions, late_count, me_ref, source_ref, scal_ref, loads, stores, nat_ref
):
    second, gpre, act, gout = loads
    rest = stores[0]
    weight = scal_ref[0]
    store_blocks(nat_ref, 0, second()[...], gpre(), weight, True)
    store_blocks(nat_ref, 64, act()[...], gout(), weight, True)

    def block_at(block):
        return nat_ref[jnp.maximum(block - late_count, 0)]

    if early_slots:
        keep, send = stores[1:]
        gather_blocks(
            me_ref, source_ref, positions, 0, early_slots, bits, keep.ref, send.ref, block_at
        )
        send.send()
        keep.send()

    @pl.loop(0, rest.ref.shape[0])
    def _(i):
        rest.ref[i] = block_at(source_ref[2 ** len(bits) * positions + i])

    rest.send()


def backward_kernel(
    chunks,
    first,
    positions,
    late_count,
    me_ref,
    source_ref,
    scal_ref,
    loads,
    stores,
    gattn_ref,
    gmix_ref,
    grads_ref,
    hid_ref,
    bias_ref,
):
    index, table, tokens, attn, norm, sums, gout = loads[:7]
    wo, seg, q, k, v, lse, normed, mixed, rest, qkv_weight, act, return_weight = loads[7:]
    late, parts = stores[:2]
    chunk_stores = stores[2:]
    length = tokens.ref.shape[0]
    half = length // 2
    width = q.ref.shape[1]
    weight = scal_ref[0]
    step = 64
    index_row, rows_of, tok_ref = index()[...], table()[...], tokens()
    fill_layer(hid_ref, index_row, rows_of, tok_ref, attn())
    norm_ref, gout_ref, sum_ref = norm(), gout(), sums()

    @pl.loop(0, length // step, unroll=2)
    def _(i):
        rows = pl.ds(pl.multiple_of(i * step, step), step)
        hat, inv_std = norm_hat(hid_ref[rows, :])
        grad = sum_ref[rows, :].astype(F32)
        value = gout_ref[rows, :].astype(F32) + norm_back(grad, hat, inv_std, norm_ref[2:3, :])
        gattn_ref[rows, :] = value.astype(BF16)

    fill_bias(bias_ref, seg()[...])
    gmix_ref[...] = dot_nt(gattn_ref[...], wo()[...]).astype(BF16)
    scale = 1.0 / math.sqrt(HEAD)
    q_ref, k_ref, v_ref, lse_ref = q(), k(), v(), lse()

    @pl.loop(0, q_ref.shape[1] // HEAD)
    def _(number):
        cols = head_columns(number)
        here = head_lanes(length, number % 2)
        keys, vals = k_ref[:, cols], v_ref[:, cols]
        query = q_ref[:, cols] * scale
        gmix = gmix_ref[:, cols]
        scores = dot_nt(jnp.where(here, query, 0.0).astype(BF16), keys) + bias_ref[...]
        probs = jnp.exp(scores - lane_of(lse_ref[...], number))
        grad_probs = dot_nt(jnp.where(here, gmix, 0.0).astype(BF16), vals)
        grad_scores = (
            probs * (grad_probs - jnp.sum(probs * grad_probs, axis=-1, keepdims=True))
        ).astype(BF16)
        for place, value in (
            (2, dot_tn(probs.astype(BF16), gmix)),
            (1, dot_tn(grad_scores, query)),
            (0, dot_nn(grad_scores, keys) * scale),
        ):
            old = grads_ref[place, :, cols]
            grads_ref[place, :, cols] = jnp.where(here, value.astype(BF16), old)

    weights_ref, act_ref, return_ref = qkv_weight(), act(), return_weight()

    @pl.loop(0, 2)
    def _(i):
        rows = pl.ds(pl.multiple_of(i * half, half), half)
        total = sum(
            dot_nt(grads_ref[place, rows, :], weights_ref[place * D : (place + 1) * D, :])
            for place in range(3)
        )
        parts.ref[pl.ds(pl.multiple_of(2 * i * half, half), half), :] = total.astype(BF16)
        parts.ref[pl.ds(pl.multiple_of((2 * i + 1) * half, half), half), :] = dot_nn(
            act_ref[rows, :], return_ref[...]
        ).astype(BF16)

    parts.send()
    pool_ref = rest.ref
    left = normed()[...]
    share = D // BLK * (width // BLK)

    @pl.loop(0, 3)
    def _(place):
        store_blocks(pool_ref, place * share, left, grads_ref.at[place], weight)

    store_blocks(pool_ref, 3 * share, mixed()[...], gattn_ref, weight)
    rest()
    for number, (count, bits) in enumerate(chunks):
        keep, send = chunk_stores[2 * number : 2 * number + 2]
        gather_blocks(
            me_ref,
            source_ref,
            positions,
            first,
            count,
            bits,
            keep.ref,
            send.ref,
            lambda place: pool_ref[place],
        )
        send.send()
        keep.send()
        first += count
    late.send_if(scal_ref[3] > 0.5, pool_ref.at[0:late_count])


def overflow_kernel(first, count, bits, positions, me_ref, source_ref, loads, stores):
    (late,) = loads
    keep, send = stores
    late_ref = late()
    last = late_ref.shape[0] - 1
    gather_blocks(
        me_ref,
        source_ref,
        positions,
        first,
        count,
        bits,
        keep.ref,
        send.ref,
        lambda place: late_ref[jnp.minimum(place, last)],
    )
    keep.send()
    send.send()


def add_rows(acc_ref, at, values):
    acc_ref[at : at + 8, :] += jnp.sum(values.reshape(values.shape[0] // 8, 8, D), axis=0)


def finish_kernel(me_ref, scal_ref, loads, stores, layer_ref, acc_ref):
    index, table, tokens, attn_a, attn_b, norm, outputs, second_a, second_b, gout = loads
    out, gin, sums = stores
    half = attn_a.ref.shape[0]
    weight = scal_ref[0]
    step = 64
    acc_ref[...] = jnp.zeros_like(acc_ref)
    index_row = index()[...]
    rows_of = table()[...]
    tok_ref = tokens()
    for row0, attn, second in ((0, attn_a, second_a), (half, attn_b, second_b)):
        part = slice(row0, row0 + half)
        fill_layer(layer_ref, index_row[:, part], rows_of, tok_ref.at[part, :])
        attn_ref, norm_ref, second_ref, gout_ref, both_ref = (
            attn(),
            norm(),
            second(),
            gout(),
            outputs(),
        )
        @pl.loop(0, half // step)
        def _(
            i,
            row0=row0,
            attn_ref=attn_ref,
            norm_ref=norm_ref,
            second_ref=second_ref,
            gout_ref=gout_ref,
            both_ref=both_ref,
        ):
            at = pl.multiple_of(i * step, step)
            here = pl.ds(at, step)
            rows = pl.ds(pl.multiple_of(row0 + at, step), step)
            first_at = pl.multiple_of(2 * row0 + at, step)
            layer = layer_ref[here, :]
            hat, inv_std = norm_hat(layer)
            hid = layer + attn_ref[here, :].astype(F32)
            mlp = both_ref[pl.ds(first_at + half, step), :].astype(F32)
            out.ref[rows, :] = hid + mlp
            hat2, inv_std2 = norm_hat(hid)
            grad2 = second_ref[here, :].astype(F32)
            ghid = gout_ref[rows, :].astype(F32) + norm_back(
                grad2, hat2, inv_std2, norm_ref[2:3, :]
            )
            add_rows(acc_ref, 16, grad2 * hat2)
            add_rows(acc_ref, 24, grad2)
            grad = both_ref[pl.ds(first_at, step), :].astype(F32)
            gin.ref[rows, :] = ghid + norm_back(grad, hat, inv_std, norm_ref[0:1, :])
            add_rows(acc_ref, 0, grad * hat)
            add_rows(acc_ref, 8, grad)

        out.send(part)
        gin.send(part)
    for i in range(4):
        sums.ref[i : i + 1, :] = (
            jnp.sum(acc_ref[8 * i : 8 * i + 8, :], axis=0, keepdims=True) * weight
        )
    sums.ref[4:5, :] = jnp.full((1, D), weight, F32)
    sums.ref[5:8, :] = jnp.zeros((3, D), F32)
    sums.send()


def columns(rows):
    count = rows.shape[0]
    if count % 8:
        return jnp.stack(
            [jnp.transpose(jnp.broadcast_to(rows[i : i + 1], (BLK, BLK)))[:, 0:1] for i in range(count)]
        )
    turned = jnp.transpose(rows)
    return jnp.stack([turned[:, i : i + 1] for i in range(count)])


def reflect(blocks, left, right, coef_left, coef_right):
    along = jnp.sum(left * blocks, axis=1, keepdims=True) * coef_left
    blocks = blocks - left * along
    across = jnp.sum(blocks * right, axis=2, keepdims=True) * coef_right
    return blocks - across * right


def reflectors(left_ref, right_ref):
    left, right = left_ref[...], right_ref[...]
    coef_left = (2.0 / jnp.sum(left * left, axis=1, keepdims=True))[:, :, None]
    coef_right = (2.0 / jnp.sum(right * right, axis=1, keepdims=True))[:, :, None]
    return (columns(left), right[:, None, :], coef_left, coef_right)


def collect_kernel(counts, group, me_ref, place_ref, loads, stores, found_ref):
    grads, total = stores
    at = 0
    for number, count in enumerate(counts):
        keep, got = loads[2 * number : 2 + 2 * number]
        found_ref[at : at + count] = keep()[...].astype(F32) + got()[...].astype(F32)
        at += count
    slots = grads.ref.shape[0]
    square = jnp.zeros((8, BLK), F32)
    for at in range(0, slots, group):
        rows = slice(at, at + group)
        for slot in range(at, at + group):
            grads.ref[slot] = found_ref[place_ref[me_ref[0] * slots + slot]]
        grads.send(rows)
        grad = grads.ref[rows]
        square = square + jnp.sum((grad * grad).reshape(group * BLK // 8, 8, BLK), axis=0)
    total.ref[...] = jnp.full((8, BLK), jnp.sum(square), F32)
    total.send()


def rotate_kernel(group, me_ref, loads, stores):
    left, right, grads = loads
    (turned,) = stores
    parts = reflectors(left(), right())
    grads_ref = grads()
    for at in range(0, turned.ref.shape[0], group):
        rows = slice(at, at + group)
        turned.ref[rows] = reflect(grads_ref[rows], *(part[rows] for part in parts))
        turned.send(rows)


def inverse(value):
    guess = pl.reciprocal(value, approx=True)
    return guess * (2.0 - value * guess)


def update_kernel(group, me_ref, scal_ref, loads, stores):
    sums, norm, norm_first, norm_second, left, right = loads[:6]
    grads, turned_grads, old_first, old_second, old_master = loads[6:]
    out_grad, out_first, out_second, out_master, out_copy = stores[:5]
    norm_pair, norm_square, norm_value, clip_out = stores[5:]
    inv_one = 1.0 / scal_ref[1]
    inv_two = 1.0 / scal_ref[2]
    sums_ref = sums()
    share = 1.0 / sums_ref[4:5, 0:BLK]
    norm_grad = sums_ref[0:4, :] * share[:, 0:1]
    total = sums_ref[5:6, 0:BLK] * (share * share) + jnp.sum(norm_grad * norm_grad)
    clip_norm = jnp.sqrt(total)
    clip = jnp.minimum(1.0, clip_max / clip_norm)
    factor = (share * clip)[:, None, :]
    parts = reflectors(left(), right())
    slots = left.ref.shape[0]
    entries = 1.0 / (BLK * BLK)
    for at in range(0, slots, group):
        rows = slice(at, at + group)
        out_grad.ref[rows] = grads()[rows] * factor
        rotated = turned_grads()[rows] * factor
        first = beta_one * old_first()[rows] + (1.0 - beta_one) * rotated
        second = beta_two * old_second()[rows] + (1.0 - beta_two) * rotated * rotated
        out_first.ref[rows] = first
        out_second.ref[rows] = second
        spread = second * inv_two
        normal = (first * inv_one) * inverse(spread * lax.rsqrt(spread) + adam_eps)
        turned = reflect(normal, *(part[rows] for part in parts))
        master = old_master()[rows]
        size = jnp.sum(jnp.sum(master * master, axis=1, keepdims=True), axis=2, keepdims=True)
        move = jnp.sum(jnp.sum(turned * turned, axis=1, keepdims=True), axis=2, keepdims=True)
        trust = jnp.sqrt(size * entries + trust_eps) / jnp.sqrt(move * entries + trust_eps)
        fresh = master - (step_rate * trust) * turned
        out_master.ref[rows] = fresh
        out_copy.ref[rows] = fresh.astype(BF16)
        for out in (out_grad, out_first, out_second, out_master, out_copy):
            out.send(rows)
    clip_out.target[0, 0] = clip_norm[0, 0]
    clipped = norm_grad * clip[:, 0:1]
    first = beta_one * norm_first()[...] + (1.0 - beta_one) * clipped
    second = beta_two * norm_second()[...] + (1.0 - beta_two) * clipped * clipped
    norm_pair.ref[0] = clipped
    norm_pair.ref[1] = first
    norm_pair.send()
    norm_square.ref[...] = second
    norm_square.send()
    norm_value.ref[...] = norm()[...] - step_rate * (first * inv_one) / (
        jnp.sqrt(second * inv_two) + adam_eps
    )
    norm_value.send()


def swap(value, axis, bit):
    count = lax.axis_size(axis)
    return lax.ppermute(value, axis, [(i, i ^ bit) for i in range(count)])


def plus(left, right):
    return (left.astype(F32) + right.astype(F32)).astype(BF16)


def after(value, *others):
    return lax.optimization_barrier((value, *others))[0]


def mp_far(total, wait=None):
    bit = 2
    while bit < lax.axis_size("mp"):
        got = swap(total, "mp", bit)
        total = plus(total, got if wait is None else after(got, wait))
        bit *= 2
    return total


def mp_sum(keep, send):
    total = mp_far(plus(keep, swap(send, "mp", 1)))
    return (total, swap(total, "mp", 1))


def early_count(slots):
    return slots // 3 if slots >= 24 else 0


def split_counts(slots, bits):
    if slots >= 8:
        last = slots // 4
        head = (slots - last + 2) // 2
        return ((head, bits), (slots - last - head, bits), (last, (bits[1], bits[0]) + bits[2:]))
    return ((1, bits),) * slots if slots <= 3 else ((slots - slots // 2, bits), (slots // 2, bits))


def exclusive_sum(values):
    size = values.shape[-1]
    before = jnp.asarray(np.tril(np.ones((size, size), np.int32), -1))
    return jnp.sum(values[..., None, :] * before, axis=-1)


def rest_count(blocks, late_count, n_dp, slots, early_slots):
    total = blocks - late_count
    full, over = divmod(total, slots)
    return total - full * early_slots - min(over, early_slots)


def slot_tables(owner_list, n_dp, slots, early_slots, late_count):
    blocks = owner_list.shape[0]
    owned = owner_list.reshape(n_dp, slots)
    early = (owned >= late_count).astype(jnp.int32)
    if early_slots:
        goes = early * (exclusive_sum(early) < early_slots).astype(jnp.int32)
        place = jnp.where(goes == 1, exclusive_sum(early), early_slots + exclusive_sum(1 - goes))
        positions = slots + early_slots
        hit = place[:, None, :] == jnp.arange(positions, dtype=jnp.int32)[None, :, None]
        source = jnp.sum(jnp.where(hit, owned[:, None, :], 0), axis=2)
        short = jnp.any(jnp.sum(early, axis=1) < early_slots)
    else:
        place = jnp.broadcast_to(jnp.arange(slots, dtype=jnp.int32), (n_dp, slots))
        source, short = owned, jnp.zeros((), bool)
    later = source[:, early_slots:].reshape(-1)
    is_rest = (later >= late_count).astype(jnp.int32)
    order = exclusive_sum(is_rest)
    count = rest_count(blocks, late_count, n_dp, slots, early_slots)
    hit = (order[None, :] == jnp.arange(count, dtype=jnp.int32)[:, None]) & (is_rest[None, :] == 1)
    rest = jnp.sum(jnp.where(hit, later[None, :], 0), axis=1)
    later = jnp.where(is_rest == 1, late_count + order, later)
    source = jnp.concatenate([source[:, :early_slots], later.reshape(n_dp, -1)], axis=1)
    return (jnp.concatenate([source.reshape(-1), rest]), place.reshape(-1), short)


def shards(
    tokens,
    cotangent,
    segment_ids,
    table_index,
    group_count,
    owner_list,
    step_count,
    query_weight,
    key_weight,
    value_weight,
    output_weight,
    hidden_weight,
    return_weight,
    norm_params,
    norm_first,
    norm_second,
    master_blocks,
    first_moment,
    second_moment,
    left_vector,
    right_vector,
):
    length = tokens.shape[0]
    half = length // 2
    width = query_weight.shape[1]
    heads = width // HEAD
    units = hidden_weight.shape[1]
    slots = master_blocks.shape[0]
    blocks = owner_list.shape[0]
    late_count = blocks // 3
    n_dp = lax.axis_size("dp")
    natural = tuple(1 << i for i in range(n_dp.bit_length() - 1))
    early_slots = early_count(slots)
    positions = slots + early_slots
    me = jnp.stack([lax.axis_index("dp"), lax.axis_index("mp")]).astype(jnp.int32)
    step_value = step_count[0].astype(F32)
    source, place, short = slot_tables(owner_list, n_dp, slots, early_slots, late_count)
    scal = jnp.stack(
        [
            group_count[0].astype(F32),
            1.0 - jnp.power(beta_one, step_value),
            1.0 - jnp.power(beta_two, step_value),
            short.astype(F32),
        ]
    )
    seg_row = segment_ids.reshape(1, length)
    index_row = table_index.reshape(1, length)
    table = jnp.asarray(position_rows())
    rows_d = (length, D)
    half_d = (half, D)
    unit = 2 * length * D * D
    wide = ((length, width), BF16)

    normed, q, k, v, mixed, lse, keep_a, send_a, keep_b, send_b = call(
        forward_kernel,
        "attention_forward",
        (me,),
        (
            index_row,
            table,
            tokens,
            seg_row,
            norm_params,
            query_weight,
            key_weight,
            value_weight,
            output_weight,
        ),
        [
            (rows_d, BF16),
            wide,
            wide,
            wide,
            wide,
            ((length, heads), F32),
            (half_d, BF16, True),
            (half_d, BF16, True),
        ],
        [(rows_d, F32), ((length, length), F32)],
        flops=5 * unit,
    )
    near_a = plus(keep_a, swap(send_a, "mp", 1))
    near_b = plus(keep_b, swap(send_b, "mp", 1))
    token = near_b
    grad_out, grad_act = call(
        grad_out_kernel,
        "grad_of_act",
        (me,),
        (seg_row, cotangent, return_weight),
        [(rows_d, BF16), ((length, units), F32)],
        flops=2 * unit,
        after=token,
    )

    far_a = mp_far(near_a, grad_act)
    attn_a = Pair(far_a, swap(far_a, "mp", 1))
    def feed(row0, name, sums, token):
        return call(
            functools.partial(feed_kernel, row0),
            name,
            (me,),
            (
                index_row,
                table,
                Rows(tokens, row0, half),
                sums,
                norm_params,
                hidden_weight,
                Rows(grad_act, row0, half),
            ),
            [
                (half_d, BF16),
                ((half, units), BF16),
                ((half, units), BF16),
                (half_d, BF16, True),
            ],
            [((half, units), F32)],
            flops=4 * unit,
            after=token,
        )

    second_a, act_a, gpre_a, keep_a, send_a = feed(0, "feed_forward_a", attn_a, None)
    far_b = mp_far(near_b, keep_a)
    attn_b = Pair(far_b, swap(far_b, "mp", 1))
    second_b, act_b, gpre_b, keep_b, send_b = feed(half, "feed_forward_b", attn_b, keep_a)
    near_a = plus(keep_a, swap(send_a, "mp", 1))
    near_b = plus(keep_b, swap(send_b, "mp", 1))
    chunk_e = [((n_dp // 2 * early_slots, BLK, BLK), BF16)] * 2 if early_slots else []
    count = rest_count(blocks, late_count, n_dp, slots, early_slots)
    rest, *chunk_e = call(
        functools.partial(feed_grad_kernel, natural, early_slots, positions, late_count),
        "feed_weight_grads",
        (me, source, scal),
        (Stack(second_a, second_b), Stack(gpre_a, gpre_b), Stack(act_a, act_b), grad_out),
        [((count, BLK, BLK), BF16)] + chunk_e,
        [((blocks - late_count, BLK, BLK), BF16)],
        flops=4 * unit,
        after=near_b,
    )
    far_a = mp_far(near_a, rest)
    far_b = mp_far(near_b, far_a)
    sum_a = Pair(far_a, swap(far_a, "mp", 1))
    sum_b = Pair(far_b, swap(far_b, "mp", 1))
    got_e = swap(chunk_e[1], "dp", 1) if early_slots else None
    chunks = split_counts(slots - early_slots, natural)
    chunk_shapes = []
    for count, _ in chunks:
        chunk_shapes += [((n_dp // 2 * count, BLK, BLK), BF16)] * 2
    outs = call(
        functools.partial(backward_kernel, chunks, early_slots, positions, late_count),
        "attention_backward",
        (me, source, scal),
        (
            index_row,
            table,
            tokens,
            Stack(attn_a, attn_b),
            norm_params,
            Stack(sum_a, sum_b),
            grad_out,
            output_weight,
            seg_row,
            q,
            k,
            v,
            lse,
            normed,
            mixed,
            Into(rest, late_count),
            Stack(query_weight, key_weight, value_weight),
            Stack(act_a, act_b),
            return_weight,
        ),
        [((late_count, BLK, BLK), BF16), ((2 * length, D), BF16, True)] + chunk_shapes,
        [(rows_d, BF16)]
        + [((length, width), BF16), ((3, length, width), BF16)]
        + [(rows_d, F32), ((length, length), F32)],
        flops=10 * unit,
    )
    late, keep, send = outs[:3]
    queue = [(outs[3 + 2 * i], outs[4 + 2 * i]) for i in range(len(chunks))]
    counts = [count for count, _ in chunks]
    orders = [bits for _, bits in chunks]

    stages = len(natural)
    state = [(first, swap(second, "dp", bits[0])) for (first, second), bits in zip(queue, orders)]
    if early_slots:
        state.insert(0, (chunk_e[0], after(got_e, keep)))
        counts.insert(0, early_slots)
        orders.insert(0, natural)
    level = [0] * len(state)
    last = []

    def in_turn(got):
        got = after(got, *last)
        last[:] = [got]
        return got

    def halve(number):
        keep, got = state[number]
        got = in_turn(got)
        if level[number] < stages - 1:
            n = keep.shape[0] // 2
            keep, send = plus(keep[:n], got[:n]), plus(keep[n:], got[n:])
            got = swap(send, "dp", orders[number][level[number] + 1])
            last.append(send)
        level[number] += 1
        state[number] = (keep, got)

    def mp_first(keep, send):
        return plus(keep, in_turn(swap(send, "mp", 1)))

    def mp_rest(near):
        bit = 2
        while bit < lax.axis_size("mp"):
            near = plus(near, in_turn(swap(near, "mp", bit)))
            bit *= 2
        return Pair(near, swap(near, "mp", 1))

    if early_slots:
        halve(0)
    def finish(both):
        outputs = call(
            finish_kernel,
            "layer_outputs",
            (me, scal),
            (
                index_row,
                table,
                tokens,
                attn_a,
                attn_b,
                norm_params,
                both,
                sum_a,
                sum_b,
                grad_out,
            ),
            [(rows_d, F32), (rows_d, F32), ((8, D), F32)],
            [(half_d, F32), ((32, D), F32)],
            flops=2 * unit,
        )
        last.append(outputs[2])
        return outputs

    overflow, early_done = [], []
    if early_slots:
        shape = (n_dp // 2 * early_slots, BLK, BLK)

        def exchange(late):
            keep, send = call(
                functools.partial(overflow_kernel, slots, early_slots, natural, positions),
                "overflow",
                (me, source),
                (late,),
                [(shape, BF16), (shape, BF16)],
            )
            bit = 1
            while True:
                got = swap(send, "dp", bit)
                bit *= 2
                if bit >= n_dp:
                    return (keep, got)
                n = keep.shape[0] // 2
                keep, send = plus(keep[:n], got[:n]), plus(keep[n:], got[n:])

        def nothing(late):
            zero = jnp.zeros((early_slots, BLK, BLK), BF16)
            return (zero, zero)

        overflow = list(lax.cond(short, exchange, nothing, late))
        early_done = [overflow[0], place]

    plan = ["near", "far", "finish"]
    if early_slots and stages == 3:
        plan = ["near",(3,0),(1,0),(0,1),(2,0),(1,1),(3,1),(0,2),(2,1),(1,2),"far","finish"]
    plan += [(i, d - i) for d in range(len(state) + stages) for i in range(len(state))]
    for entry in plan:
        if entry == "near":
            near = plus(keep, in_turn(swap(send, "mp", 1)))
            last += early_done
        elif entry == "far":
            bit = 2
            while bit < lax.axis_size("mp"):
                near = plus(near, in_turn(swap(near, "mp", bit)))
                bit *= 2
            both = Pair(near, swap(near, "mp", 1))
        elif entry == "finish":
            out, input_grad, sums = finish(both)
        elif level[entry[0]] == entry[1] < stages:
            halve(entry[0])
    pending = [array for pair in state for array in pair]

    pending += overflow
    counts += [early_slots] if early_slots else []
    left = left_vector.reshape(slots, BLK)
    right = right_vector.reshape(slots, BLK)
    block_f32 = ((slots, BLK, BLK), F32)
    group = 4 if slots % 4 == 0 else 1
    grads, square = call(
        functools.partial(collect_kernel, counts, group),
        "collect",
        (me, place),
        tuple(pending),
        [block_f32, ((8, BLK), F32)],
        [((sum(counts), BLK, BLK), F32)],
        flops=unit,
        limit=40 * MIB,
    )
    (rotated,) = call(
        functools.partial(rotate_kernel, group),
        "rotate",
        (me,),
        (left, right, grads),
        [block_f32],
        flops=unit,
        limit=40 * MIB,
    )
    bit = 1
    while bit < lax.axis_size("mp"):
        square = square + swap(square, "mp", bit)
        bit *= 2
    sums = sums + jnp.pad(square[0:1], ((5, 2), (0, D - BLK)))
    bit = 1
    while bit < n_dp:
        sums = sums + swap(sums, "dp", bit)
        bit *= 2
    new = call(
        functools.partial(update_kernel, group),
        "update",
        (me, scal),
        (
            sums,
            norm_params,
            norm_first,
            norm_second,
            left,
            right,
            grads,
            rotated,
            first_moment.reshape(slots, BLK, BLK),
            second_moment.reshape(slots, BLK, BLK),
            master_blocks.reshape(slots, BLK, BLK),
        ),
        [block_f32] * 4
        + [
            ((slots, BLK, BLK), BF16),
            ((2, 4, D), F32),
            ((4, D), F32),
            ((4, D), F32),
            ((1, 1), F32),
        ],
        flops=unit,
        limit=40 * MIB,
    )
    shard_shape = (slots, 1, BLK, BLK)
    return (
        out,
        input_grad,
        new[0].reshape(shard_shape),
        new[1].reshape(shard_shape),
        new[2].reshape(shard_shape),
        new[3].reshape(shard_shape),
        new[4].reshape(shard_shape),
        new[5],
        new[6],
        new[7],
        new[8].reshape(()),
    )


def solution(mesh):
    placed = (
        P("dp", None),
        P("dp", None),
        P("dp"),
        P("dp"),
        P("dp"),
        P(),
        P(),
        P(None, "mp"),
        P(None, "mp"),
        P(None, "mp"),
        P("mp", None),
        P(None, "mp"),
        P("mp", None),
        P(),
        P(),
        P(),
        P("dp", "mp", None, None),
        P("dp", "mp", None, None),
        P("dp", "mp", None, None),
        P("dp", "mp", None),
        P("dp", "mp", None),
    )
    return jax.shard_map(
        shards,
        mesh=mesh,
        in_specs=placed,
        out_specs=(
            P("dp", None),
            P("dp", None),
            P("dp", "mp", None, None),
            P("dp", "mp", None, None),
            P("dp", "mp", None, None),
            P("dp", "mp", None, None),
            P("dp", "mp", None, None),
            P(),
            P(),
            P(),
            P(),
        ),
        check_vma=False,
    )
```

```python
import functools
import math

import jax
import jax.numpy as jnp
import numpy as np
from jax import lax
from jax.experimental import pallas as pl
from jax.experimental.pallas import tpu as pltpu
from jax.sharding import PartitionSpec as P

D = 1024
HEAD = 64
BLK = 128
LANES = 128
POS_ROWS = 64
SEG_ROWS = 32

clip_max = 1.0
beta_one = 0.5
beta_two = 0.5
adam_eps = 1e-08
step_rate = 0.25
norm_eps = 1e-06
trust_eps = 1e-06

F32 = jnp.float32
BF16 = jnp.bfloat16
MIB = 1024 * 1024
VMEM_LIMIT = 60 * MIB

ERF_P = 0.425
ERF_COEF = (
    0.11983931305209315,
    0.12092032287702306,
    0.10035292560006456,
    0.12754356284084392,
    -0.051626023300101125,
    0.20380940869554587,
    -0.1565787944569494,
    0.035739213095996265,
)


def position_rows():
    coords = np.concatenate(
        [1.75 * np.arange(8), 1.0 * np.arange(14), 0.5 * np.arange(28), np.zeros(POS_ROWS - 50)]
    )
    quarter = D // 4
    freqs = np.power(np.float32(10000.0), -np.arange(quarter, dtype=np.float32) / np.float32(quarter))
    args = (coords.astype(np.float32)[:, None] * freqs.astype(np.float32)[None, :]).astype(np.float64)
    table = np.concatenate([np.sin(args), np.cos(args)], axis=1).astype(np.float32)
    parts = []
    rest = table
    for _ in range(3):
        part = rest.astype(jnp.bfloat16)
        parts.append(part)
        rest = rest - part.astype(np.float32)
    return np.concatenate(parts, axis=0)


def dot_nn(left, right):
    return lax.dot_general(left, right, (((1,), (0,)), ((), ())), preferred_element_type=F32)


def dot_nt(left, right):
    return lax.dot_general(left, right, (((1,), (1,)), ((), ())), preferred_element_type=F32)


def dot_tn(left, right):
    return lax.dot_general(left, right, (((0,), (0,)), ((), ())), preferred_element_type=F32)


def norm_hat(values):
    center = values - jnp.mean(values, axis=-1, keepdims=True)
    inv_std = lax.rsqrt(jnp.mean(center * center, axis=-1, keepdims=True) + norm_eps)
    return (center * inv_std, inv_std)


def norm_back(grad_out, normal, inv_std, gain):
    scaled = grad_out * gain
    return inv_std * (
        scaled
        - jnp.mean(scaled, axis=-1, keepdims=True)
        - normal * jnp.mean(scaled * normal, axis=-1, keepdims=True)
    )


def gelu_parts(values):
    bell = jnp.exp(-0.5 * values * values)
    t = 1.0 / (1.0 + (ERF_P / math.sqrt(2.0)) * jnp.abs(values))
    poly = ERF_COEF[-1]
    for coef in ERF_COEF[-2::-1]:
        poly = poly * t + coef
    tail = poly * t * bell
    dist = jnp.where(values >= 0.0, 1.0 - tail, tail)
    return (values * dist, dist + values * ((1.0 / math.sqrt(2.0 * math.pi)) * bell))


def item_rows(seg_row):
    rows = lax.broadcasted_iota(jnp.int32, (SEG_ROWS, seg_row.shape[1]), 0)
    return jnp.where(rows == seg_row, 1.0, 0.0).astype(BF16)


def head_lanes(rows, head):
    lanes = lax.broadcasted_iota(jnp.int32, (rows, LANES), 1)
    return (lanes // HEAD) == head


def position_hots(index):
    length = index.shape[1]
    big = index >= 260
    mid = index >= 64
    offset = jnp.where(big, 260, jnp.where(mid, 64, 0))
    base = jnp.where(big, 22, jnp.where(mid, 8, 0))
    side = jnp.where(big, 28, jnp.where(mid, 14, 8))
    inv_side = jnp.where(big, 1.0 / 28.0, jnp.where(mid, 1.0 / 14.0, 1.0 / 8.0)).astype(F32)
    local = index - offset
    row = jnp.floor((local.astype(F32) + 0.5) * inv_side).astype(jnp.int32)
    col = local - row * side
    rows = lax.broadcasted_iota(jnp.int32, (3 * POS_ROWS, length), 0) & (POS_ROWS - 1)
    row_hot = jnp.where(rows == base + row, 1.0, 0.0).astype(BF16)
    col_hot = jnp.where(rows == base + col, 1.0, 0.0).astype(BF16)
    return (row_hot, col_hot)


def fill_layer(out_ref, index_row, table, tok_ref, sum_ref=None):
    half = D // 2
    for hot, cols in zip(position_hots(index_row), (slice(0, half), slice(half, D))):
        value = dot_tn(hot, table) + tok_ref[:, cols].astype(F32)
        if sum_ref is not None:
            value = value + sum_ref[:, cols].astype(F32)
        out_ref[:, cols] = value


def fill_bias(bias_ref, seg_row):
    length = seg_row.shape[1]
    items = item_rows(seg_row)
    same = dot_tn(items, items)
    diag = lax.broadcasted_iota(jnp.int32, (length, length), 0) == lax.broadcasted_iota(
        jnp.int32, (length, length), 1
    )
    bias_ref[...] = jnp.where((same > 0.5) | diag, 0.0, -1e30)


def lane_of(values, number):
    lanes = lax.broadcasted_iota(jnp.int32, values.shape, 1)
    return jnp.sum(jnp.where(lanes == number, values, 0.0), axis=1, keepdims=True)


def head_columns(number):
    return pl.ds(pl.multiple_of((number // 2) * LANES, LANES), LANES)


def attend(q_ref, k_ref, v_ref, bias_ref, mixed_ref, lse_ref):
    count = q_ref.shape[0]
    scale = 1.0 / math.sqrt(HEAD)
    step = 512
    for pair in range(q_ref.shape[1] // LANES):
        cols = slice(pair * LANES, (pair + 1) * LANES)
        keys = k_ref[:, cols]
        vals = v_ref[:, cols]
        for at in range(0, count, step):
            rows = slice(at, at + step)
            query = q_ref[rows, cols] * scale
            outs = []
            for head in range(2):
                here = head_lanes(step, head)
                scores = dot_nt(jnp.where(here, query, 0.0).astype(BF16), keys) + bias_ref[rows, :]
                peak = jnp.max(scores, axis=-1, keepdims=True)
                expon = jnp.exp(scores - peak)
                total = jnp.sum(expon, axis=-1, keepdims=True)
                outs.append(dot_nn(expon.astype(BF16), vals) * (1.0 / total))
                number = pair * 2 + head
                lse_ref[rows, number : number + 1] = peak + jnp.log(total)
            mixed_ref[rows, cols] = jnp.where(
                head_lanes(step, 0), outs[0], outs[1]
            ).astype(BF16)


class Load:
    def __init__(self, ref):
        self.ref = ref
        self.copies = []

    def __call__(self):
        for copy in self.copies:
            copy.wait()
        self.copies = []
        return self.ref


class Store:
    def __init__(self, ref, target, sem, running):
        self.ref = ref
        self.target = target
        self.sem = sem
        self.running = running
        self.sent = 0

    def send(self, rows=None):
        source = self.ref if rows is None else self.ref.at[rows]
        target = self.target if rows is None else self.target.at[rows]
        copy = pltpu.make_async_copy(source, target, self.sem.at[self.sent])
        copy.start()
        self.sent += 1
        self.running.append(copy)


    def send_if(self, flag, source):
        @pl.when(flag)
        def _():
            copy = pltpu.make_async_copy(source, self.target, self.sem.at[0])
            copy.start()
            copy.wait()


class Split:
    def __init__(self, ref, keep, send, sem, running, bit):
        self.ref = ref
        self.targets = ((send, 1 - bit), (keep, bit))
        self.sem = sem
        self.running = running

    def send(self):
        half = self.ref.shape[0] // 2
        for i, (target, which) in enumerate(self.targets):
            rows = pl.ds(pl.multiple_of(which * half, half), half)
            copy = pltpu.make_async_copy(self.ref.at[rows], target, self.sem.at[i])
            copy.start()
            self.running.append(copy)


class Rows:
    def __init__(self, array, first, count):
        self.array = array
        self.first = first
        self.count = count


class Into:
    def __init__(self, array, first):
        self.array = array
        self.first = first


class Pair:
    def __init__(self, own, other, first=0, count=None):
        self.own = own
        self.other = other
        self.first = first
        self.count = own.shape[0] if count is None else count


class Stack:
    def __init__(self, *parts):
        self.parts = parts


SEMS = 24


def row_moves(entry, sources, ref, first, bit):
    if isinstance(entry, Stack):
        moves = []
        for part in entry.parts:
            more, first = row_moves(part, sources, ref, first, bit)
            moves += more
        return (moves, first)
    if isinstance(entry, Pair):
        moves = []
        for which in (bit, 1 - bit):
            rows = pl.ds(pl.multiple_of(first + which * entry.count, entry.count), entry.count)
            part = sources.pop(0).at[entry.first : entry.first + entry.count]
            moves.append((part, ref.at[rows]))
        return (moves, first + 2 * entry.count)
    count = entry.count if isinstance(entry, Rows) else entry.shape[0]
    source = sources.pop(0)
    if isinstance(entry, Rows):
        source = source.at[entry.first : entry.first + count]
    whole = count == ref.shape[0]
    return ([(source, ref if whole else ref.at[first : first + count])], first + count)


def flat(entry):
    if isinstance(entry, Stack):
        parts = [flat(part) for part in entry.parts]
        return (sum((p[0] for p in parts), []), sum(p[1] for p in parts), parts[0][2])
    if isinstance(entry, Pair):
        return ([entry.own, entry.other], 2 * entry.count, entry.own)
    if isinstance(entry, Rows):
        return ([entry.array], entry.count, entry.array)
    if isinstance(entry, Into):
        return ([entry.array], entry.first + entry.array.shape[0], entry.array)
    return ([entry], entry.shape[0], entry)


def call(kernel, name, scalars, ins, outs, scratch=(), flops=0, after=None, limit=VMEM_LIMIT):
    operands = []
    shapes = []
    for entry in ins:
        arrays, rows, like = flat(entry)
        operands += arrays
        shapes.append(((rows,) + like.shape[1:], like.dtype))
    if after is not None:
        operands.append(after)
    results = []
    for shape, kind, *split in outs:
        if split:
            results += [jax.ShapeDtypeStruct((shape[0] // 2,) + shape[1:], kind)] * 2
        else:
            results.append(jax.ShapeDtypeStruct(shape, kind))
    n_scalar, n_in, n_out = len(scalars), len(operands), len(results)

    def body(*refs):
        smem_refs = refs[:n_scalar]
        sources = list(refs[n_scalar : n_scalar + n_in])
        targets = list(refs[n_scalar + n_in : n_scalar + n_in + n_out])
        rest = list(refs[n_scalar + n_in + n_out :])
        in_refs, rest = rest[: len(ins)], rest[len(ins) :]
        out_refs, rest = rest[: len(outs)], rest[len(outs) :]
        in_sem, out_sem = rest[:2]
        bit = smem_refs[0][1] & 1
        loads = []
        number = 0
        for entry, ref in zip(ins, in_refs):
            load = Load(ref)
            if isinstance(entry, Into):
                moves = [(sources.pop(0), ref.at[entry.first : ref.shape[0]])]
            else:
                moves, _ = row_moves(entry, sources, ref, 0, bit)
            for source, target in moves:
                copy = pltpu.make_async_copy(source, target, in_sem.at[number])
                copy.start()
                load.copies.append(copy)
                number += 1
            loads.append(load)
        running = []
        stores = []
        for i, (entry, ref) in enumerate(zip(outs, out_refs)):
            if len(entry) > 2:
                keep, send = targets.pop(0), targets.pop(0)
                stores.append(Split(ref, keep, send, out_sem.at[i], running, bit))
            else:
                stores.append(Store(ref, targets.pop(0), out_sem.at[i], running))
        kernel(*smem_refs, loads, stores, *rest[2:])
        for load in loads:
            load()
        for copy in running:
            copy.wait()

    hbm = pl.BlockSpec(memory_space=pltpu.HBM)
    scalar = pl.BlockSpec(memory_space=pltpu.SMEM)
    return pl.pallas_call(
        body,
        name=name,
        out_shape=results,
        in_specs=[pl.BlockSpec(memory_space=pltpu.SMEM)] * n_scalar + [hbm] * n_in,
        out_specs=[scalar if r.shape == (1, 1) else hbm for r in results],
        scratch_shapes=[pltpu.VMEM(shape, kind) for shape, kind in shapes]
        + [pltpu.VMEM(shape, kind) for shape, kind, *_ in outs]
        + [pltpu.SemaphoreType.DMA((max(n_in, 1),)), pltpu.SemaphoreType.DMA((len(outs), SEMS))]
        + [pltpu.VMEM(shape, kind) for shape, kind in scratch],
        compiler_params=pltpu.CompilerParams(vmem_limit_bytes=limit),
        cost_estimate=pl.CostEstimate(flops=int(flops), bytes_accessed=0, transcendentals=0),
    )(*scalars, *operands)


def forward_kernel(me_ref, loads, stores, layer_ref, bias_ref):
    index, table, tokens, seg, norm, wq, wk, wv, wo = loads
    normed, q, k, v, mixed, lse, first, last = stores
    length = tokens.ref.shape[0]
    half = length // 2
    index_row = index()[...]
    rows_of = table()[...]
    tok_ref = tokens()
    fill_layer(layer_ref, index_row, rows_of, tok_ref)
    fill_bias(bias_ref, seg()[...])
    norm_ref = norm()
    step = 128
    for at in range(0, length, step):
        rows = slice(at, at + step)
        hat, _ = norm_hat(layer_ref[rows, :])
        normed.ref[rows, :] = (hat * norm_ref[0:1, :] + norm_ref[1:2, :]).astype(BF16)
    normed.send()
    left = normed.ref[...]
    for weight, out in ((wq, q), (wk, k), (wv, v)):
        out.ref[...] = dot_nn(left, weight()[...]).astype(BF16)
        out.send()
    attend(q.ref, k.ref, v.ref, bias_ref, mixed.ref, lse.ref)
    mixed.send()
    lse.send()
    wo_ref = wo()
    for at, out in ((0, first), (half, last)):
        out.ref[...] = dot_nn(mixed.ref[at : at + half, :], wo_ref[...]).astype(BF16)
        out.send()


def grad_out_kernel(me_ref, loads, stores):
    seg, cotangent, return_weight = loads
    gout, gact = stores
    items = item_rows(seg()[...])
    valid = dot_tn(items, jnp.ones((SEG_ROWS, LANES), BF16))
    cot_ref = cotangent()
    for at in range(0, D, LANES):
        cols = slice(at, at + LANES)
        gout.ref[:, cols] = (cot_ref[:, cols].astype(F32) * valid).astype(BF16)
    gout.send()
    weight = return_weight()[...]
    half = gact.ref.shape[0] // 2
    for at in (0, half):
        rows = slice(at, at + half)
        gact.ref[rows, :] = dot_nt(gout.ref[rows, :], weight)
        gact.send(rows)


def feed_kernel(row0, me_ref, loads, stores, pre_ref):
    index, table, tokens, sums, norm, hidden_weight, gact = loads
    second, act, gpre, part = stores
    length = tokens.ref.shape[0]
    index_row = index()[:, row0 : row0 + length]
    rows_of = table()[...]
    tok_ref = tokens()
    fill_layer(pre_ref, index_row, rows_of, tok_ref, sums())
    norm_ref = norm()
    step = 64
    for at in range(0, length, step):
        rows = slice(at, at + step)
        hat, _ = norm_hat(pre_ref[rows, :])
        second.ref[rows, :] = (hat * norm_ref[2:3, :] + norm_ref[3:4, :]).astype(BF16)
    second.send()
    weight_ref = hidden_weight()
    pre_ref[...] = dot_nn(second.ref[...], weight_ref[...])
    gact_ref = gact()
    step = 32

    @pl.loop(0, length // step)
    def _(i):
        rows = pl.ds(pl.multiple_of(i * step, step), step)
        value, slope = gelu_parts(pre_ref[rows, :])
        act.ref[rows, :] = value.astype(BF16)
        gpre.ref[rows, :] = (gact_ref[rows, :] * slope).astype(BF16)

    act.send()
    gpre.send()
    part.ref[...] = dot_nt(gpre.ref[...], weight_ref[...]).astype(BF16)
    part.send()


def store_blocks(nat_ref, base, left, right_ref, weight, unroll=False):
    width = right_ref.shape[1]
    across = width // BLK
    wide = 256

    @pl.loop(0, width // wide, unroll=unroll)
    def _(step):
        cols = pl.ds(pl.multiple_of(step * wide, wide), wide)
        grad = (dot_tn(left, right_ref[:, cols]) * weight).astype(BF16)
        for i in range(grad.shape[0] // BLK):
            for j in range(wide // BLK):
                nat_ref[base + i * across + step * (wide // BLK) + j] = grad[
                    i * BLK : (i + 1) * BLK, j * BLK : (j + 1) * BLK
                ]


def relative(order, bits):
    out = 0
    for i, bit in enumerate(bits):
        if (order >> (len(bits) - 1 - i)) & 1:
            out |= bit
    return out


def gather_blocks(me_ref, source_ref, positions, first, count, bits, keep_ref, send_ref, block_at):
    owners = 2 ** len(bits)
    for order in range(owners):
        dest = me_ref[0] ^ relative(order, bits)
        out_ref = keep_ref if order < owners // 2 else send_ref
        at = (order % (owners // 2)) * count

        @pl.loop(0, count)
        def _(j, out_ref=out_ref, at=at, place=dest * positions + first):
            out_ref[at + j] = block_at(source_ref[place + j])


def feed_grad_kernel(
    bits, early_slots, positions, late_count, me_ref, source_ref, scal_ref, loads, stores, nat_ref
):
    second, gpre, act, gout = loads
    rest = stores[0]
    weight = scal_ref[0]
    store_blocks(nat_ref, 0, second()[...], gpre(), weight, True)
    store_blocks(nat_ref, 64, act()[...], gout(), weight, True)

    def block_at(block):
        return nat_ref[jnp.maximum(block - late_count, 0)]

    if early_slots:
        keep, send = stores[1:]
        gather_blocks(
            me_ref, source_ref, positions, 0, early_slots, bits, keep.ref, send.ref, block_at
        )
        send.send()
        keep.send()

    @pl.loop(0, rest.ref.shape[0])
    def _(i):
        rest.ref[i] = block_at(source_ref[2 ** len(bits) * positions + i])

    rest.send()


def backward_kernel(
    chunks,
    first,
    positions,
    late_count,
    me_ref,
    source_ref,
    scal_ref,
    loads,
    stores,
    gattn_ref,
    gmix_ref,
    grads_ref,
    hid_ref,
    bias_ref,
):
    index, table, tokens, attn, norm, sums, gout = loads[:7]
    wo, seg, q, k, v, lse, normed, mixed, rest, qkv_weight, act, return_weight = loads[7:]
    late, parts = stores[:2]
    chunk_stores = stores[2:]
    length = tokens.ref.shape[0]
    half = length // 2
    width = q.ref.shape[1]
    weight = scal_ref[0]
    step = 64
    index_row, rows_of, tok_ref = index()[...], table()[...], tokens()
    fill_layer(hid_ref, index_row, rows_of, tok_ref, attn())
    norm_ref, gout_ref, sum_ref = norm(), gout(), sums()

    @pl.loop(0, length // step, unroll=2)
    def _(i):
        rows = pl.ds(pl.multiple_of(i * step, step), step)
        hat, inv_std = norm_hat(hid_ref[rows, :])
        grad = sum_ref[rows, :].astype(F32)
        value = gout_ref[rows, :].astype(F32) + norm_back(grad, hat, inv_std, norm_ref[2:3, :])
        gattn_ref[rows, :] = value.astype(BF16)

    fill_bias(bias_ref, seg()[...])
    gmix_ref[...] = dot_nt(gattn_ref[...], wo()[...]).astype(BF16)
    scale = 1.0 / math.sqrt(HEAD)
    q_ref, k_ref, v_ref, lse_ref = q(), k(), v(), lse()

    @pl.loop(0, q_ref.shape[1] // HEAD)
    def _(number):
        cols = head_columns(number)
        here = head_lanes(length, number % 2)
        keys, vals = k_ref[:, cols], v_ref[:, cols]
        query = q_ref[:, cols] * scale
        gmix = gmix_ref[:, cols]
        scores = dot_nt(jnp.where(here, query, 0.0).astype(BF16), keys) + bias_ref[...]
        probs = jnp.exp(scores - lane_of(lse_ref[...], number))
        grad_probs = dot_nt(jnp.where(here, gmix, 0.0).astype(BF16), vals)
        grad_scores = (
            probs * (grad_probs - jnp.sum(probs * grad_probs, axis=-1, keepdims=True))
        ).astype(BF16)
        for place, value in (
            (2, dot_tn(probs.astype(BF16), gmix)),
            (1, dot_tn(grad_scores, query)),
            (0, dot_nn(grad_scores, keys) * scale),
        ):
            old = grads_ref[place, :, cols]
            grads_ref[place, :, cols] = jnp.where(here, value.astype(BF16), old)

    weights_ref, act_ref, return_ref = qkv_weight(), act(), return_weight()

    @pl.loop(0, 2)
    def _(i):
        rows = pl.ds(pl.multiple_of(i * half, half), half)
        total = sum(
            dot_nt(grads_ref[place, rows, :], weights_ref[place * D : (place + 1) * D, :])
            for place in range(3)
        )
        parts.ref[pl.ds(pl.multiple_of(2 * i * half, half), half), :] = total.astype(BF16)
        parts.ref[pl.ds(pl.multiple_of((2 * i + 1) * half, half), half), :] = dot_nn(
            act_ref[rows, :], return_ref[...]
        ).astype(BF16)

    parts.send()
    pool_ref = rest.ref
    left = normed()[...]
    share = D // BLK * (width // BLK)

    @pl.loop(0, 3)
    def _(place):
        store_blocks(pool_ref, place * share, left, grads_ref.at[place], weight)

    store_blocks(pool_ref, 3 * share, mixed()[...], gattn_ref, weight)
    rest()
    for number, (count, bits) in enumerate(chunks):
        keep, send = chunk_stores[2 * number : 2 * number + 2]
        gather_blocks(
            me_ref,
            source_ref,
            positions,
            first,
            count,
            bits,
            keep.ref,
            send.ref,
            lambda place: pool_ref[place],
        )
        send.send()
        keep.send()
        first += count
    late.send_if(scal_ref[3] > 0.5, pool_ref.at[0:late_count])


def overflow_kernel(first, count, bits, positions, me_ref, source_ref, loads, stores):
    (late,) = loads
    keep, send = stores
    late_ref = late()
    last = late_ref.shape[0] - 1
    gather_blocks(
        me_ref,
        source_ref,
        positions,
        first,
        count,
        bits,
        keep.ref,
        send.ref,
        lambda place: late_ref[jnp.minimum(place, last)],
    )
    keep.send()
    send.send()


def add_rows(acc_ref, at, values):
    acc_ref[at : at + 8, :] += jnp.sum(values.reshape(values.shape[0] // 8, 8, D), axis=0)


def finish_kernel(me_ref, scal_ref, loads, stores, layer_ref, acc_ref):
    index, table, tokens, attn_a, attn_b, norm, outputs, second_a, second_b, gout = loads
    out, gin, sums = stores
    half = attn_a.ref.shape[0]
    weight = scal_ref[0]
    step = 64
    acc_ref[...] = jnp.zeros_like(acc_ref)
    index_row = index()[...]
    rows_of = table()[...]
    tok_ref = tokens()
    for row0, attn, second in ((0, attn_a, second_a), (half, attn_b, second_b)):
        part = slice(row0, row0 + half)
        fill_layer(layer_ref, index_row[:, part], rows_of, tok_ref.at[part, :])
        attn_ref, norm_ref, second_ref, gout_ref, both_ref = (
            attn(),
            norm(),
            second(),
            gout(),
            outputs(),
        )
        @pl.loop(0, half // step)
        def _(
            i,
            row0=row0,
            attn_ref=attn_ref,
            norm_ref=norm_ref,
            second_ref=second_ref,
            gout_ref=gout_ref,
            both_ref=both_ref,
        ):
            at = pl.multiple_of(i * step, step)
            here = pl.ds(at, step)
            rows = pl.ds(pl.multiple_of(row0 + at, step), step)
            first_at = pl.multiple_of(2 * row0 + at, step)
            layer = layer_ref[here, :]
            hat, inv_std = norm_hat(layer)
            hid = layer + attn_ref[here, :].astype(F32)
            mlp = both_ref[pl.ds(first_at + half, step), :].astype(F32)
            out.ref[rows, :] = hid + mlp
            hat2, inv_std2 = norm_hat(hid)
            grad2 = second_ref[here, :].astype(F32)
            ghid = gout_ref[rows, :].astype(F32) + norm_back(
                grad2, hat2, inv_std2, norm_ref[2:3, :]
            )
            add_rows(acc_ref, 16, grad2 * hat2)
            add_rows(acc_ref, 24, grad2)
            grad = both_ref[pl.ds(first_at, step), :].astype(F32)
            gin.ref[rows, :] = ghid + norm_back(grad, hat, inv_std, norm_ref[0:1, :])
            add_rows(acc_ref, 0, grad * hat)
            add_rows(acc_ref, 8, grad)

        out.send(part)
        gin.send(part)
    for i in range(4):
        sums.ref[i : i + 1, :] = (
            jnp.sum(acc_ref[8 * i : 8 * i + 8, :], axis=0, keepdims=True) * weight
        )
    sums.ref[4:5, :] = jnp.full((1, D), weight, F32)
    sums.ref[5:8, :] = jnp.zeros((3, D), F32)
    sums.send()


def columns(rows):
    count = rows.shape[0]
    if count % 8:
        return jnp.stack(
            [jnp.transpose(jnp.broadcast_to(rows[i : i + 1], (BLK, BLK)))[:, 0:1] for i in range(count)]
        )
    turned = jnp.transpose(rows)
    return jnp.stack([turned[:, i : i + 1] for i in range(count)])


def reflect(blocks, left, right, coef_left, coef_right):
    along = jnp.sum(left * blocks, axis=1, keepdims=True) * coef_left
    blocks = blocks - left * along
    across = jnp.sum(blocks * right, axis=2, keepdims=True) * coef_right
    return blocks - across * right


def reflectors(left_ref, right_ref):
    left, right = left_ref[...], right_ref[...]
    coef_left = (2.0 / jnp.sum(left * left, axis=1, keepdims=True))[:, :, None]
    coef_right = (2.0 / jnp.sum(right * right, axis=1, keepdims=True))[:, :, None]
    return (columns(left), right[:, None, :], coef_left, coef_right)


def collect_kernel(counts, group, me_ref, place_ref, loads, stores, found_ref):
    grads, total = stores
    at = 0
    for number, count in enumerate(counts):
        keep, got = loads[2 * number : 2 + 2 * number]
        found_ref[at : at + count] = keep()[...].astype(F32) + got()[...].astype(F32)
        at += count
    slots = grads.ref.shape[0]
    square = jnp.zeros((8, BLK), F32)
    for at in range(0, slots, group):
        rows = slice(at, at + group)
        for slot in range(at, at + group):
            grads.ref[slot] = found_ref[place_ref[me_ref[0] * slots + slot]]
        grads.send(rows)
        grad = grads.ref[rows]
        square = square + jnp.sum((grad * grad).reshape(group * BLK // 8, 8, BLK), axis=0)
    total.ref[...] = jnp.full((8, BLK), jnp.sum(square), F32)
    total.send()


def rotate_kernel(group, me_ref, loads, stores):
    left, right, grads = loads
    (turned,) = stores
    parts = reflectors(left(), right())
    grads_ref = grads()
    for at in range(0, turned.ref.shape[0], group):
        rows = slice(at, at + group)
        turned.ref[rows] = reflect(grads_ref[rows], *(part[rows] for part in parts))
        turned.send(rows)


def inverse(value):
    guess = pl.reciprocal(value, approx=True)
    return guess * (2.0 - value * guess)


def update_kernel(group, me_ref, scal_ref, loads, stores):
    sums, norm, norm_first, norm_second, left, right = loads[:6]
    grads, turned_grads, old_first, old_second, old_master = loads[6:]
    out_grad, out_first, out_second, out_master, out_copy = stores[:5]
    norm_pair, norm_square, norm_value, clip_out = stores[5:]
    inv_one = 1.0 / scal_ref[1]
    inv_two = 1.0 / scal_ref[2]
    sums_ref = sums()
    share = 1.0 / sums_ref[4:5, 0:BLK]
    norm_grad = sums_ref[0:4, :] * share[:, 0:1]
    total = sums_ref[5:6, 0:BLK] * (share * share) + jnp.sum(norm_grad * norm_grad)
    clip_norm = jnp.sqrt(total)
    clip = jnp.minimum(1.0, clip_max / clip_norm)
    factor = (share * clip)[:, None, :]
    parts = reflectors(left(), right())
    slots = left.ref.shape[0]
    entries = 1.0 / (BLK * BLK)
    for at in range(0, slots, group):
        rows = slice(at, at + group)
        out_grad.ref[rows] = grads()[rows] * factor
        rotated = turned_grads()[rows] * factor
        first = beta_one * old_first()[rows] + (1.0 - beta_one) * rotated
        second = beta_two * old_second()[rows] + (1.0 - beta_two) * rotated * rotated
        out_first.ref[rows] = first
        out_second.ref[rows] = second
        spread = second * inv_two
        normal = (first * inv_one) * inverse(spread * lax.rsqrt(spread) + adam_eps)
        turned = reflect(normal, *(part[rows] for part in parts))
        master = old_master()[rows]
        size = jnp.sum(jnp.sum(master * master, axis=1, keepdims=True), axis=2, keepdims=True)
        move = jnp.sum(jnp.sum(turned * turned, axis=1, keepdims=True), axis=2, keepdims=True)
        trust = jnp.sqrt(size * entries + trust_eps) / jnp.sqrt(move * entries + trust_eps)
        fresh = master - (step_rate * trust) * turned
        out_master.ref[rows] = fresh
        out_copy.ref[rows] = fresh.astype(BF16)
        for out in (out_grad, out_first, out_second, out_master, out_copy):
            out.send(rows)
    clip_out.target[0, 0] = clip_norm[0, 0]
    clipped = norm_grad * clip[:, 0:1]
    first = beta_one * norm_first()[...] + (1.0 - beta_one) * clipped
    second = beta_two * norm_second()[...] + (1.0 - beta_two) * clipped * clipped
    norm_pair.ref[0] = clipped
    norm_pair.ref[1] = first
    norm_pair.send()
    norm_square.ref[...] = second
    norm_square.send()
    norm_value.ref[...] = norm()[...] - step_rate * (first * inv_one) / (
        jnp.sqrt(second * inv_two) + adam_eps
    )
    norm_value.send()


def swap(value, axis, bit):
    count = lax.axis_size(axis)
    return lax.ppermute(value, axis, [(i, i ^ bit) for i in range(count)])


def plus(left, right):
    return (left.astype(F32) + right.astype(F32)).astype(BF16)


def after(value, *others):
    return lax.optimization_barrier((value, *others))[0]


def mp_far(total, wait=None):
    bit = 2
    while bit < lax.axis_size("mp"):
        got = swap(total, "mp", bit)
        total = plus(total, got if wait is None else after(got, wait))
        bit *= 2
    return total


def mp_sum(keep, send):
    total = mp_far(plus(keep, swap(send, "mp", 1)))
    return (total, swap(total, "mp", 1))


def early_count(slots):
    return slots // 3 if slots >= 24 else 0


def split_counts(slots, bits):
    if slots >= 8:
        last = slots // 4
        head = (slots - last + 2) // 2
        return ((head, bits), (slots - last - head, bits), (last, (bits[1], bits[0]) + bits[2:]))
    return ((1, bits),) * slots if slots <= 3 else ((slots - slots // 2, bits), (slots // 2, bits))


def exclusive_sum(values):
    size = values.shape[-1]
    before = jnp.asarray(np.tril(np.ones((size, size), np.int32), -1))
    return jnp.sum(values[..., None, :] * before, axis=-1)


def rest_count(blocks, late_count, n_dp, slots, early_slots):
    total = blocks - late_count
    full, over = divmod(total, slots)
    return total - full * early_slots - min(over, early_slots)


def slot_tables(owner_list, n_dp, slots, early_slots, late_count):
    blocks = owner_list.shape[0]
    owned = owner_list.reshape(n_dp, slots)
    early = (owned >= late_count).astype(jnp.int32)
    if early_slots:
        goes = early * (exclusive_sum(early) < early_slots).astype(jnp.int32)
        place = jnp.where(goes == 1, exclusive_sum(early), early_slots + exclusive_sum(1 - goes))
        positions = slots + early_slots
        hit = place[:, None, :] == jnp.arange(positions, dtype=jnp.int32)[None, :, None]
        source = jnp.sum(jnp.where(hit, owned[:, None, :], 0), axis=2)
        short = jnp.any(jnp.sum(early, axis=1) < early_slots)
    else:
        place = jnp.broadcast_to(jnp.arange(slots, dtype=jnp.int32), (n_dp, slots))
        source, short = owned, jnp.zeros((), bool)
    later = source[:, early_slots:].reshape(-1)
    is_rest = (later >= late_count).astype(jnp.int32)
    order = exclusive_sum(is_rest)
    count = rest_count(blocks, late_count, n_dp, slots, early_slots)
    hit = (order[None, :] == jnp.arange(count, dtype=jnp.int32)[:, None]) & (is_rest[None, :] == 1)
    rest = jnp.sum(jnp.where(hit, later[None, :], 0), axis=1)
    later = jnp.where(is_rest == 1, late_count + order, later)
    source = jnp.concatenate([source[:, :early_slots], later.reshape(n_dp, -1)], axis=1)
    return (jnp.concatenate([source.reshape(-1), rest]), place.reshape(-1), short)


def shards(
    tokens,
    cotangent,
    segment_ids,
    table_index,
    group_count,
    owner_list,
    step_count,
    query_weight,
    key_weight,
    value_weight,
    output_weight,
    hidden_weight,
    return_weight,
    norm_params,
    norm_first,
    norm_second,
    master_blocks,
    first_moment,
    second_moment,
    left_vector,
    right_vector,
):
    length = tokens.shape[0]
    half = length // 2
    width = query_weight.shape[1]
    heads = width // HEAD
    units = hidden_weight.shape[1]
    slots = master_blocks.shape[0]
    blocks = owner_list.shape[0]
    late_count = blocks // 3
    n_dp = lax.axis_size("dp")
    natural = tuple(1 << i for i in range(n_dp.bit_length() - 1))
    early_slots = early_count(slots)
    positions = slots + early_slots
    me = jnp.stack([lax.axis_index("dp"), lax.axis_index("mp")]).astype(jnp.int32)
    step_value = step_count[0].astype(F32)
    source, place, short = slot_tables(owner_list, n_dp, slots, early_slots, late_count)
    scal = jnp.stack(
        [
            group_count[0].astype(F32),
            1.0 - jnp.power(beta_one, step_value),
            1.0 - jnp.power(beta_two, step_value),
            short.astype(F32),
        ]
    )
    seg_row = segment_ids.reshape(1, length)
    index_row = table_index.reshape(1, length)
    table = jnp.asarray(position_rows())
    rows_d = (length, D)
    half_d = (half, D)
    unit = 2 * length * D * D
    wide = ((length, width), BF16)

    normed, q, k, v, mixed, lse, keep_a, send_a, keep_b, send_b = call(
        forward_kernel,
        "attention_forward",
        (me,),
        (
            index_row,
            table,
            tokens,
            seg_row,
            norm_params,
            query_weight,
            key_weight,
            value_weight,
            output_weight,
        ),
        [
            (rows_d, BF16),
            wide,
            wide,
            wide,
            wide,
            ((length, heads), F32),
            (half_d, BF16, True),
            (half_d, BF16, True),
        ],
        [(rows_d, F32), ((length, length), F32)],
        flops=5 * unit,
    )
    near_a = plus(keep_a, swap(send_a, "mp", 1))
    near_b = plus(keep_b, swap(send_b, "mp", 1))
    token = near_b
    grad_out, grad_act = call(
        grad_out_kernel,
        "grad_of_act",
        (me,),
        (seg_row, cotangent, return_weight),
        [(rows_d, BF16), ((length, units), F32)],
        flops=2 * unit,
        after=token,
    )

    far_a = mp_far(near_a, grad_act)
    attn_a = Pair(far_a, swap(far_a, "mp", 1))
    def feed(row0, name, sums, token):
        return call(
            functools.partial(feed_kernel, row0),
            name,
            (me,),
            (
                index_row,
                table,
                Rows(tokens, row0, half),
                sums,
                norm_params,
                hidden_weight,
                Rows(grad_act, row0, half),
            ),
            [
                (half_d, BF16),
                ((half, units), BF16),
                ((half, units), BF16),
                (half_d, BF16, True),
            ],
            [((half, units), F32)],
            flops=4 * unit,
            after=token,
            limit=50 * MIB,
        )

    second_a, act_a, gpre_a, keep_a, send_a = feed(0, "feed_forward_a", attn_a, None)
    far_b = mp_far(near_b, keep_a)
    attn_b = Pair(far_b, swap(far_b, "mp", 1))
    second_b, act_b, gpre_b, keep_b, send_b = feed(half, "feed_forward_b", attn_b, keep_a)
    near_a = plus(keep_a, swap(send_a, "mp", 1))
    near_b = plus(keep_b, swap(send_b, "mp", 1))
    chunk_e = [((n_dp // 2 * early_slots, BLK, BLK), BF16)] * 2 if early_slots else []
    count = rest_count(blocks, late_count, n_dp, slots, early_slots)
    rest, *chunk_e = call(
        functools.partial(feed_grad_kernel, natural, early_slots, positions, late_count),
        "feed_weight_grads",
        (me, source, scal),
        (Stack(second_a, second_b), Stack(gpre_a, gpre_b), Stack(act_a, act_b), grad_out),
        [((count, BLK, BLK), BF16)] + chunk_e,
        [((blocks - late_count, BLK, BLK), BF16)],
        flops=4 * unit,
        limit=48 * MIB,
        after=near_b,
    )
    far_a = mp_far(near_a, rest)
    far_b = mp_far(near_b, far_a)
    sum_a = Pair(far_a, swap(far_a, "mp", 1))
    sum_b = Pair(far_b, swap(far_b, "mp", 1))
    got_e = swap(chunk_e[1], "dp", 1) if early_slots else None
    chunks = split_counts(slots - early_slots, natural)
    chunk_shapes = []
    for count, _ in chunks:
        chunk_shapes += [((n_dp // 2 * count, BLK, BLK), BF16)] * 2
    outs = call(
        functools.partial(backward_kernel, chunks, early_slots, positions, late_count),
        "attention_backward",
        (me, source, scal),
        (
            index_row,
            table,
            tokens,
            Stack(attn_a, attn_b),
            norm_params,
            Stack(sum_a, sum_b),
            grad_out,
            output_weight,
            seg_row,
            q,
            k,
            v,
            lse,
            normed,
            mixed,
            Into(rest, late_count),
            Stack(query_weight, key_weight, value_weight),
            Stack(act_a, act_b),
            return_weight,
        ),
        [((late_count, BLK, BLK), BF16), ((2 * length, D), BF16, True)] + chunk_shapes,
        [(rows_d, BF16)]
        + [((length, width), BF16), ((3, length, width), BF16)]
        + [(rows_d, F32), ((length, length), F32)],
        flops=10 * unit,
    )
    late, keep, send = outs[:3]
    queue = [(outs[3 + 2 * i], outs[4 + 2 * i]) for i in range(len(chunks))]
    counts = [count for count, _ in chunks]
    orders = [bits for _, bits in chunks]

    stages = len(natural)
    state = [(first, swap(second, "dp", bits[0])) for (first, second), bits in zip(queue, orders)]
    if early_slots:
        state.insert(0, (chunk_e[0], after(got_e, keep)))
        counts.insert(0, early_slots)
        orders.insert(0, natural)
    level = [0] * len(state)
    last = []

    def in_turn(got):
        got = after(got, *last)
        last[:] = [got]
        return got

    def halve(number):
        keep, got = state[number]
        got = in_turn(got)
        if level[number] < stages - 1:
            n = keep.shape[0] // 2
            keep, send = plus(keep[:n], got[:n]), plus(keep[n:], got[n:])
            got = swap(send, "dp", orders[number][level[number] + 1])
            last.append(send)
        level[number] += 1
        state[number] = (keep, got)

    def mp_first(keep, send):
        return plus(keep, in_turn(swap(send, "mp", 1)))

    def mp_rest(near):
        bit = 2
        while bit < lax.axis_size("mp"):
            near = plus(near, in_turn(swap(near, "mp", bit)))
            bit *= 2
        return Pair(near, swap(near, "mp", 1))

    if early_slots:
        halve(0)
    def finish(both):
        outputs = call(
            finish_kernel,
            "layer_outputs",
            (me, scal),
            (
                index_row,
                table,
                tokens,
                attn_a,
                attn_b,
                norm_params,
                both,
                sum_a,
                sum_b,
                grad_out,
            ),
            [(rows_d, F32), (rows_d, F32), ((8, D), F32)],
            [(half_d, F32), ((32, D), F32)],
            flops=2 * unit,
            limit=40 * MIB,
        )
        last.append(outputs[2])
        return outputs

    overflow, early_done = [], []
    if early_slots:
        shape = (n_dp // 2 * early_slots, BLK, BLK)

        def exchange(late):
            keep, send = call(
                functools.partial(overflow_kernel, slots, early_slots, natural, positions),
                "overflow",
                (me, source),
                (late,),
                [(shape, BF16), (shape, BF16)],
            )
            bit = 1
            while True:
                got = swap(send, "dp", bit)
                bit *= 2
                if bit >= n_dp:
                    return (keep, got)
                n = keep.shape[0] // 2
                keep, send = plus(keep[:n], got[:n]), plus(keep[n:], got[n:])

        def nothing(late):
            zero = jnp.zeros((early_slots, BLK, BLK), BF16)
            return (zero, zero)

        overflow = list(lax.cond(short, exchange, nothing, late))
        early_done = [overflow[0], place]

    plan = ["near", "far", "finish"]
    if early_slots and stages == 3:
        plan = ["near",(3,0),(1,0),(0,1),(2,0),(1,1),(0,2),(3,1),(2,1),(1,2),"far","finish"]
    plan += [(i, d - i) for d in range(len(state) + stages) for i in range(len(state))]
    for entry in plan:
        if entry == "near":
            near = plus(keep, in_turn(swap(send, "mp", 1)))
            last += early_done
        elif entry == "far":
            bit = 2
            while bit < lax.axis_size("mp"):
                near = plus(near, in_turn(swap(near, "mp", bit)))
                bit *= 2
            both = Pair(near, swap(near, "mp", 1))
        elif entry == "finish":
            out, input_grad, sums = finish(both)
        elif level[entry[0]] == entry[1] < stages:
            halve(entry[0])
    pending = [array for pair in state for array in pair]

    pending += overflow
    counts += [early_slots] if early_slots else []
    left = left_vector.reshape(slots, BLK)
    right = right_vector.reshape(slots, BLK)
    block_f32 = ((slots, BLK, BLK), F32)
    group = 4 if slots % 4 == 0 else 1
    grads, square = call(
        functools.partial(collect_kernel, counts, group),
        "collect",
        (me, place),
        tuple(pending),
        [block_f32, ((8, BLK), F32)],
        [((sum(counts), BLK, BLK), F32)],
        flops=unit,
        limit=28 * MIB,
    )
    (rotated,) = call(
        functools.partial(rotate_kernel, group),
        "rotate",
        (me,),
        (left, right, grads),
        [block_f32],
        flops=unit,
        limit=28 * MIB,
    )
    bit = 1
    while bit < lax.axis_size("mp"):
        square = square + swap(square, "mp", bit)
        bit *= 2
    sums = sums + jnp.pad(square[0:1], ((5, 2), (0, D - BLK)))
    bit = 1
    while bit < n_dp:
        sums = sums + swap(sums, "dp", bit)
        bit *= 2
    new = call(
        functools.partial(update_kernel, group),
        "update",
        (me, scal),
        (
            sums,
            norm_params,
            norm_first,
            norm_second,
            left,
            right,
            grads,
            rotated,
            first_moment.reshape(slots, BLK, BLK),
            second_moment.reshape(slots, BLK, BLK),
            master_blocks.reshape(slots, BLK, BLK),
        ),
        [block_f32] * 4
        + [
            ((slots, BLK, BLK), BF16),
            ((2, 4, D), F32),
            ((4, D), F32),
            ((4, D), F32),
            ((1, 1), F32),
        ],
        flops=unit,
        limit=28 * MIB,
    )
    shard_shape = (slots, 1, BLK, BLK)
    return (
        out,
        input_grad,
        new[0].reshape(shard_shape),
        new[1].reshape(shard_shape),
        new[2].reshape(shard_shape),
        new[3].reshape(shard_shape),
        new[4].reshape(shard_shape),
        new[5],
        new[6],
        new[7],
        new[8].reshape(()),
    )


def solution(mesh):
    placed = (
        P("dp", None),
        P("dp", None),
        P("dp"),
        P("dp"),
        P("dp"),
        P(),
        P(),
        P(None, "mp"),
        P(None, "mp"),
        P(None, "mp"),
        P("mp", None),
        P(None, "mp"),
        P("mp", None),
        P(),
        P(),
        P(),
        P("dp", "mp", None, None),
        P("dp", "mp", None, None),
        P("dp", "mp", None, None),
        P("dp", "mp", None),
        P("dp", "mp", None),
    )
    return jax.shard_map(
        shards,
        mesh=mesh,
        in_specs=placed,
        out_specs=(
            P("dp", None),
            P("dp", None),
            P("dp", "mp", None, None),
            P("dp", "mp", None, None),
            P("dp", "mp", None, None),
            P("dp", "mp", None, None),
            P("dp", "mp", None, None),
            P(),
            P(),
            P(),
            P(),
        ),
        check_vma=False,
    )
```
